128 devices in a mesh: dev: 128 (over z, y, x, core).
Axes of the slice: x: 4, y: 4, z: 4, core: 2. Of those that a mesh axis runs over, the one named last changes fastest.
Arguments:
- displacement: float32 [3, 524288], P(None, 'dev'), may hold values from -2 to 2
- send_node: int32 [1048576], P('dev'), may hold values from -1 to 4095, as said below
- member_slot: int32 [512, 1024], P('dev'), may hold values from 0 to 8191, as said below
- inverse_part: bfloat16 [512, 1024, 1024], P('dev'), may hold values from -0.09375 to 0.09375
- source_coord: float32 [512, 3, 1024], P('dev'), may hold values from 0 to 1
- target_coord: float32 [512, 3, 1024], P('dev'), may hold values from 0 to 1
- unity_weight: float32 [512, 1024], P('dev'), may hold values from 0.1 to 1
- result_pick: int32 [1048576], P('dev'), may hold values from -1 to 4095, as said below
- receive_vertex: int32 [1048576], P('dev'), may hold values from 0 to 8191
- mesh_before: float32 [3, 2048, 96, 512], P(None, 'dev'), may hold values from -6 to 6
Outputs:
- mesh_motion: float32 [3, 2048, 96, 512], P(None, 'dev')
The draws below stay inside these ranges and needn't reach their ends.
Inputs may be any that keep to these rules, and one draw needn't show every extreme that they name: `send_node`: each device's entries form 128 blocks of 64, block e for cluster owner e; in each block the live entries (0 or more) come first and -1 fills the rest; each block has at least one live entry and each device has one block with all 64 live. `member_slot`: every entry names a live slot of send_node sent to the cluster's owner. `result_pick`: each device's entries form 128 blocks of 64, block e for fluid owner e; in each block the live entries (0 or more) come first and -1 fills the rest; each block has at least one live entry and each device has one block with all 64 live.
All inputs are finite; a program needn't handle non-finite values.
Results may differ from the reference program's by a relative error of at most 0.00043.
Values sent between devices are 32-bit elements; how exact they have to be, the bound alone decides.
A program may use at most 128 MiB of HBM per device.

```python
import jax
import jax.numpy as jnp
from jax import lax

NODE_DEV = 4096
CL_DEV = 4
CP = 1024
FT = 1024
GX = 16
GY = 96
GZ = 512
SCAP = 64
RCAP = 64
FIV = 8192
NODES = 524288
CLUSTERS = 512
NX = 2048
N_DEV = 128


def slot_counts(key, capacity):
    low = max(1, capacity // 4)
    load = jax.random.randint(jax.random.fold_in(key, 1), (N_DEV,), 1, 5)
    high = jnp.maximum(low, load * capacity // 4)
    raw = jax.random.randint(jax.random.fold_in(key, 2), (N_DEV, N_DEV), 0, 1 << 20)
    counts = low + raw % (high[None, :] - low + 1)
    offset = jax.random.randint(jax.random.fold_in(key, 3), (), 0, N_DEV)
    rows = jnp.arange(N_DEV, dtype=jnp.int32)
    full = rows[None, :] == (rows[:, None] + offset) % N_DEV
    return jnp.where(full, capacity, counts).astype(jnp.int32)


def draw_send_node(key, part):
    base = jax.random.fold_in(key, 101)
    counts = slot_counts(base, SCAP)
    nodes = jax.random.randint(jax.random.fold_in(base, 4), (N_DEV, N_DEV, SCAP), 0, NODE_DEV)
    live = jnp.arange(SCAP, dtype=jnp.int32)[None, None, :] < counts[:, :, None]
    return jnp.where(live, nodes, -1).reshape(-1).astype(jnp.int32)


def draw_member_slot(key, part):
    base = jax.random.fold_in(key, 101)
    counts = slot_counts(base, SCAP)
    source = jax.random.randint(jax.random.fold_in(base, 5), (N_DEV, CL_DEV, CP), 0, N_DEV)
    raw = jax.random.randint(jax.random.fold_in(base, 6), (N_DEV, CL_DEV, CP), 0, 1 << 20)
    owner = jnp.arange(N_DEV, dtype=jnp.int32)[:, None, None]
    live = counts[source, owner]
    slot = source * SCAP + raw % live
    return slot.reshape(N_DEV * CL_DEV, CP).astype(jnp.int32)


def draw_result_pick(key, part):
    base = jax.random.fold_in(key, 202)
    counts = slot_counts(base, RCAP)
    picks = jax.random.randint(jax.random.fold_in(base, 4), (N_DEV, N_DEV, RCAP), 0, CL_DEV * FT)
    live = jnp.arange(RCAP, dtype=jnp.int32)[None, None, :] < counts[:, :, None]
    return jnp.where(live, picks, -1).reshape(-1).astype(jnp.int32)


def with_ends(values, rng, least, top_value):
    spot = [jax.random.randint(jax.random.fold_in(rng, axis), (), 0, length) for axis, length in enumerate(values.shape)]
    longest = values.shape.index(max(values.shape))
    neighbour = spot[:longest] + [(spot[longest] + 1) % values.shape[longest]] + spot[longest + 1:]
    return values.at[tuple(spot)].set(least).at[tuple(neighbour)].set(top_value)


def levels(own_key, dims, pieces, low, high):
    gain, own = 1.0, jax.random.fold_in(own_key, 6)
    for dim, blocks in pieces:
        steps = jnp.exp(jax.random.uniform(jax.random.fold_in(own, dim), (blocks,), jnp.float32, low / len(pieces), high / len(pieces)))
        gain = gain * jnp.repeat(steps, dims[dim] // blocks).reshape([-1 if axis == dim else 1 for axis in range(len(dims))])
    return gain


def scatter_about(key, dims, width, limit, cuts=(), kind=jnp.bfloat16):
    values = jax.random.normal(key, dims, jnp.float32) * width
    if len(cuts) > 0:
        values = levels(key, dims, cuts, -0.22, 0.18) * values
    return jnp.clip(values, min=-limit, max=limit).astype(kind)


def setup_inputs(seed: int = 0) -> dict:
    key_of = jax.random.split(jax.random.key(seed), 11)
    displacement = scatter_about(key_of[0], (3, NODES), 0.25, 2.0, ((1, 128),), jnp.float32)
    send_node = draw_send_node(jax.random.fold_in(key_of[10], 71), 0)
    member_slot = draw_member_slot(jax.random.fold_in(key_of[10], 71), 0)
    inverse_part = scatter_about(key_of[3], (CLUSTERS, CP, CP), (4 * CP) ** -0.5, 0.09375, ((0, 128),))
    source_coord = jnp.clip(1.0 * jax.random.uniform(key_of[4], (CLUSTERS, 3, CP), jnp.float32) ** levels(key_of[4], (CLUSTERS, 3, CP), ((0, 128),), -0.2, 0.2), 0.0, 1.0)
    target_coord = jnp.clip(1.0 * jax.random.uniform(key_of[5], (CLUSTERS, 3, FT), jnp.float32) ** levels(key_of[5], (CLUSTERS, 3, FT), ((0, 128),), -0.2, 0.2), 0.0, 1.0)
    unity_weight = jnp.clip(0.1 + 0.9 * jax.random.uniform(key_of[6], (CLUSTERS, FT), jnp.float32) ** levels(key_of[6], (CLUSTERS, FT), ((0, 128),), -0.2, 0.2), 0.1, 1.0)
    result_pick = draw_result_pick(jax.random.fold_in(key_of[10], 71), 0)
    receive_vertex = with_ends(jax.random.randint(key_of[8], (N_DEV * N_DEV * RCAP,), 0, FIV), jax.random.fold_in(key_of[8], 1), 0, FIV - 1).astype(jnp.int32)
    mesh_before = scatter_about(key_of[9], (3, NX, GY, GZ), 1.0, 6.0, ((1, 128),), jnp.float32)
    return {"displacement": displacement, "send_node": send_node, "member_slot": member_slot, "inverse_part": inverse_part, "source_coord": source_coord, "target_coord": target_coord, "unity_weight": unity_weight, "result_pick": result_pick, "receive_vertex": receive_vertex, "mesh_before": mesh_before}


relax_rate = 0.8
kernel_sharpness = 8.0


def relax(field):
    padded = jnp.pad(field, ((0, 0), (1, 1), (1, 1), (1, 1)))
    beside = padded[:, 2:, 1:-1, 1:-1] + padded[:, :-2, 1:-1, 1:-1]
    beside = beside + padded[:, 1:-1, 2:, 1:-1] + padded[:, 1:-1, :-2, 1:-1]
    beside = beside + padded[:, 1:-1, 1:-1, 2:] + padded[:, 1:-1, 1:-1, :-2]
    moved = field + relax_rate * (beside * (1.0 / 6.0) - field)
    yrows = lax.broadcasted_iota(jnp.int32, field.shape, 2)
    return jnp.where(yrows == 0, field, moved)


def one_cluster(inputs):
    members, inverse, source, target, weight = inputs
    coupling = lax.dot_general(members.astype(jnp.bfloat16), inverse, (((1,), (1,)), ((), ())), preferred_element_type=jnp.float32)
    coefficient = members + coupling
    gap = target[0][:, None] - source[0][None, :]
    spread = gap * gap
    gap = target[1][:, None] - source[1][None, :]
    spread = spread + gap * gap
    gap = target[2][:, None] - source[2][None, :]
    spread = spread + gap * gap
    kernel = jnp.exp(-kernel_sharpness * spread)
    contrib = lax.dot_general(coefficient, kernel, (((1,), (1,)), ((), ())), precision=lax.Precision.HIGHEST, preferred_element_type=jnp.float32)
    return contrib * weight[None, :]


def reference(displacement, send_node, member_slot, inverse_part, source_coord, target_coord, unity_weight, result_pick, receive_vertex, mesh_before):
    count = N_DEV
    plan = send_node.reshape(count, count, SCAP)
    source_dev = jnp.arange(count, dtype=jnp.int32)[:, None, None]
    global_node = (source_dev * NODE_DEV + jnp.maximum(plan, 0)).astype(jnp.int32)
    sent = jnp.where(plan[None] >= 0, displacement[:, global_node], 0.0)
    received = sent.transpose(0, 2, 1, 3).reshape(3, count * count * SCAP)
    owner = (jnp.arange(CLUSTERS, dtype=jnp.int32) // CL_DEV)[:, None]
    flat_slot = (owner * (count * SCAP) + member_slot).astype(jnp.int32)
    members = received[:, flat_slot].transpose(1, 0, 2)
    contrib = lax.map(one_cluster, (members, inverse_part, source_coord, target_coord, unity_weight))
    contrib = contrib.reshape(count, CL_DEV, 3, FT).transpose(0, 2, 1, 3).reshape(count, 3, CL_DEV * FT)
    picks = result_pick.reshape(count, 1, count * RCAP)
    taken = jnp.take_along_axis(contrib, jnp.broadcast_to(jnp.maximum(picks, 0), (count, 3, count * RCAP)), axis=2)
    taken = jnp.where(picks >= 0, taken, 0.0)
    taken = taken.reshape(count, 3, count, RCAP).transpose(1, 2, 0, 3).reshape(3, count * count * RCAP)
    receiver = (jnp.arange(count, dtype=jnp.int32) * FIV)[:, None]
    target_index = (receiver + receive_vertex.reshape(count, count * RCAP)).reshape(-1).astype(jnp.int32)
    interface = jnp.zeros((3, count * FIV), jnp.float32).at[:, target_index].add(taken)
    interface = interface.reshape(3, count * GX, GZ)
    yrows = lax.broadcasted_iota(jnp.int32, mesh_before.shape, 2)
    start_field = jnp.where(yrows == 0, interface[:, :, None, :], mesh_before)
    return relax(relax(start_field))
```

```python
import functools

import jax
import jax.numpy as jnp
from jax import lax
from jax.experimental import pallas as pl
from jax.experimental.pallas import tpu as pltpu
from jax.sharding import PartitionSpec as P

relax_rate = 0.8
kernel_sharpness = 8.0
log2_e = 1.4426950408889634
spread_rate = relax_rate / 6.0
keep_rate = 1.0 - relax_rate

MESH = pl.DeviceIdType.MESH
f32 = jnp.float32
bf16 = jnp.bfloat16


def vmem():
    return pl.BlockSpec(memory_space=pltpu.VMEM)


def lookup(row, lanes):
    spread = jnp.broadcast_to(row, lanes.shape)
    return jnp.take_along_axis(spread, lanes, axis=1, mode="promise_in_bounds")


def message_index(index_ref, step):
    x, core = step // 2, step % 2
    even = index_ref[pl.ds(x, 8, stride=8), :]
    odd = index_ref[pl.ds(4 + x, 8, stride=8), :]
    lane = lax.broadcasted_iota(jnp.int32, (8, 128), 1)
    if core == 0:
        return jnp.where(lane < 64, even, pltpu.roll(odd, 64, 1))
    return jnp.where(lane < 64, pltpu.roll(even, 64, 1), odd)


def pick_messages(index_ref, row_of, out_ref):
    for half in range(2):
        index = [message_index(index_ref, 4 * half + g) for g in range(4)]
        high = [jnp.right_shift(i, 7) for i in index]
        low = [jnp.bitwise_and(i, 127) for i in index]
        total = [[jnp.zeros((8, 128), f32) for _ in range(3)] for _ in range(4)]
        for r in range(32):
            hit = [h == r for h in high]
            for k in range(3):
                row = row_of(k, r)
                for g in range(4):
                    total[g][k] = jnp.where(hit[g], lookup(row, low[g]), total[g][k])
        for g in range(4):
            for k in range(3):
                out_ref[(4 * half + g) * 3 + k] = total[g][k]


def send_kernel(disp_ref, node_ref, out_ref):
    pick_messages(
        node_ref, lambda k, r: disp_ref[k : k + 1, r * 128 : (r + 1) * 128], out_ref
    )


def exchange_kernel(y_ref, t_ref, held, ready, landed, send1, recv1, send2, recv2):
    me = lax.axis_index("dev")
    outer, inner = me // 8, me % 8

    barrier = pltpu.get_barrier_semaphore()
    for i in range(1, 8):
        peer = outer * 8 + (inner + i) % 8
        pl.semaphore_signal(barrier, inc=1, device_id=(peer,), device_id_type=MESH)
    for i in range(1, 16):
        peer = ((outer + i) % 16) * 8 + inner
        pl.semaphore_signal(barrier, inc=1, device_id=(peer,), device_id_type=MESH)
    pl.semaphore_wait(barrier, 22)

    copies = []
    for i in range(1, 8):
        p = (inner + i) % 8
        copies.append(
            pltpu.make_async_remote_copy(
                src_ref=y_ref.at[pl.ds(pl.multiple_of(p * 24, 8), 24)],
                dst_ref=held.at[pl.ds(pl.multiple_of(inner * 24, 8), 24)],
                send_sem=send1.at[i - 1],
                recv_sem=recv1.at[i - 1],
                device_id=(outer * 8 + p,),
                device_id_type=MESH,
            )
        )
        copies[-1].start()
    mine = pl.ds(pl.multiple_of(inner * 24, 8), 24)
    held[mine, :] = y_ref[mine, :]
    for copy in copies:
        copy.wait()

    lane = lax.broadcasted_iota(jnp.int32, (4, 128), 1)
    for m in range(8):
        for k in range(3):
            first = held[pl.ds(k * 8 + m, 4, stride=48), :]
            second = held[pl.ds(24 + k * 8 + m, 4, stride=48), :]
            ready[2 * m, 4 * k : 4 * k + 4, :] = jnp.where(
                lane < 64, first, pltpu.roll(second, 64, 1)
            )
            ready[2 * m + 1, 4 * k : 4 * k + 4, :] = jnp.where(
                lane < 64, pltpu.roll(first, 64, 1), second
            )

    copies = []
    for i in range(1, 16):
        p = (outer + i) % 16
        copies.append(
            pltpu.make_async_remote_copy(
                src_ref=ready.at[p],
                dst_ref=landed.at[outer],
                send_sem=send2.at[i - 1],
                recv_sem=recv2.at[i - 1],
                device_id=(p * 8 + inner,),
                device_id_type=MESH,
            )
        )
        copies[-1].start()
    landed[outer] = ready[outer]
    for copy in copies:
        copy.wait()
    t_ref[...] = landed[...]


def exchange(messages, collective_id):
    return pl.pallas_call(
        exchange_kernel,
        out_shape=jax.ShapeDtypeStruct((16, 12, 128), f32),
        in_specs=[vmem()],
        out_specs=vmem(),
        scratch_shapes=[
            pltpu.VMEM((192, 128), f32),
            pltpu.VMEM((16, 12, 128), f32),
            pltpu.VMEM((16, 12, 128), f32),
            pltpu.SemaphoreType.DMA((7,)),
            pltpu.SemaphoreType.DMA((7,)),
            pltpu.SemaphoreType.DMA((15,)),
            pltpu.SemaphoreType.DMA((15,)),
        ],
        compiler_params=pltpu.CompilerParams(
            collective_id=collective_id, has_side_effects=True
        ),
    )(messages.reshape(192, 128))


def three_parts(value):
    high = value.astype(bf16).astype(f32)
    rest = value - high
    middle = rest.astype(bf16).astype(f32)
    return high, middle, rest - middle


def cluster_rows(ref, c, rows):
    return jnp.concatenate([ref[q, pl.ds(c, rows, stride=4), :] for q in range(8)], axis=1)


def cluster_kernel(
    t_ref, slot_ref, inv_hbm, source_ref, target_ref, weight_ref, pick_ref, out_ref,
    inv, loaded, member, left, right, result,
):
    for c in range(4):
        pltpu.make_async_copy(inv_hbm.at[c], inv.at[c], loaded.at[c]).start()

    left[...] = jnp.zeros_like(left)
    right[...] = jnp.zeros_like(right)
    ones = jnp.ones((4, 1024), f32)
    row = 0
    source_norm = jnp.zeros((4, 1024), f32)
    target_norm = jnp.zeros((4, 1024), f32)

    def put(a, b):
        nonlocal row
        for q in range(8):
            left[q, 4 * row : 4 * row + 4, :] = a[:, 128 * q : 128 * (q + 1)]
            right[q, 4 * row : 4 * row + 4, :] = b[:, 128 * q : 128 * (q + 1)]
        row += 1

    for d in range(3):
        s = source_ref[d]
        t = target_ref[d]
        source_norm += s * s
        target_norm += t * t
        sh, sm, sl = three_parts(s)
        th, tm, tl = three_parts(t * (2.0 * kernel_sharpness * log2_e))
        for a, b in ((sh, th), (sh, tm), (sm, th), (sh, tl), (sl, th), (sm, tm)):
            put(a, b)
    for part in three_parts(source_norm * (-kernel_sharpness * log2_e)):
        put(part, ones)
    for part in three_parts(target_norm * (-kernel_sharpness * log2_e)):
        put(ones, part)

    member[...] = jnp.zeros_like(member)
    index = [
        jnp.concatenate(
            [slot_ref[:, 256 * m : 256 * m + 128], slot_ref[:, 256 * m + 128 : 256 * m + 256]],
            axis=0,
        )
        for m in range(4)
    ]
    high = [jnp.right_shift(i, 7) for i in index]
    low = [jnp.bitwise_and(i, 127) for i in index]

    def gather(zy, total):
        total = list(total)
        for j in range(4):
            hit = [h == zy * 4 + j for h in high]
            for k in range(3):
                line = t_ref[zy, 4 * k + j : 4 * k + j + 1, :]
                for m in range(4):
                    total[3 * m + k] = jnp.where(hit[m], lookup(line, low[m]), total[3 * m + k])
        return tuple(total)

    total = lax.fori_loop(
        0, 16, gather, tuple(jnp.zeros((8, 128), f32) for _ in range(12))
    )
    for m in range(4):
        for k in range(3):
            value = total[3 * m + k]
            member[2 * m, 4 * k : 4 * k + 4, :] = value[0:4]
            member[2 * m + 1, 4 * k : 4 * k + 4, :] = value[4:8]

    for c in range(4):
        members = cluster_rows(member, c, 8)
        padded = jnp.concatenate([members, jnp.zeros((8, 1024), f32)], axis=0)
        pltpu.make_async_copy(inv_hbm.at[c], inv.at[c], loaded.at[c]).wait()
        coupling = lax.dot_general(
            padded.astype(bf16), inv[c], (((1,), (1,)), ((), ())), preferred_element_type=f32
        )
        coefficient = members + coupling[0:8]
        upper = coefficient.astype(bf16).astype(f32)
        both = jnp.concatenate([upper, coefficient - upper], axis=0).astype(bf16)

        source_rows = cluster_rows(left, c, 32).T.astype(bf16)
        target_rows = cluster_rows(right, c, 32).astype(bf16)
        summed = jnp.zeros((16, 1024), f32)
        for p in range(4):
            exponent = jnp.dot(
                source_rows[256 * p : 256 * (p + 1)], target_rows, preferred_element_type=f32
            )
            kernel = jnp.exp2(exponent)
            kernel_high = kernel.astype(bf16)
            kernel_low = (kernel - kernel_high.astype(f32)).astype(bf16)
            part = both[:, 256 * p : 256 * (p + 1)]
            summed += jnp.dot(part, kernel_high, preferred_element_type=f32)
            summed += jnp.dot(part, kernel_low, preferred_element_type=f32)
        result[c] = (summed[0:8] + summed[8:16]) * weight_ref[c : c + 1, :]

    pick_messages(
        pick_ref,
        lambda k, r: result[r // 8, k : k + 1, (r % 8) * 128 : (r % 8 + 1) * 128],
        out_ref,
    )


def scatter_kernel(t_ref, vertex_ref, out_ref, values, places, total):
    def chunk(zy, carry):
        for j in range(4):
            vertex = vertex_ref[pl.ds(zy * 4 + j, 1), :]
            high = jnp.broadcast_to(jnp.right_shift(vertex, 7), (64, 128))
            low = jnp.broadcast_to(jnp.bitwise_and(vertex, 127), (128, 128))
            at_high = high == lax.broadcasted_iota(jnp.int32, (64, 128), 0)
            at_low = low == lax.broadcasted_iota(jnp.int32, (128, 128), 0)
            lanes = slice(128 * j, 128 * j + 128)
            places[:, lanes] = jnp.where(at_low, 1.0, 0.0).astype(bf16)
            for k in range(3):
                value = t_ref[zy, 4 * k + j : 4 * k + j + 1, :]
                for s, part in enumerate(three_parts(value)):
                    spread = jnp.broadcast_to(part, (64, 128))
                    top = (3 * k + s) * 64
                    values[top : top + 64, lanes] = jnp.where(at_high, spread, 0.0).astype(bf16)
        product = lax.dot_general(
            values[...], places[...], (((1,), (1,)), ((), ())), preferred_element_type=f32
        )
        total[...] += product
        return carry

    total[...] = jnp.zeros_like(total)
    lax.fori_loop(0, 16, chunk, 0)
    for k in range(3):
        top = 3 * k * 64
        for q in range(4):
            out_ref[k, :, 128 * q : 128 * (q + 1)] = (
                total[pl.ds(top + q, 16, stride=4), :]
                + total[pl.ds(top + 64 + q, 16, stride=4), :]
                + total[pl.ds(top + 128 + q, 16, stride=4), :]
            )


def swept(ref, out_ref, source, target, wall, scale=None):
    before, after = source - 1, source + 1
    rows = 16
    lane = lax.broadcasted_iota(jnp.int32, (rows, 512), 1)
    line = lax.broadcasted_iota(jnp.int32, (rows, 512), 0)
    for y in range(0, 96, rows):
        center = ref[source, y : y + rows, :]
        if y == 0:
            if wall:
                center = jnp.where(line == 0, 0.0, center)
            above = pltpu.roll(center, 1, 0)
        else:
            above = ref[source, y - 1 : y - 1 + rows, :]
        if y + rows == 96:
            below = jnp.where(line == rows - 1, 0.0, pltpu.roll(center, rows - 1, 0))
        else:
            below = ref[source, y + 1 : y + 1 + rows, :]
        beside = ref[before, y : y + rows, :] + ref[after, y : y + rows, :]
        beside = beside + (above + below)
        beside = beside + jnp.where(lane == 0, 0.0, pltpu.roll(center, 1, 1))
        beside = beside + jnp.where(lane == 511, 0.0, pltpu.roll(center, 511, 1))
        moved = center * keep_rate + beside * spread_rate
        if scale is not None:
            moved = moved * scale
        if y == 0:
            moved = jnp.where(line == 0, 0.0, moved)
        out_ref[target, y : y + rows, :] = moved


def smooth_kernel(edge_ref, mesh_hbm, left_hbm, right_hbm, out_hbm, field, once, arrived, leaving):
    def fetch(k):
        return (
            pltpu.make_async_copy(left_hbm.at[k], field.at[k, pl.ds(0, 2)], arrived.at[k, 0]),
            pltpu.make_async_copy(mesh_hbm.at[k], field.at[k, pl.ds(2, 16)], arrived.at[k, 1]),
            pltpu.make_async_copy(right_hbm.at[k], field.at[k, pl.ds(18, 2)], arrived.at[k, 2]),
        )

    def store(k):
        return pltpu.make_async_copy(field.at[k, pl.ds(2, 16)], out_hbm.at[k], leaving.at[k])

    for k in range(3):
        for copy in fetch(k):
            copy.start()
    for k in range(3):
        for copy in fetch(k):
            copy.wait()
        part = field.at[k]

        def first(x, carry):
            swept(part, once, x + 1, x, True)
            return carry

        def second(x, carry):
            swept(once, part, x + 1, x + 2, False)
            return carry

        swept(part, once, 1, 0, True, edge_ref[0])
        lax.fori_loop(1, 17, first, 0)
        swept(part, once, 18, 17, True, edge_ref[1])
        lax.fori_loop(0, 16, second, 0)
        store(k).start()
    for k in range(3):
        store(k).wait()


def wall_kernel(inter_ref, left_ref, right_ref, tile_ref, out_ref):
    inter = inter_ref[0]
    lane = lax.broadcasted_iota(jnp.int32, (16, 512), 1)
    line = lax.broadcasted_iota(jnp.int32, (16, 512), 0)
    before = jnp.where(line == 0, left_ref[0], pltpu.roll(inter, 1, 0))
    after = jnp.where(line == 15, right_ref[0], pltpu.roll(inter, 15, 0))
    beside = before + after
    beside = beside + jnp.where(lane == 0, 0.0, pltpu.roll(inter, 1, 1))
    beside = beside + jnp.where(lane == 511, 0.0, pltpu.roll(inter, 511, 1))
    first = spread_rate * ((1.0 + keep_rate) * inter + spread_rate * beside)
    second = (spread_rate * spread_rate) * inter
    row = lax.broadcasted_iota(jnp.int32, (8, 512), 0)
    for x in range(16):
        extra = jnp.where(
            row == 0,
            inter[x : x + 1],
            jnp.where(row == 1, first[x : x + 1], jnp.where(row == 2, second[x : x + 1], 0.0)),
        )
        out_ref[0, x] = tile_ref[0, x] + extra


def send_messages(displacement, send_node):
    return pl.pallas_call(
        send_kernel,
        out_shape=jax.ShapeDtypeStruct((24, 8, 128), f32),
        in_specs=[vmem()] * 2,
        out_specs=vmem(),
    )(displacement, send_node.reshape(64, 128))


def cluster_messages(
    table, member_slot, inverse_part, source_coord, target_coord, unity_weight, result_pick
):
    return pl.pallas_call(
        cluster_kernel,
        out_shape=jax.ShapeDtypeStruct((24, 8, 128), f32),
        in_specs=[vmem(), vmem(), pl.BlockSpec(memory_space=pl.ANY)] + [vmem()] * 4,
        out_specs=vmem(),
        scratch_shapes=[
            pltpu.VMEM((4, 1024, 1024), bf16),
            pltpu.SemaphoreType.DMA((4,)),
            pltpu.VMEM((8, 32, 128), f32),
            pltpu.VMEM((8, 128, 128), f32),
            pltpu.VMEM((8, 128, 128), f32),
            pltpu.VMEM((4, 8, 1024), f32),
        ],
        compiler_params=pltpu.CompilerParams(vmem_limit_bytes=40 << 20),
    )(
        table,
        member_slot,
        inverse_part,
        source_coord.transpose(1, 0, 2),
        target_coord.transpose(1, 0, 2),
        unity_weight,
        result_pick.reshape(64, 128),
    )


def scatter(table, receive_vertex):
    return pl.pallas_call(
        scatter_kernel,
        out_shape=jax.ShapeDtypeStruct((3, 16, 512), f32),
        in_specs=[vmem()] * 2,
        out_specs=vmem(),
        scratch_shapes=[
            pltpu.VMEM((576, 512), bf16),
            pltpu.VMEM((128, 512), bf16),
            pltpu.VMEM((576, 128), f32),
        ],
    )(table, receive_vertex.reshape(64, 128))


def smooth(edges, mesh_before, left, right):
    hbm = pl.BlockSpec(memory_space=pl.ANY)
    return pl.pallas_call(
        smooth_kernel,
        out_shape=jax.ShapeDtypeStruct((3, 16, 96, 512), f32),
        in_specs=[pl.BlockSpec(memory_space=pltpu.SMEM), hbm, hbm, hbm],
        out_specs=hbm,
        scratch_shapes=[
            pltpu.VMEM((3, 20, 96, 512), f32),
            pltpu.VMEM((18, 96, 512), f32),
            pltpu.SemaphoreType.DMA((3, 3)),
            pltpu.SemaphoreType.DMA((3,)),
        ],
        compiler_params=pltpu.CompilerParams(vmem_limit_bytes=24 << 20),
    )(edges, mesh_before, left, right)


def add_wall(interface, left, right, field):
    tile = pl.BlockSpec((1, 16, 8, 512), lambda k: (k, 0, 0, 0))
    return pl.pallas_call(
        wall_kernel,
        grid=(3,),
        out_shape=jax.ShapeDtypeStruct((3, 16, 96, 512), f32),
        in_specs=[
            pl.BlockSpec((1, 16, 512), lambda k: (k, 0, 0)),
            pl.BlockSpec((1, 1, 512), lambda k: (k, 0, 0)),
            pl.BlockSpec((1, 1, 512), lambda k: (k, 0, 0)),
            tile,
        ],
        out_specs=tile,
        input_output_aliases={3: 0},
    )(interface, left, right, field)


def local(
    displacement,
    send_node,
    member_slot,
    inverse_part,
    source_coord,
    target_coord,
    unity_weight,
    result_pick,
    receive_vertex,
    mesh_before,
):
    count = lax.axis_size("dev")
    me = lax.axis_index("dev")
    up = [(i, i + 1) for i in range(count - 1)]
    down = [(i + 1, i) for i in range(count - 1)]
    edges = jnp.stack([me > 0, me < count - 1]).astype(f32)

    mesh_left = lax.ppermute(mesh_before[:, 14:16], "dev", up)
    mesh_right = lax.ppermute(mesh_before[:, 0:2], "dev", down)

    messages = send_messages(displacement, send_node)
    table = exchange(messages, 1)
    results = cluster_messages(
        table, member_slot, inverse_part, source_coord, target_coord, unity_weight, result_pick
    )
    returned = exchange(results, 1)
    interface = scatter(returned, receive_vertex)
    wall_left = lax.ppermute(interface[:, 15:16], "dev", up)
    wall_right = lax.ppermute(interface[:, 0:1], "dev", down)
    field = smooth(edges, mesh_before, mesh_left, mesh_right)
    return add_wall(interface, wall_left, wall_right, field)


def solution(mesh):
    in_specs = (
        P(None, "dev"),
        P("dev"),
        P("dev", None),
        P("dev", None, None),
        P("dev", None, None),
        P("dev", None, None),
        P("dev", None),
        P("dev"),
        P("dev"),
        P(None, "dev", None, None),
    )
    out_specs = P(None, "dev", None, None)
    return jax.shard_map(local, mesh=mesh, in_specs=in_specs, out_specs=out_specs, check_vma=False)
```

```python
import jax
import jax.numpy as jnp
from jax import lax
from jax.experimental import pallas as pl
from jax.experimental.pallas import tpu as pltpu
from jax.sharding import PartitionSpec as P

relax_rate = 0.8
kernel_sharpness = 8.0
log2_e = 1.4426950408889634
spread_rate = relax_rate / 6.0
keep_rate = 1.0 - relax_rate

MESH = pl.DeviceIdType.MESH
f32 = jnp.float32
bf16 = jnp.bfloat16


def vmem():
    return pl.BlockSpec(memory_space=pltpu.VMEM)


def lookup(row, lanes):
    spread = jnp.broadcast_to(row, lanes.shape)
    return jnp.take_along_axis(spread, lanes, axis=1, mode="promise_in_bounds")


def message_index(index_ref, step):
    x, core = step // 2, step % 2
    even = index_ref[pl.ds(x, 8, stride=8), :]
    odd = index_ref[pl.ds(4 + x, 8, stride=8), :]
    lane = lax.broadcasted_iota(jnp.int32, (8, 128), 1)
    if core == 0:
        return jnp.where(lane < 64, even, pltpu.roll(odd, 64, 1))
    return jnp.where(lane < 64, pltpu.roll(even, 64, 1), odd)


def pick_messages(index_ref, row_of, out_ref):
    for half in range(2):
        index = [message_index(index_ref, 4 * half + g) for g in range(4)]
        high = [jnp.right_shift(i, 7) for i in index]
        low = [jnp.bitwise_and(i, 127) for i in index]
        total = [[jnp.zeros((8, 128), f32) for _ in range(3)] for _ in range(4)]
        for r in range(32):
            hit = [h == r for h in high]
            for k in range(3):
                row = row_of(k, r)
                for g in range(4):
                    total[g][k] = jnp.where(hit[g], lookup(row, low[g]), total[g][k])
        for g in range(4):
            for k in range(3):
                top = ((4 * half + g) * 3 + k) * 8
                out_ref[top : top + 8, :] = total[g][k]


def three_parts(value):
    high = value.astype(bf16).astype(f32)
    rest = value - high
    middle = rest.astype(bf16).astype(f32)
    return high, middle, rest - middle


def cluster_rows(ref, c, rows):
    return jnp.concatenate([ref[q, pl.ds(c, rows, stride=4), :] for q in range(8)], axis=1)


def remote(source, target, send, receive, device):
    copy = pltpu.make_async_remote_copy(
        src_ref=source,
        dst_ref=target,
        send_sem=send,
        recv_sem=receive,
        device_id=(device,),
        device_id_type=MESH,
    )
    copy.start()
    return copy


def first_stage(messages, held, send, receive, outer, inner):
    copies = []
    for i in range(1, 8):
        p = (inner + i) % 8
        copies.append(
            remote(
                messages.at[pl.ds(pl.multiple_of(p * 24, 8), 24)],
                held.at[pl.ds(pl.multiple_of(inner * 24, 8), 24)],
                send.at[i - 1],
                receive.at[i - 1],
                outer * 8 + p,
            )
        )
    mine = pl.ds(pl.multiple_of(inner * 24, 8), 24)
    held[mine, :] = messages[mine, :]
    return copies


def second_stage(held, ready, landed, send, receive, outer, inner):
    lane = lax.broadcasted_iota(jnp.int32, (4, 128), 1)
    for m in range(8):
        for k in range(3):
            first = held[pl.ds(k * 8 + m, 4, stride=48), :]
            second = held[pl.ds(24 + k * 8 + m, 4, stride=48), :]
            ready[2 * m, 4 * k : 4 * k + 4, :] = jnp.where(
                lane < 64, first, pltpu.roll(second, 64, 1)
            )
            ready[2 * m + 1, 4 * k : 4 * k + 4, :] = jnp.where(
                lane < 64, pltpu.roll(first, 64, 1), second
            )
    copies = []
    for i in range(1, 16):
        p = (outer + i) % 16
        copies.append(
            remote(
                ready.at[p],
                landed.at[outer],
                send.at[i - 1],
                receive.at[i - 1],
                p * 8 + inner,
            )
        )
    landed[outer] = ready[outer]
    return copies


def finish(copies):
    for copy in copies:
        copy.wait()


def exponent_rows(source_ref, target_ref, left, right):
    left[...] = jnp.zeros_like(left)
    right[...] = jnp.zeros_like(right)
    ones = jnp.ones((4, 1024), f32)
    source_norm = jnp.zeros((4, 1024), f32)
    target_norm = jnp.zeros((4, 1024), f32)
    pairs = []
    for d in range(3):
        s = source_ref[d]
        t = target_ref[d]
        source_norm += s * s
        target_norm += t * t
        sh, sm, sl = three_parts(s)
        th, tm, tl = three_parts(t * (2.0 * kernel_sharpness * log2_e))
        pairs += [(sh, th), (sh, tm), (sm, th), (sh, tl), (sl, th), (sm, tm)]
    pairs += [(p, ones) for p in three_parts(source_norm * (-kernel_sharpness * log2_e))]
    pairs += [(ones, p) for p in three_parts(target_norm * (-kernel_sharpness * log2_e))]
    for row, (a, b) in enumerate(pairs):
        for q in range(8):
            left[q, 4 * row : 4 * row + 4, :] = a[:, 128 * q : 128 * (q + 1)]
            right[q, 4 * row : 4 * row + 4, :] = b[:, 128 * q : 128 * (q + 1)]


def kernel_values(c, left, right, upper, lower):
    source_rows = cluster_rows(left, c, 32).T.astype(bf16)
    target_rows = cluster_rows(right, c, 32).astype(bf16)
    for p in range(4):
        rows = slice(256 * p, 256 * (p + 1))
        kernel = jnp.exp2(jnp.dot(source_rows[rows], target_rows, preferred_element_type=f32))
        high = kernel.astype(bf16)
        upper[c, rows, :] = high
        lower[c, rows, :] = (kernel - high.astype(f32)).astype(bf16)


def gather_members(table, slot_ref, member):
    member[...] = jnp.zeros_like(member)
    index = [
        jnp.concatenate(
            [slot_ref[:, 256 * m : 256 * m + 128], slot_ref[:, 256 * m + 128 : 256 * m + 256]],
            axis=0,
        )
        for m in range(4)
    ]
    high = [jnp.right_shift(i, 7) for i in index]
    low = [jnp.bitwise_and(i, 127) for i in index]

    def gather(zy, total):
        total = list(total)
        for j in range(4):
            hit = [h == zy * 4 + j for h in high]
            for k in range(3):
                line = table[zy, 4 * k + j : 4 * k + j + 1, :]
                for m in range(4):
                    total[3 * m + k] = jnp.where(hit[m], lookup(line, low[m]), total[3 * m + k])
        return tuple(total)

    total = lax.fori_loop(
        0, 16, gather, tuple(jnp.zeros((8, 128), f32) for _ in range(12))
    )
    for m in range(4):
        for k in range(3):
            value = total[3 * m + k]
            member[2 * m, 4 * k : 4 * k + 4, :] = value[0:4]
            member[2 * m + 1, 4 * k : 4 * k + 4, :] = value[4:8]


def contribute(c, member, inverse, upper, lower, weight_ref, result):
    members = cluster_rows(member, c, 8)
    padded = jnp.concatenate([members, jnp.zeros((8, 1024), f32)], axis=0)
    coupling = lax.dot_general(
        padded.astype(bf16), inverse[c], (((1,), (1,)), ((), ())), preferred_element_type=f32
    )
    coefficient = members + coupling[0:8]
    high = coefficient.astype(bf16).astype(f32)
    both = jnp.concatenate([high, coefficient - high], axis=0).astype(bf16)
    summed = jnp.dot(both, upper[c], preferred_element_type=f32)
    summed += jnp.dot(both, lower[c], preferred_element_type=f32)
    result[c] = (summed[0:8] + summed[8:16]) * weight_ref[c : c + 1, :]


def scatter(table, vertex_ref, values, places, total, out_ref):
    def chunk(zy, carry):
        for j in range(4):
            vertex = vertex_ref[pl.ds(zy * 4 + j, 1), :]
            high = jnp.broadcast_to(jnp.right_shift(vertex, 7), (64, 128))
            low = jnp.broadcast_to(jnp.bitwise_and(vertex, 127), (128, 128))
            at_high = high == lax.broadcasted_iota(jnp.int32, (64, 128), 0)
            at_low = low == lax.broadcasted_iota(jnp.int32, (128, 128), 0)
            lanes = slice(128 * j, 128 * j + 128)
            places[:, lanes] = jnp.where(at_low, 1.0, 0.0).astype(bf16)
            for k in range(3):
                value = table[zy, 4 * k + j : 4 * k + j + 1, :]
                for s, part in enumerate(three_parts(value)):
                    spread = jnp.broadcast_to(part, (64, 128))
                    top = (3 * k + s) * 64
                    values[top : top + 64, lanes] = jnp.where(at_high, spread, 0.0).astype(bf16)
        product = lax.dot_general(
            values[...], places[...], (((1,), (1,)), ((), ())), preferred_element_type=f32
        )
        total[...] += product
        return carry

    total[...] = jnp.zeros_like(total)
    lax.fori_loop(0, 16, chunk, 0)
    for k in range(3):
        top = 3 * k * 64
        for q in range(4):
            out_ref[k, :, 128 * q : 128 * (q + 1)] = (
                total[pl.ds(top + q, 16, stride=4), :]
                + total[pl.ds(top + 64 + q, 16, stride=4), :]
                + total[pl.ds(top + 128 + q, 16, stride=4), :]
            )


def transfer_kernel(
    disp_ref, node_ref, slot_ref, source_ref, target_ref, weight_ref, pick_ref, vertex_ref,
    inv_hbm, mesh_hbm,
    inter_ref, edge_ref, left_hbm, right_hbm,
    messages, held, ready, landed, messages2, held2, ready2, landed2,
    inverse, member, left, right, upper, lower, result, values, places, total, ends, near,
    loaded, send1, recv1, send2, recv2, send3, recv3, send4, recv4, send5, recv5,
):
    me = lax.axis_index("dev")
    outer, inner = me // 8, me % 8
    before, after = (me + 127) % 128, (me + 1) % 128

    barrier = pltpu.get_barrier_semaphore()
    peers = [outer * 8 + (inner + i) % 8 for i in range(1, 8)]
    peers += [((outer + i) % 16) * 8 + inner for i in range(1, 16)]
    peers += [before, after]
    for peer in peers:
        pl.semaphore_signal(barrier, inc=1, device_id=(peer,), device_id_type=MESH)
    loads = [pltpu.make_async_copy(inv_hbm.at[c], inverse.at[c], loaded.at[c]) for c in range(4)]
    for load in loads:
        load.start()

    pick_messages(
        node_ref, lambda k, r: disp_ref[k : k + 1, r * 128 : (r + 1) * 128], messages
    )
    pl.semaphore_wait(barrier, 24)

    copies = first_stage(messages, held, send1, recv1, outer, inner)
    exponent_rows(source_ref, target_ref, left, right)
    kernel_values(0, left, right, upper, lower)
    finish(copies)
    copies = second_stage(held, ready, landed, send2, recv2, outer, inner)
    halos = [
        remote(mesh_hbm.at[:, pl.ds(14, 2)], left_hbm, send5.at[0], recv5.at[0], after),
        remote(mesh_hbm.at[:, pl.ds(0, 2)], right_hbm, send5.at[1], recv5.at[1], before),
    ]
    for c in range(1, 4):
        kernel_values(c, left, right, upper, lower)
    finish(copies)

    gather_members(landed, slot_ref, member)
    for c in range(4):
        loads[c].wait()
        contribute(c, member, inverse, upper, lower, weight_ref, result)
    pick_messages(
        pick_ref,
        lambda k, r: result[r // 8, k : k + 1, (r % 8) * 128 : (r % 8 + 1) * 128],
        messages2,
    )
    finish(first_stage(messages2, held2, send3, recv3, outer, inner))
    finish(second_stage(held2, ready2, landed2, send4, recv4, outer, inner))

    scatter(landed2, vertex_ref, values, places, total, inter_ref)
    ends[...] = jnp.zeros_like(ends)
    for k in range(3):
        ends[0, k : k + 1, :] = inter_ref[k, 0:1, :]
        ends[1, k : k + 1, :] = inter_ref[k, 15:16, :]
    edges = [
        remote(ends.at[1], near.at[0], send5.at[2], recv5.at[2], after),
        remote(ends.at[0], near.at[1], send5.at[3], recv5.at[3], before),
    ]
    finish(edges)
    edge_ref[...] = near[...]
    finish(halos)


def swept(ref, out_ref, source, target, inside=None):
    rows = 16
    lane = lax.broadcasted_iota(jnp.int32, (rows, 512), 1)
    line = lax.broadcasted_iota(jnp.int32, (rows, 512), 0)
    for y in range(0, 96, rows):
        center = ref[source, y : y + rows, :]
        if y == 0:
            above = pltpu.roll(center, 1, 0)
        else:
            above = ref[source, y - 1 : y - 1 + rows, :]
        if y + rows == 96:
            below = jnp.where(line == rows - 1, 0.0, pltpu.roll(center, rows - 1, 0))
        else:
            below = ref[source, y + 1 : y + 1 + rows, :]
        beside = ref[source - 1, y : y + rows, :] + ref[source + 1, y : y + rows, :]
        beside = beside + (above + below)
        beside = beside + jnp.where(lane == 0, 0.0, pltpu.roll(center, 1, 1))
        beside = beside + jnp.where(lane == 511, 0.0, pltpu.roll(center, 511, 1))
        moved = center * keep_rate + beside * spread_rate
        if y == 0:
            moved = jnp.where(line == 0, center, moved)
        if inside is not None:
            moved = jnp.where(inside, moved, 0.0)
        out_ref[target, y : y + rows, :] = moved


def smooth_kernel(
    place_ref, inter_ref, edge_ref, mesh_hbm, left_hbm, right_hbm, out_hbm,
    field, once, arrived, leaving,
):
    place = place_ref[0]
    has_left, has_right = place > 0, place < 127

    def fetch(k):
        return (
            pltpu.make_async_copy(left_hbm.at[k], field.at[k, pl.ds(0, 2)], arrived.at[k, 0]),
            pltpu.make_async_copy(mesh_hbm.at[k], field.at[k, pl.ds(2, 16)], arrived.at[k, 1]),
            pltpu.make_async_copy(right_hbm.at[k], field.at[k, pl.ds(18, 2)], arrived.at[k, 2]),
        )

    def store(k):
        return pltpu.make_async_copy(field.at[k, pl.ds(2, 16)], out_hbm.at[k], leaving.at[k])

    for k in range(3):
        for copy in fetch(k):
            copy.start()
    for k in range(3):
        for copy in fetch(k):
            copy.wait()
        part = field.at[k]
        for x in range(16):
            part[x + 2, 0:1, :] = inter_ref[k, x : x + 1, :]
        part[1, 0:1, :] = edge_ref[0, k : k + 1, :]
        part[18, 0:1, :] = edge_ref[1, k : k + 1, :]

        @pl.when(jnp.logical_not(has_left))
        def _():
            part[1] = jnp.zeros((96, 512), f32)

        @pl.when(jnp.logical_not(has_right))
        def _():
            part[18] = jnp.zeros((96, 512), f32)

        def first(x, carry):
            swept(part, once, x + 1, x)
            return carry

        def second(x, carry):
            swept(once, part, x + 1, x + 2)
            return carry

        swept(part, once, 1, 0, has_left)
        lax.fori_loop(1, 17, first, 0)
        swept(part, once, 18, 17, has_right)
        lax.fori_loop(0, 16, second, 0)
        store(k).start()
    for k in range(3):
        store(k).wait()


def transfer(
    displacement, send_node, member_slot, inverse_part, source_coord, target_coord,
    unity_weight, result_pick, receive_vertex, mesh_before,
):
    hbm = pl.BlockSpec(memory_space=pl.ANY)
    dma = pltpu.SemaphoreType.DMA
    halo = jax.ShapeDtypeStruct((3, 2, 96, 512), f32)
    exchange = [
        pltpu.VMEM((192, 128), f32),
        pltpu.VMEM((192, 128), f32),
        pltpu.VMEM((16, 12, 128), f32),
        pltpu.VMEM((16, 12, 128), f32),
    ]
    return pl.pallas_call(
        transfer_kernel,
        out_shape=(
            jax.ShapeDtypeStruct((3, 16, 512), f32),
            jax.ShapeDtypeStruct((2, 8, 512), f32),
            halo,
            halo,
        ),
        in_specs=[vmem()] * 8 + [hbm, hbm],
        out_specs=(vmem(), vmem(), hbm, hbm),
        scratch_shapes=exchange
        + exchange
        + [
            pltpu.VMEM((4, 1024, 1024), bf16),
            pltpu.VMEM((8, 32, 128), f32),
            pltpu.VMEM((8, 128, 128), f32),
            pltpu.VMEM((8, 128, 128), f32),
            pltpu.VMEM((4, 1024, 1024), bf16),
            pltpu.VMEM((4, 1024, 1024), bf16),
            pltpu.VMEM((4, 8, 1024), f32),
            pltpu.VMEM((576, 512), bf16),
            pltpu.VMEM((128, 512), bf16),
            pltpu.VMEM((576, 128), f32),
            pltpu.VMEM((2, 8, 512), f32),
            pltpu.VMEM((2, 8, 512), f32),
            dma((4,)),
            dma((7,)),
            dma((7,)),
            dma((15,)),
            dma((15,)),
            dma((7,)),
            dma((7,)),
            dma((15,)),
            dma((15,)),
            dma((4,)),
            dma((4,)),
        ],
        compiler_params=pltpu.CompilerParams(
            collective_id=1, has_side_effects=True, vmem_limit_bytes=48 << 20
        ),
    )(
        displacement,
        send_node.reshape(64, 128),
        member_slot,
        source_coord.transpose(1, 0, 2),
        target_coord.transpose(1, 0, 2),
        unity_weight,
        result_pick.reshape(64, 128),
        receive_vertex.reshape(64, 128),
        inverse_part,
        mesh_before,
    )


def smooth(place, interface, edges, mesh_before, left, right):
    hbm = pl.BlockSpec(memory_space=pl.ANY)
    return pl.pallas_call(
        smooth_kernel,
        out_shape=jax.ShapeDtypeStruct((3, 16, 96, 512), f32),
        in_specs=[pl.BlockSpec(memory_space=pltpu.SMEM), vmem(), vmem(), hbm, hbm, hbm],
        out_specs=hbm,
        scratch_shapes=[
            pltpu.VMEM((3, 20, 96, 512), f32),
            pltpu.VMEM((18, 96, 512), f32),
            pltpu.SemaphoreType.DMA((3, 3)),
            pltpu.SemaphoreType.DMA((3,)),
        ],
        compiler_params=pltpu.CompilerParams(vmem_limit_bytes=56 << 20),
    )(place, interface, edges, mesh_before, left, right)


def local(
    displacement,
    send_node,
    member_slot,
    inverse_part,
    source_coord,
    target_coord,
    unity_weight,
    result_pick,
    receive_vertex,
    mesh_before,
):
    place = lax.axis_index("dev").astype(jnp.int32).reshape(1)
    interface, edges, left, right = transfer(
        displacement, send_node, member_slot, inverse_part, source_coord, target_coord,
        unity_weight, result_pick, receive_vertex, mesh_before,
    )
    return smooth(place, interface, edges, mesh_before, left, right)


def solution(mesh):
    in_specs = (
        P(None, "dev"),
        P("dev"),
        P("dev", None),
        P("dev", None, None),
        P("dev", None, None),
        P("dev", None, None),
        P("dev", None),
        P("dev"),
        P("dev"),
        P(None, "dev", None, None),
    )
    out_specs = P(None, "dev", None, None)
    return jax.shard_map(local, mesh=mesh, in_specs=in_specs, out_specs=out_specs, check_vma=False)
```

```python
import jax
import jax.numpy as jnp
from jax import lax
from jax.experimental import pallas as pl
from jax.experimental.pallas import tpu as pltpu
from jax.sharding import PartitionSpec as P

relax_rate = 0.8
kernel_sharpness = 8.0
log2_e = 1.4426950408889634
spread_rate = relax_rate / 6.0
keep_rate = 1.0 - relax_rate

MESH = pl.DeviceIdType.MESH
f32 = jnp.float32
bf16 = jnp.bfloat16


def vmem():
    return pl.BlockSpec(memory_space=pltpu.VMEM)


def lookup(row, lanes):
    spread = jnp.broadcast_to(row, lanes.shape)
    return jnp.take_along_axis(spread, lanes, axis=1, mode="promise_in_bounds")


def message_index(index_ref, step):
    x, core = step // 2, step % 2
    even = index_ref[pl.ds(x, 8, stride=8), :]
    odd = index_ref[pl.ds(4 + x, 8, stride=8), :]
    lane = lax.broadcasted_iota(jnp.int32, (8, 128), 1)
    if core == 0:
        return jnp.where(lane < 64, even, pltpu.roll(odd, 64, 1))
    return jnp.where(lane < 64, pltpu.roll(even, 64, 1), odd)


def pick_messages(index_ref, row_of, out_ref):
    for half in range(2):
        index = [message_index(index_ref, 4 * half + g) for g in range(4)]
        high = [jnp.right_shift(i, 7) for i in index]
        low = [jnp.bitwise_and(i, 127) for i in index]
        total = [[jnp.zeros((8, 128), f32) for _ in range(3)] for _ in range(4)]
        for r in range(32):
            hit = [h == r for h in high]
            for k in range(3):
                row = row_of(k, r)
                for g in range(4):
                    total[g][k] = jnp.where(hit[g], lookup(row, low[g]), total[g][k])
        for g in range(4):
            for k in range(3):
                top = ((4 * half + g) * 3 + k) * 8
                out_ref[top : top + 8, :] = total[g][k]


def three_parts(value):
    high = value.astype(bf16).astype(f32)
    rest = value - high
    middle = rest.astype(bf16).astype(f32)
    return high, middle, rest - middle


def cluster_rows(ref, c, rows):
    return jnp.concatenate([ref[q, pl.ds(c, rows, stride=4), :] for q in range(8)], axis=1)


def remote(source, target, send, receive, device):
    copy = pltpu.make_async_remote_copy(
        src_ref=source,
        dst_ref=target,
        send_sem=send,
        recv_sem=receive,
        device_id=(device,),
        device_id_type=MESH,
    )
    copy.start()
    return copy


def first_stage(messages, held, send, receive, outer, inner):
    copies = []
    for i in range(1, 8):
        p = (inner + i) % 8
        copies.append(
            remote(
                messages.at[pl.ds(pl.multiple_of(p * 24, 8), 24)],
                held.at[pl.ds(pl.multiple_of(inner * 24, 8), 24)],
                send.at[i - 1],
                receive.at[i - 1],
                outer * 8 + p,
            )
        )
    mine = pl.ds(pl.multiple_of(inner * 24, 8), 24)
    held[mine, :] = messages[mine, :]
    return copies


def second_stage(held, ready, landed, send, receive, outer, inner):
    lane = lax.broadcasted_iota(jnp.int32, (4, 128), 1)
    for m in range(8):
        for k in range(3):
            first = held[pl.ds(k * 8 + m, 4, stride=48), :]
            second = held[pl.ds(24 + k * 8 + m, 4, stride=48), :]
            ready[2 * m, 4 * k : 4 * k + 4, :] = jnp.where(
                lane < 64, first, pltpu.roll(second, 64, 1)
            )
            ready[2 * m + 1, 4 * k : 4 * k + 4, :] = jnp.where(
                lane < 64, pltpu.roll(first, 64, 1), second
            )
    copies = []
    for i in range(1, 16):
        p = (outer + i) % 16
        copies.append(
            remote(
                ready.at[p],
                landed.at[outer],
                send.at[i - 1],
                receive.at[i - 1],
                p * 8 + inner,
            )
        )
    landed[outer] = ready[outer]
    return copies


def finish(copies):
    for copy in copies:
        copy.wait()


def exponent_rows(source_ref, target_ref, left, right):
    left[...] = jnp.zeros_like(left)
    right[...] = jnp.zeros_like(right)
    ones = jnp.ones((4, 1024), f32)
    source_norm = jnp.zeros((4, 1024), f32)
    target_norm = jnp.zeros((4, 1024), f32)
    pairs = []
    for d in range(3):
        s = source_ref[d]
        t = target_ref[d]
        source_norm += s * s
        target_norm += t * t
        sh, sm, sl = three_parts(s)
        th, tm, tl = three_parts(t * (2.0 * kernel_sharpness * log2_e))
        pairs += [(sh, th), (sh, tm), (sm, th), (sh, tl), (sl, th), (sm, tm)]
    pairs += [(p, ones) for p in three_parts(source_norm * (-kernel_sharpness * log2_e))]
    pairs += [(ones, p) for p in three_parts(target_norm * (-kernel_sharpness * log2_e))]
    for row, (a, b) in enumerate(pairs):
        for q in range(8):
            left[q, 4 * row : 4 * row + 4, :] = a[:, 128 * q : 128 * (q + 1)]
            right[q, 4 * row : 4 * row + 4, :] = b[:, 128 * q : 128 * (q + 1)]


def kernel_values(c, left, right, upper, lower):
    source_rows = cluster_rows(left, c, 32).T.astype(bf16)
    target_rows = cluster_rows(right, c, 32).astype(bf16)
    for p in range(4):
        rows = slice(256 * p, 256 * (p + 1))
        kernel = jnp.exp2(jnp.dot(source_rows[rows], target_rows, preferred_element_type=f32))
        high = kernel.astype(bf16)
        upper[c, rows, :] = high
        lower[c, rows, :] = (kernel - high.astype(f32)).astype(bf16)


def gather_members(table, slot_ref, member):
    member[...] = jnp.zeros_like(member)
    index = [
        jnp.concatenate(
            [slot_ref[:, 256 * m : 256 * m + 128], slot_ref[:, 256 * m + 128 : 256 * m + 256]],
            axis=0,
        )
        for m in range(4)
    ]
    high = [jnp.right_shift(i, 7) for i in index]
    low = [jnp.bitwise_and(i, 127) for i in index]

    def gather(part, total):
        total = list(total)
        for r in range(16):
            zy, j = part * 4 + r // 4, r % 4
            hit = [h == part * 16 + r for h in high]
            for k in range(3):
                line = table[zy, 4 * k + j : 4 * k + j + 1, :]
                for m in range(4):
                    total[3 * m + k] = jnp.where(hit[m], lookup(line, low[m]), total[3 * m + k])
        return tuple(total)

    total = lax.fori_loop(
        0, 4, gather, tuple(jnp.zeros((8, 128), f32) for _ in range(12))
    )
    for m in range(4):
        for k in range(3):
            value = total[3 * m + k]
            member[2 * m, 4 * k : 4 * k + 4, :] = value[0:4]
            member[2 * m + 1, 4 * k : 4 * k + 4, :] = value[4:8]


def contribute(c, member, inverse, upper, lower, weight_ref, result):
    members = cluster_rows(member, c, 8)
    padded = jnp.concatenate([members, jnp.zeros((8, 1024), f32)], axis=0)
    coupling = lax.dot_general(
        padded.astype(bf16), inverse[c], (((1,), (1,)), ((), ())), preferred_element_type=f32
    )
    coefficient = members + coupling[0:8]
    high = coefficient.astype(bf16).astype(f32)
    both = jnp.concatenate([high, coefficient - high], axis=0).astype(bf16)
    summed = jnp.dot(both, upper[c], preferred_element_type=f32)
    summed += jnp.dot(both, lower[c], preferred_element_type=f32)
    result[c] = (summed[0:8] + summed[8:16]) * weight_ref[c : c + 1, :]


def scatter(table, vertex_ref, values, places, total, out_ref):
    def chunk(group, carry):
        product = jnp.zeros((384, 128), f32)
        for part in range(4):
            zy = group * 4 + part
            for j in range(4):
                vertex = vertex_ref[pl.ds(zy * 4 + j, 1), :]
                high = jnp.broadcast_to(jnp.right_shift(vertex, 7), (64, 128))
                low = jnp.broadcast_to(jnp.bitwise_and(vertex, 127), (128, 128))
                at_high = high == lax.broadcasted_iota(jnp.int32, (64, 128), 0)
                at_low = low == lax.broadcasted_iota(jnp.int32, (128, 128), 0)
                lanes = slice(128 * j, 128 * j + 128)
                places[part, :, lanes] = jnp.where(at_low, 1.0, 0.0).astype(bf16)
                for k in range(3):
                    value = table[zy, 4 * k + j : 4 * k + j + 1, :]
                    upper = value.astype(bf16).astype(f32)
                    for s, half in enumerate((upper, value - upper)):
                        spread = jnp.broadcast_to(half, (64, 128))
                        top = (2 * k + s) * 64
                        values[part, top : top + 64, lanes] = jnp.where(
                            at_high, spread, 0.0
                        ).astype(bf16)
            product += lax.dot_general(
                values[part],
                places[part],
                (((1,), (1,)), ((), ())),
                preferred_element_type=f32,
            )
        total[...] += product
        return carry

    total[...] = jnp.zeros_like(total)
    lax.fori_loop(0, 4, chunk, 0)
    for k in range(3):
        top = 2 * k * 64
        for q in range(4):
            out_ref[k, :, 128 * q : 128 * (q + 1)] = (
                total[pl.ds(top + q, 16, stride=4), :]
                + total[pl.ds(top + 64 + q, 16, stride=4), :]
            )


def swept(ref, out_ref, source, target, inside=None):
    rows = 16
    lane = lax.broadcasted_iota(jnp.int32, (rows, 512), 1)
    line = lax.broadcasted_iota(jnp.int32, (rows, 512), 0)
    for y in range(0, 96, rows):
        center = ref[source, y : y + rows, :]
        if y == 0:
            above = pltpu.roll(center, 1, 0)
        else:
            above = ref[source, y - 1 : y - 1 + rows, :]
        if y + rows == 96:
            below = jnp.where(line == rows - 1, 0.0, pltpu.roll(center, rows - 1, 0))
        else:
            below = ref[source, y + 1 : y + 1 + rows, :]
        beside = ref[source - 1, y : y + rows, :] + ref[source + 1, y : y + rows, :]
        beside = beside + (above + below)
        beside = beside + jnp.where(lane == 0, 0.0, pltpu.roll(center, 1, 1))
        beside = beside + jnp.where(lane == 511, 0.0, pltpu.roll(center, 511, 1))
        moved = center * keep_rate + beside * spread_rate
        if y == 0:
            moved = jnp.where(line == 0, center, moved)
        if inside is not None:
            moved = jnp.where(inside, moved, 0.0)
        out_ref[target, y : y + rows, :] = moved


def sweep_once(field, once, has_left, has_right):
    def plane(x, carry):
        swept(field, once, x + 1, x)
        return carry

    swept(field, once, 1, 0, has_left)
    lax.fori_loop(1, 17, plane, 0)
    swept(field, once, 18, 17, has_right)


def sweep_again(field, once):
    def plane(x, carry):
        swept(once, field, x + 1, x + 2)
        return carry

    lax.fori_loop(0, 16, plane, 0)


def close_ends(field, has_left, has_right):
    @pl.when(jnp.logical_not(has_left))
    def _():
        field[1] = jnp.zeros((96, 512), f32)

    @pl.when(jnp.logical_not(has_right))
    def _():
        field[18] = jnp.zeros((96, 512), f32)


def add_wall(inter, before, after, field):
    lane = lax.broadcasted_iota(jnp.int32, (16, 512), 1)
    line = lax.broadcasted_iota(jnp.int32, (16, 512), 0)
    beside = jnp.where(line == 0, before, pltpu.roll(inter, 1, 0))
    beside = beside + jnp.where(line == 15, after, pltpu.roll(inter, 15, 0))
    beside = beside + jnp.where(lane == 0, 0.0, pltpu.roll(inter, 1, 1))
    beside = beside + jnp.where(lane == 511, 0.0, pltpu.roll(inter, 511, 1))
    first = spread_rate * ((1.0 + keep_rate) * inter + spread_rate * beside)
    second = (spread_rate * spread_rate) * inter
    row = lax.broadcasted_iota(jnp.int32, (8, 512), 0)
    for x in range(16):
        extra = jnp.where(
            row == 0,
            inter[x : x + 1],
            jnp.where(row == 1, first[x : x + 1], jnp.where(row == 2, second[x : x + 1], 0.0)),
        )
        field[x + 2, 0:8, :] += extra


def transfer_kernel(
    disp_hbm, node_hbm, slot_hbm, source_hbm, target_hbm, weight_hbm, pick_hbm, vertex_hbm,
    inv_hbm, mesh_hbm,
    inter_hbm, edge_hbm, left_hbm, right_hbm, part_hbm,
    disp_ref, node_ref, slot_ref, source_ref, target_ref, weight_ref, pick_ref, vertex_ref,
    messages, held, ready, landed, messages2, held2, ready2, landed2,
    inverse, member, left, right, upper, lower, result, values, places, total,
    inter_ref, ends, near, field, once,
    fetched, loaded, send1, recv1, send2, recv2, send3, recv3, send4, recv4, send5, recv5, stored,
):
    me = lax.axis_index("dev")
    outer, inner = me // 8, me % 8
    before, after = (me + 127) % 128, (me + 1) % 128
    has_left, has_right = me > 0, me < 127

    small = [
        (disp_hbm, disp_ref), (node_hbm, node_ref), (slot_hbm, slot_ref),
        (source_hbm, source_ref), (target_hbm, target_ref), (weight_hbm, weight_ref),
        (pick_hbm, pick_ref), (vertex_hbm, vertex_ref),
    ]
    fetches = [pltpu.make_async_copy(a, b, fetched.at[i]) for i, (a, b) in enumerate(small)]
    for fetch in fetches:
        fetch.start()
    barrier = pltpu.get_barrier_semaphore()
    peers = [outer * 8 + (inner + i) % 8 for i in range(1, 8)]
    peers += [((outer + i) % 16) * 8 + inner for i in range(1, 16)]
    peers += [before, after]
    for peer in peers:
        pl.semaphore_signal(barrier, inc=1, device_id=(peer,), device_id_type=MESH)
    loads = [pltpu.make_async_copy(inv_hbm.at[c], inverse.at[c], loaded.at[c]) for c in range(4)]
    loads.append(pltpu.make_async_copy(mesh_hbm.at[0], field.at[pl.ds(2, 16)], loaded.at[4]))
    for load in loads:
        load.start()

    finish(fetches[:2])
    pick_messages(
        node_ref, lambda k, r: disp_ref[k : k + 1, r * 128 : (r + 1) * 128], messages
    )
    pl.semaphore_wait(barrier, 24)

    copies = first_stage(messages, held, send1, recv1, outer, inner)
    finish(fetches[2:])
    exponent_rows(source_ref, target_ref, left, right)
    kernel_values(0, left, right, upper, lower)
    kernel_values(1, left, right, upper, lower)
    finish(copies)
    copies = second_stage(held, ready, landed, send2, recv2, outer, inner)
    kernel_values(2, left, right, upper, lower)
    kernel_values(3, left, right, upper, lower)
    finish(copies)
    halos = [
        remote(
            mesh_hbm.at[0, pl.ds(14, 2)], field.at[pl.ds(0, 2)], send5.at[0], recv5.at[0], after
        ),
        remote(
            mesh_hbm.at[0, pl.ds(0, 2)], field.at[pl.ds(18, 2)], send5.at[1], recv5.at[1], before
        ),
    ]

    gather_members(landed, slot_ref, member)
    for c in range(4):
        loads[c].wait()
        contribute(c, member, inverse, upper, lower, weight_ref, result)
    pick_messages(
        pick_ref,
        lambda k, r: result[r // 8, k : k + 1, (r % 8) * 128 : (r % 8 + 1) * 128],
        messages2,
    )
    loads[4].wait()
    copies = first_stage(messages2, held2, send3, recv3, outer, inner)
    finish(halos)
    field[1, 0:1, :] = jnp.zeros((1, 512), f32)
    field[18, 0:1, :] = jnp.zeros((1, 512), f32)
    for x in range(16):
        field[x + 2, 0:1, :] = jnp.zeros((1, 512), f32)
    close_ends(field, has_left, has_right)
    sweep_once(field, once, has_left, has_right)
    finish(copies)
    copies = second_stage(held2, ready2, landed2, send4, recv4, outer, inner)
    sweep_again(field, once)
    whole = pltpu.make_async_copy(field.at[pl.ds(2, 16)], part_hbm, stored.at[0])
    whole.start()
    finish(copies)
    two = pl.ds(1, 2)
    halos = [
        remote(mesh_hbm.at[two, pl.ds(14, 2)], left_hbm, send5.at[2], recv5.at[2], after),
        remote(mesh_hbm.at[two, pl.ds(0, 2)], right_hbm, send5.at[3], recv5.at[3], before),
    ]

    scatter(landed2, vertex_ref, values, places, total, inter_ref)
    ends[...] = jnp.zeros_like(ends)
    for k in range(3):
        ends[0, k : k + 1, :] = inter_ref[k, 0:1, :]
        ends[1, k : k + 1, :] = inter_ref[k, 15:16, :]
    edges = [
        remote(ends.at[1], near.at[0], send5.at[4], recv5.at[4], after),
        remote(ends.at[0], near.at[1], send5.at[5], recv5.at[5], before),
    ]
    wall = pltpu.make_async_copy(inter_ref, inter_hbm, stored.at[1])
    wall.start()
    whole.wait()
    finish(edges)
    edge = pltpu.make_async_copy(near, edge_hbm, stored.at[2])
    edge.start()
    add_wall(
        inter_ref[0],
        jnp.where(has_left, near[0, 0:1, :], 0.0),
        jnp.where(has_right, near[1, 0:1, :], 0.0),
        field,
    )
    rows = pltpu.make_async_copy(
        field.at[pl.ds(2, 16), pl.ds(0, 8)], part_hbm.at[:, pl.ds(0, 8)], stored.at[3]
    )
    rows.start()
    wall.wait()
    edge.wait()
    rows.wait()
    finish(halos)


def smooth_kernel(
    place_ref, inter_ref, edge_ref, part_hbm, mesh_hbm, left_hbm, right_hbm, out_hbm,
    field, once, arrived, leaving,
):
    place = place_ref[0]
    has_left, has_right = place > 0, place < 127

    def fetch(k):
        return (
            pltpu.make_async_copy(left_hbm.at[k - 1], field.at[k - 1, pl.ds(0, 2)], arrived.at[k, 0]),
            pltpu.make_async_copy(mesh_hbm.at[k], field.at[k - 1, pl.ds(2, 16)], arrived.at[k, 1]),
            pltpu.make_async_copy(
                right_hbm.at[k - 1], field.at[k - 1, pl.ds(18, 2)], arrived.at[k, 2]
            ),
        )

    def store(k):
        return pltpu.make_async_copy(field.at[k - 1, pl.ds(2, 16)], out_hbm.at[k], leaving.at[k])

    for k in (1, 2):
        for copy in fetch(k):
            copy.start()
    done = pltpu.make_async_copy(part_hbm, out_hbm.at[0], leaving.at[0])
    done.start()
    for k in (1, 2):
        finish(fetch(k))
        part = field.at[k - 1]
        for x in range(16):
            part[x + 2, 0:1, :] = inter_ref[k, x : x + 1, :]
        part[1, 0:1, :] = edge_ref[0, k : k + 1, :]
        part[18, 0:1, :] = edge_ref[1, k : k + 1, :]
        close_ends(part, has_left, has_right)
        sweep_once(part, once, has_left, has_right)
        sweep_again(part, once)
        store(k).start()
    done.wait()
    for k in (1, 2):
        store(k).wait()


def transfer(
    displacement, send_node, member_slot, inverse_part, source_coord, target_coord,
    unity_weight, result_pick, receive_vertex, mesh_before,
):
    hbm = pl.BlockSpec(memory_space=pl.ANY)
    dma = pltpu.SemaphoreType.DMA
    halo = jax.ShapeDtypeStruct((2, 2, 96, 512), f32)
    exchange = [
        pltpu.VMEM((192, 128), f32),
        pltpu.VMEM((192, 128), f32),
        pltpu.VMEM((16, 12, 128), f32),
        pltpu.VMEM((16, 12, 128), f32),
    ]
    small = [
        displacement,
        send_node.reshape(64, 128),
        member_slot,
        source_coord.transpose(1, 0, 2),
        target_coord.transpose(1, 0, 2),
        unity_weight,
        result_pick.reshape(64, 128),
        receive_vertex.reshape(64, 128),
    ]
    return pl.pallas_call(
        transfer_kernel,
        out_shape=(
            jax.ShapeDtypeStruct((3, 16, 512), f32),
            jax.ShapeDtypeStruct((2, 8, 512), f32),
            halo,
            halo,
            jax.ShapeDtypeStruct((16, 96, 512), f32),
        ),
        in_specs=[hbm] * 10,
        out_specs=(hbm,) * 5,
        scratch_shapes=[pltpu.VMEM(a.shape, a.dtype) for a in small]
        + exchange
        + exchange
        + [
            pltpu.VMEM((4, 1024, 1024), bf16),
            pltpu.VMEM((8, 32, 128), f32),
            pltpu.VMEM((8, 128, 128), f32),
            pltpu.VMEM((8, 128, 128), f32),
            pltpu.VMEM((4, 1024, 1024), bf16),
            pltpu.VMEM((4, 1024, 1024), bf16),
            pltpu.VMEM((4, 8, 1024), f32),
            pltpu.VMEM((4, 384, 512), bf16),
            pltpu.VMEM((4, 128, 512), bf16),
            pltpu.VMEM((384, 128), f32),
            pltpu.VMEM((3, 16, 512), f32),
            pltpu.VMEM((2, 8, 512), f32),
            pltpu.VMEM((2, 8, 512), f32),
            pltpu.VMEM((20, 96, 512), f32),
            pltpu.VMEM((18, 96, 512), f32),
            dma((8,)),
            dma((5,)),
            dma((7,)),
            dma((7,)),
            dma((15,)),
            dma((15,)),
            dma((7,)),
            dma((7,)),
            dma((15,)),
            dma((15,)),
            dma((6,)),
            dma((6,)),
            dma((4,)),
        ],
        compiler_params=pltpu.CompilerParams(
            collective_id=1, has_side_effects=True, vmem_limit_bytes=63 << 20
        ),
    )(*small, inverse_part, mesh_before)


def smooth(place, interface, edges, part, mesh_before, left, right):
    hbm = pl.BlockSpec(memory_space=pl.ANY)
    return pl.pallas_call(
        smooth_kernel,
        out_shape=jax.ShapeDtypeStruct((3, 16, 96, 512), f32),
        in_specs=[pl.BlockSpec(memory_space=pltpu.SMEM), vmem(), vmem(), hbm, hbm, hbm, hbm],
        out_specs=hbm,
        scratch_shapes=[
            pltpu.VMEM((2, 20, 96, 512), f32),
            pltpu.VMEM((18, 96, 512), f32),
            pltpu.SemaphoreType.DMA((3, 3)),
            pltpu.SemaphoreType.DMA((3,)),
        ],
        compiler_params=pltpu.CompilerParams(vmem_limit_bytes=63 << 20),
    )(place, interface, edges, part, mesh_before, left, right)


def local(
    displacement,
    send_node,
    member_slot,
    inverse_part,
    source_coord,
    target_coord,
    unity_weight,
    result_pick,
    receive_vertex,
    mesh_before,
):
    place = lax.axis_index("dev").astype(jnp.int32).reshape(1)
    interface, edges, left, right, part = transfer(
        displacement, send_node, member_slot, inverse_part, source_coord, target_coord,
        unity_weight, result_pick, receive_vertex, mesh_before,
    )
    return smooth(place, interface, edges, part, mesh_before, left, right)


def solution(mesh):
    in_specs = (
        P(None, "dev"),
        P("dev"),
        P("dev", None),
        P("dev", None, None),
        P("dev", None, None),
        P("dev", None, None),
        P("dev", None),
        P("dev"),
        P("dev"),
        P(None, "dev", None, None),
    )
    out_specs = P(None, "dev", None, None)
    return jax.shard_map(local, mesh=mesh, in_specs=in_specs, out_specs=out_specs, check_vma=False)
```

```python
import jax
import jax.numpy as jnp
from jax import lax
from jax.experimental import pallas as pl
from jax.experimental.pallas import tpu as pltpu
from jax.sharding import PartitionSpec as P

relax_rate = 0.8
kernel_sharpness = 8.0
log2_e = 1.4426950408889634
spread_rate = relax_rate / 6.0
keep_rate = 1.0 - relax_rate

MESH = pl.DeviceIdType.MESH
f32 = jnp.float32
bf16 = jnp.bfloat16


def vmem():
    return pl.BlockSpec(memory_space=pltpu.VMEM)


def lookup(row, lanes):
    spread = jnp.broadcast_to(row, lanes.shape)
    return jnp.take_along_axis(spread, lanes, axis=1, mode="promise_in_bounds")


def message_index(index_ref, step):
    x, core = step // 2, step % 2
    even = index_ref[pl.ds(x, 8, stride=8), :]
    odd = index_ref[pl.ds(4 + x, 8, stride=8), :]
    lane = lax.broadcasted_iota(jnp.int32, (8, 128), 1)
    if core == 0:
        return jnp.where(lane < 64, even, pltpu.roll(odd, 64, 1))
    return jnp.where(lane < 64, pltpu.roll(even, 64, 1), odd)


def pick_messages(index_ref, row_of, out_ref):
    for half in range(2):
        index = [message_index(index_ref, 4 * half + g) for g in range(4)]
        high = [jnp.right_shift(i, 7) for i in index]
        low = [jnp.bitwise_and(i, 127) for i in index]
        total = [[jnp.zeros((8, 128), f32) for _ in range(3)] for _ in range(4)]
        for r in range(32):
            hit = [h == r for h in high]
            for k in range(3):
                row = row_of(k, r)
                for g in range(4):
                    total[g][k] = jnp.where(hit[g], lookup(row, low[g]), total[g][k])
        for g in range(4):
            for k in range(3):
                top = ((4 * half + g) * 3 + k) * 8
                out_ref[top : top + 8, :] = total[g][k]


def three_parts(value):
    high = value.astype(bf16).astype(f32)
    rest = value - high
    middle = rest.astype(bf16).astype(f32)
    return high, middle, rest - middle


def cluster_rows(ref, c, rows):
    return jnp.concatenate([ref[q, pl.ds(c, rows, stride=4), :] for q in range(8)], axis=1)


def remote(source, target, send, receive, device):
    copy = pltpu.make_async_remote_copy(
        src_ref=source,
        dst_ref=target,
        send_sem=send,
        recv_sem=receive,
        device_id=(device,),
        device_id_type=MESH,
    )
    copy.start()
    return copy


def first_stage(messages, held, send, receive, outer, inner):
    copies = []
    for i in range(1, 8):
        p = (inner + i) % 8
        copies.append(
            remote(
                messages.at[pl.ds(pl.multiple_of(p * 24, 8), 24)],
                held.at[pl.ds(pl.multiple_of(inner * 24, 8), 24)],
                send.at[i - 1],
                receive.at[i - 1],
                outer * 8 + p,
            )
        )
    mine = pl.ds(pl.multiple_of(inner * 24, 8), 24)
    held[mine, :] = messages[mine, :]
    return copies


def second_stage(held, ready, landed, send, receive, outer, inner):
    lane = lax.broadcasted_iota(jnp.int32, (4, 128), 1)
    for m in range(8):
        for k in range(3):
            first = held[pl.ds(k * 8 + m, 4, stride=48), :]
            second = held[pl.ds(24 + k * 8 + m, 4, stride=48), :]
            ready[2 * m, 4 * k : 4 * k + 4, :] = jnp.where(
                lane < 64, first, pltpu.roll(second, 64, 1)
            )
            ready[2 * m + 1, 4 * k : 4 * k + 4, :] = jnp.where(
                lane < 64, pltpu.roll(first, 64, 1), second
            )
    copies = []
    for i in range(1, 16):
        p = (outer + i) % 16
        copies.append(
            remote(
                ready.at[p],
                landed.at[outer],
                send.at[i - 1],
                receive.at[i - 1],
                p * 8 + inner,
            )
        )
    landed[outer] = ready[outer]
    return copies


def finish(copies):
    for copy in copies:
        copy.wait()


def exponent_rows(source_ref, target_ref, left, right):
    left[...] = jnp.zeros_like(left)
    right[...] = jnp.zeros_like(right)
    ones = jnp.ones((4, 1024), f32)
    source_norm = jnp.zeros((4, 1024), f32)
    target_norm = jnp.zeros((4, 1024), f32)
    pairs = []
    for d in range(3):
        s = source_ref[d]
        t = target_ref[d]
        source_norm += s * s
        target_norm += t * t
        sh, sm, sl = three_parts(s)
        th, tm, tl = three_parts(t * (2.0 * kernel_sharpness * log2_e))
        pairs += [(sh, th), (sh, tm), (sm, th), (sh, tl), (sl, th), (sm, tm)]
    pairs += [(p, ones) for p in three_parts(source_norm * (-kernel_sharpness * log2_e))]
    pairs += [(ones, p) for p in three_parts(target_norm * (-kernel_sharpness * log2_e))]
    for row, (a, b) in enumerate(pairs):
        for q in range(8):
            left[q, 4 * row : 4 * row + 4, :] = a[:, 128 * q : 128 * (q + 1)]
            right[q, 4 * row : 4 * row + 4, :] = b[:, 128 * q : 128 * (q + 1)]


def kernel_values(c, left, right, upper, lower):
    source_rows = cluster_rows(left, c, 32).T.astype(bf16)
    target_rows = cluster_rows(right, c, 32).astype(bf16)
    for p in range(4):
        rows = slice(256 * p, 256 * (p + 1))
        kernel = jnp.exp2(jnp.dot(source_rows[rows], target_rows, preferred_element_type=f32))
        high = kernel.astype(bf16)
        upper[c, rows, :] = high
        lower[c, rows, :] = (kernel - high.astype(f32)).astype(bf16)


def gather_members(table, slot_ref, member):
    member[...] = jnp.zeros_like(member)
    index = [
        jnp.concatenate(
            [slot_ref[:, 256 * m : 256 * m + 128], slot_ref[:, 256 * m + 128 : 256 * m + 256]],
            axis=0,
        )
        for m in range(4)
    ]
    high = [jnp.right_shift(i, 7) for i in index]
    low = [jnp.bitwise_and(i, 127) for i in index]

    def gather(part, total):
        total = list(total)
        for r in range(16):
            zy, j = part * 4 + r // 4, r % 4
            hit = [h == part * 16 + r for h in high]
            for k in range(3):
                line = table[zy, 4 * k + j : 4 * k + j + 1, :]
                for m in range(4):
                    total[3 * m + k] = jnp.where(hit[m], lookup(line, low[m]), total[3 * m + k])
        return tuple(total)

    total = lax.fori_loop(
        0, 4, gather, tuple(jnp.zeros((8, 128), f32) for _ in range(12))
    )
    for m in range(4):
        for k in range(3):
            value = total[3 * m + k]
            member[2 * m, 4 * k : 4 * k + 4, :] = value[0:4]
            member[2 * m + 1, 4 * k : 4 * k + 4, :] = value[4:8]


def contribute(c, member, inverse, upper, lower, weight_ref, result):
    members = cluster_rows(member, c, 8)
    padded = jnp.concatenate([members, jnp.zeros((8, 1024), f32)], axis=0)
    coupling = lax.dot_general(
        padded.astype(bf16), inverse[c], (((1,), (1,)), ((), ())), preferred_element_type=f32
    )
    coefficient = members + coupling[0:8]
    high = coefficient.astype(bf16).astype(f32)
    both = jnp.concatenate([high, coefficient - high], axis=0).astype(bf16)
    summed = jnp.dot(both, upper[c], preferred_element_type=f32)
    summed += jnp.dot(both, lower[c], preferred_element_type=f32)
    result[c] = (summed[0:8] + summed[8:16]) * weight_ref[c : c + 1, :]


def scatter(table, vertex_ref, values, places, total, out_ref):
    def chunk(group, carry):
        product = jnp.zeros((384, 128), f32)
        for part in range(4):
            zy = group * 4 + part
            for j in range(4):
                vertex = vertex_ref[pl.ds(zy * 4 + j, 1), :]
                high = jnp.broadcast_to(jnp.right_shift(vertex, 7), (64, 128))
                low = jnp.broadcast_to(jnp.bitwise_and(vertex, 127), (128, 128))
                at_high = high == lax.broadcasted_iota(jnp.int32, (64, 128), 0)
                at_low = low == lax.broadcasted_iota(jnp.int32, (128, 128), 0)
                lanes = slice(128 * j, 128 * j + 128)
                places[part, :, lanes] = jnp.where(at_low, 1.0, 0.0).astype(bf16)
                for k in range(3):
                    value = table[zy, 4 * k + j : 4 * k + j + 1, :]
                    upper = value.astype(bf16).astype(f32)
                    for s, half in enumerate((upper, value - upper)):
                        spread = jnp.broadcast_to(half, (64, 128))
                        top = (2 * k + s) * 64
                        values[part, top : top + 64, lanes] = jnp.where(
                            at_high, spread, 0.0
                        ).astype(bf16)
            product += lax.dot_general(
                values[part],
                places[part],
                (((1,), (1,)), ((), ())),
                preferred_element_type=f32,
            )
        total[...] += product
        return carry

    total[...] = jnp.zeros_like(total)
    lax.fori_loop(0, 4, chunk, 0)
    for k in range(3):
        top = 2 * k * 64
        for q in range(4):
            out_ref[k, :, 128 * q : 128 * (q + 1)] = (
                total[pl.ds(top + q, 16, stride=4), :]
                + total[pl.ds(top + 64 + q, 16, stride=4), :]
            )


def swept(ref, out_ref, source, target, inside=None):
    rows = 16
    lane = lax.broadcasted_iota(jnp.int32, (rows, 512), 1)
    line = lax.broadcasted_iota(jnp.int32, (rows, 512), 0)
    for y in range(0, 96, rows):
        center = ref[source, y : y + rows, :]
        if y == 0:
            above = pltpu.roll(center, 1, 0)
        else:
            above = ref[source, y - 1 : y - 1 + rows, :]
        if y + rows == 96:
            below = jnp.where(line == rows - 1, 0.0, pltpu.roll(center, rows - 1, 0))
        else:
            below = ref[source, y + 1 : y + 1 + rows, :]
        beside = ref[source - 1, y : y + rows, :] + ref[source + 1, y : y + rows, :]
        beside = beside + (above + below)
        beside = beside + jnp.where(lane == 0, 0.0, pltpu.roll(center, 1, 1))
        beside = beside + jnp.where(lane == 511, 0.0, pltpu.roll(center, 511, 1))
        moved = center * keep_rate + beside * spread_rate
        if y == 0:
            moved = jnp.where(line == 0, center, moved)
        if inside is not None:
            moved = jnp.where(inside, moved, 0.0)
        out_ref[target, y : y + rows, :] = moved


def sweep_once(field, once, has_left, has_right):
    def plane(x, carry):
        swept(field, once, x + 1, x)
        return carry

    swept(field, once, 1, 0, has_left)
    lax.fori_loop(1, 17, plane, 0)
    swept(field, once, 18, 17, has_right)


def sweep_again(field, once):
    def plane(x, carry):
        swept(once, field, x + 1, x + 2)
        return carry

    lax.fori_loop(0, 16, plane, 0)


def close_ends(field, has_left, has_right):
    @pl.when(jnp.logical_not(has_left))
    def _():
        field[1] = jnp.zeros((96, 512), f32)

    @pl.when(jnp.logical_not(has_right))
    def _():
        field[18] = jnp.zeros((96, 512), f32)


def add_wall(inter, before, after, field):
    lane = lax.broadcasted_iota(jnp.int32, (16, 512), 1)
    line = lax.broadcasted_iota(jnp.int32, (16, 512), 0)
    beside = jnp.where(line == 0, before, pltpu.roll(inter, 1, 0))
    beside = beside + jnp.where(line == 15, after, pltpu.roll(inter, 15, 0))
    beside = beside + jnp.where(lane == 0, 0.0, pltpu.roll(inter, 1, 1))
    beside = beside + jnp.where(lane == 511, 0.0, pltpu.roll(inter, 511, 1))
    first = spread_rate * ((1.0 + keep_rate) * inter + spread_rate * beside)
    second = (spread_rate * spread_rate) * inter
    row = lax.broadcasted_iota(jnp.int32, (8, 512), 0)
    for x in range(16):
        extra = jnp.where(
            row == 0,
            inter[x : x + 1],
            jnp.where(row == 1, first[x : x + 1], jnp.where(row == 2, second[x : x + 1], 0.0)),
        )
        field[x + 2, 0:8, :] += extra


def transfer_kernel(
    disp_hbm, node_hbm, slot_hbm, source_hbm, target_hbm, weight_hbm, pick_hbm, vertex_hbm,
    inv_hbm, mesh_hbm,
    inter_hbm, edge_hbm, left_hbm, right_hbm, part_hbm,
    disp_ref, node_ref, slot_ref, source_ref, target_ref, weight_ref, pick_ref, vertex_ref,
    messages, held, ready, landed, messages2, held2, ready2, landed2,
    inverse, member, left, right, upper, lower, result, values, places, total,
    inter_ref, ends, near, field, once,
    fetched, loaded, send1, recv1, send2, recv2, send3, recv3, send4, recv4, send5, recv5, stored,
):
    me = lax.axis_index("dev")
    outer, inner = me // 8, me % 8
    before, after = (me + 127) % 128, (me + 1) % 128
    has_left, has_right = me > 0, me < 127

    small = [
        (disp_hbm, disp_ref), (node_hbm, node_ref), (slot_hbm, slot_ref),
        (source_hbm, source_ref), (target_hbm, target_ref), (weight_hbm, weight_ref),
        (pick_hbm, pick_ref), (vertex_hbm, vertex_ref),
    ]
    fetches = [pltpu.make_async_copy(a, b, fetched.at[i]) for i, (a, b) in enumerate(small)]
    for fetch in fetches:
        fetch.start()
    barrier = pltpu.get_barrier_semaphore()
    peers = [outer * 8 + (inner + i) % 8 for i in range(1, 8)]
    peers += [((outer + i) % 16) * 8 + inner for i in range(1, 16)]
    peers += [before, after]
    for peer in peers:
        pl.semaphore_signal(barrier, inc=1, device_id=(peer,), device_id_type=MESH)
    loads = [pltpu.make_async_copy(inv_hbm.at[c], inverse.at[c], loaded.at[c]) for c in range(4)]
    loads.append(pltpu.make_async_copy(mesh_hbm.at[0], field.at[pl.ds(2, 16)], loaded.at[4]))
    for load in loads:
        load.start()

    finish(fetches[:2])
    pick_messages(
        node_ref, lambda k, r: disp_ref[k : k + 1, r * 128 : (r + 1) * 128], messages
    )
    pl.semaphore_wait(barrier, 24)

    copies = first_stage(messages, held, send1, recv1, outer, inner)
    finish(fetches[2:])
    exponent_rows(source_ref, target_ref, left, right)
    kernel_values(0, left, right, upper, lower)
    kernel_values(1, left, right, upper, lower)
    finish(copies)
    copies = second_stage(held, ready, landed, send2, recv2, outer, inner)
    kernel_values(2, left, right, upper, lower)
    kernel_values(3, left, right, upper, lower)
    finish(copies)
    halos = [
        remote(
            mesh_hbm.at[0, pl.ds(14, 2)], field.at[pl.ds(0, 2)], send5.at[0], recv5.at[0], after
        ),
        remote(
            mesh_hbm.at[0, pl.ds(0, 2)], field.at[pl.ds(18, 2)], send5.at[1], recv5.at[1], before
        ),
    ]

    late = [
        remote(mesh_hbm.at[1, pl.ds(14, 2)], left_hbm.at[0], send5.at[2], recv5.at[2], after),
        remote(mesh_hbm.at[1, pl.ds(0, 2)], right_hbm.at[0], send5.at[3], recv5.at[3], before),
    ]

    gather_members(landed, slot_ref, member)
    for c in range(4):
        loads[c].wait()
        contribute(c, member, inverse, upper, lower, weight_ref, result)
    pick_messages(
        pick_ref,
        lambda k, r: result[r // 8, k : k + 1, (r % 8) * 128 : (r % 8 + 1) * 128],
        messages2,
    )
    loads[4].wait()
    copies = first_stage(messages2, held2, send3, recv3, outer, inner)
    finish(halos)
    field[1, 0:1, :] = jnp.zeros((1, 512), f32)
    field[18, 0:1, :] = jnp.zeros((1, 512), f32)
    for x in range(16):
        field[x + 2, 0:1, :] = jnp.zeros((1, 512), f32)
    close_ends(field, has_left, has_right)
    sweep_once(field, once, has_left, has_right)
    finish(copies)
    copies = second_stage(held2, ready2, landed2, send4, recv4, outer, inner)
    sweep_again(field, once)
    whole = pltpu.make_async_copy(field.at[pl.ds(2, 16)], part_hbm, stored.at[0])
    whole.start()
    finish(copies)
    halos = late + [
        remote(mesh_hbm.at[2, pl.ds(14, 2)], left_hbm.at[1], send5.at[6], recv5.at[6], after),
        remote(mesh_hbm.at[2, pl.ds(0, 2)], right_hbm.at[1], send5.at[7], recv5.at[7], before),
    ]

    scatter(landed2, vertex_ref, values, places, total, inter_ref)
    ends[...] = jnp.zeros_like(ends)
    for k in range(3):
        ends[0, k : k + 1, :] = inter_ref[k, 0:1, :]
        ends[1, k : k + 1, :] = inter_ref[k, 15:16, :]
    edges = [
        remote(ends.at[1], near.at[0], send5.at[4], recv5.at[4], after),
        remote(ends.at[0], near.at[1], send5.at[5], recv5.at[5], before),
    ]
    wall = pltpu.make_async_copy(inter_ref, inter_hbm, stored.at[1])
    wall.start()
    whole.wait()
    finish(edges)
    edge = pltpu.make_async_copy(near, edge_hbm, stored.at[2])
    edge.start()
    add_wall(
        inter_ref[0],
        jnp.where(has_left, near[0, 0:1, :], 0.0),
        jnp.where(has_right, near[1, 0:1, :], 0.0),
        field,
    )
    rows = pltpu.make_async_copy(
        field.at[pl.ds(2, 16), pl.ds(0, 8)], part_hbm.at[:, pl.ds(0, 8)], stored.at[3]
    )
    rows.start()
    wall.wait()
    edge.wait()
    rows.wait()
    finish(halos)


def smooth_kernel(
    place_ref, inter_ref, edge_ref, part_hbm, mesh_hbm, left_hbm, right_hbm, out_hbm,
    field, once, swept_part, arrived, leaving,
):
    place = place_ref[0]
    has_left, has_right = place > 0, place < 127

    def fetch(k):
        return (
            pltpu.make_async_copy(left_hbm.at[k - 1], field.at[k - 1, pl.ds(0, 2)], arrived.at[k, 0]),
            pltpu.make_async_copy(mesh_hbm.at[k], field.at[k - 1, pl.ds(2, 16)], arrived.at[k, 1]),
            pltpu.make_async_copy(
                right_hbm.at[k - 1], field.at[k - 1, pl.ds(18, 2)], arrived.at[k, 2]
            ),
        )

    def store(k):
        return pltpu.make_async_copy(field.at[k - 1, pl.ds(2, 16)], out_hbm.at[k], leaving.at[k])

    for k in (1, 2):
        for copy in fetch(k):
            copy.start()
    early = pltpu.make_async_copy(part_hbm, swept_part, arrived.at[0, 0])
    early.start()
    done = pltpu.make_async_copy(swept_part, out_hbm.at[0], leaving.at[0])
    for k in (1, 2):
        finish(fetch(k))
        part = field.at[k - 1]
        for x in range(16):
            part[x + 2, 0:1, :] = inter_ref[k, x : x + 1, :]
        part[1, 0:1, :] = edge_ref[0, k : k + 1, :]
        part[18, 0:1, :] = edge_ref[1, k : k + 1, :]
        close_ends(part, has_left, has_right)
        sweep_once(part, once, has_left, has_right)
        if k == 1:
            early.wait()
            done.start()
        sweep_again(part, once)
        store(k).start()
    done.wait()
    for k in (1, 2):
        store(k).wait()


def transfer(
    displacement, send_node, member_slot, inverse_part, source_coord, target_coord,
    unity_weight, result_pick, receive_vertex, mesh_before,
):
    hbm = pl.BlockSpec(memory_space=pl.ANY)
    dma = pltpu.SemaphoreType.DMA
    halo = jax.ShapeDtypeStruct((2, 2, 96, 512), f32)
    exchange = [
        pltpu.VMEM((192, 128), f32),
        pltpu.VMEM((192, 128), f32),
        pltpu.VMEM((16, 12, 128), f32),
        pltpu.VMEM((16, 12, 128), f32),
    ]
    small = [
        displacement,
        send_node.reshape(64, 128),
        member_slot,
        source_coord.transpose(1, 0, 2),
        target_coord.transpose(1, 0, 2),
        unity_weight,
        result_pick.reshape(64, 128),
        receive_vertex.reshape(64, 128),
    ]
    return pl.pallas_call(
        transfer_kernel,
        out_shape=(
            jax.ShapeDtypeStruct((3, 16, 512), f32),
            jax.ShapeDtypeStruct((2, 8, 512), f32),
            halo,
            halo,
            jax.ShapeDtypeStruct((16, 96, 512), f32),
        ),
        in_specs=[hbm] * 10,
        out_specs=(hbm,) * 5,
        scratch_shapes=[pltpu.VMEM(a.shape, a.dtype) for a in small]
        + exchange
        + exchange
        + [
            pltpu.VMEM((4, 1024, 1024), bf16),
            pltpu.VMEM((8, 32, 128), f32),
            pltpu.VMEM((8, 128, 128), f32),
            pltpu.VMEM((8, 128, 128), f32),
            pltpu.VMEM((4, 1024, 1024), bf16),
            pltpu.VMEM((4, 1024, 1024), bf16),
            pltpu.VMEM((4, 8, 1024), f32),
            pltpu.VMEM((4, 384, 512), bf16),
            pltpu.VMEM((4, 128, 512), bf16),
            pltpu.VMEM((384, 128), f32),
            pltpu.VMEM((3, 16, 512), f32),
            pltpu.VMEM((2, 8, 512), f32),
            pltpu.VMEM((2, 8, 512), f32),
            pltpu.VMEM((20, 96, 512), f32),
            pltpu.VMEM((18, 96, 512), f32),
            dma((8,)),
            dma((5,)),
            dma((7,)),
            dma((7,)),
            dma((15,)),
            dma((15,)),
            dma((7,)),
            dma((7,)),
            dma((15,)),
            dma((15,)),
            dma((8,)),
            dma((8,)),
            dma((4,)),
        ],
        compiler_params=pltpu.CompilerParams(
            collective_id=1, has_side_effects=True, vmem_limit_bytes=63 << 20
        ),
    )(*small, inverse_part, mesh_before)


def smooth(place, interface, edges, part, mesh_before, left, right):
    hbm = pl.BlockSpec(memory_space=pl.ANY)
    return pl.pallas_call(
        smooth_kernel,
        out_shape=jax.ShapeDtypeStruct((3, 16, 96, 512), f32),
        in_specs=[pl.BlockSpec(memory_space=pltpu.SMEM), vmem(), vmem(), hbm, hbm, hbm, hbm],
        out_specs=hbm,
        scratch_shapes=[
            pltpu.VMEM((2, 20, 96, 512), f32),
            pltpu.VMEM((18, 96, 512), f32),
            pltpu.VMEM((16, 96, 512), f32),
            pltpu.SemaphoreType.DMA((3, 3)),
            pltpu.SemaphoreType.DMA((3,)),
        ],
        compiler_params=pltpu.CompilerParams(vmem_limit_bytes=63 << 20),
    )(place, interface, edges, part, mesh_before, left, right)


def local(
    displacement,
    send_node,
    member_slot,
    inverse_part,
    source_coord,
    target_coord,
    unity_weight,
    result_pick,
    receive_vertex,
    mesh_before,
):
    place = lax.axis_index("dev").astype(jnp.int32).reshape(1)
    interface, edges, left, right, part = transfer(
        displacement, send_node, member_slot, inverse_part, source_coord, target_coord,
        unity_weight, result_pick, receive_vertex, mesh_before,
    )
    return smooth(place, interface, edges, part, mesh_before, left, right)


def solution(mesh):
    in_specs = (
        P(None, "dev"),
        P("dev"),
        P("dev", None),
        P("dev", None, None),
        P("dev", None, None),
        P("dev", None, None),
        P("dev", None),
        P("dev"),
        P("dev"),
        P(None, "dev", None, None),
    )
    out_specs = P(None, "dev", None, None)
    return jax.shard_map(local, mesh=mesh, in_specs=in_specs, out_specs=out_specs, check_vma=False)
```

```python
import jax
import jax.numpy as jnp
from jax import lax
from jax.experimental import pallas as pl
from jax.experimental.pallas import tpu as pltpu
from jax.sharding import PartitionSpec as P

relax_rate = 0.8
kernel_sharpness = 8.0
log2_e = 1.4426950408889634
spread_rate = relax_rate / 6.0
keep_rate = 1.0 - relax_rate

MESH = pl.DeviceIdType.MESH
f32 = jnp.float32
bf16 = jnp.bfloat16


def vmem():
    return pl.BlockSpec(memory_space=pltpu.VMEM)


def lookup(row, lanes):
    spread = jnp.broadcast_to(row, lanes.shape)
    return jnp.take_along_axis(spread, lanes, axis=1, mode="promise_in_bounds")


def message_index(index_ref, step):
    x, core = step // 2, step % 2
    even = index_ref[pl.ds(x, 8, stride=8), :]
    odd = index_ref[pl.ds(4 + x, 8, stride=8), :]
    lane = lax.broadcasted_iota(jnp.int32, (8, 128), 1)
    if core == 0:
        return jnp.where(lane < 64, even, pltpu.roll(odd, 64, 1))
    return jnp.where(lane < 64, pltpu.roll(even, 64, 1), odd)


def pick_messages(index_ref, row_of, out_ref):
    for half in range(2):
        index = [message_index(index_ref, 4 * half + g) for g in range(4)]
        high = [jnp.right_shift(i, 7) for i in index]
        low = [jnp.bitwise_and(i, 127) for i in index]
        total = [[jnp.zeros((8, 128), f32) for _ in range(3)] for _ in range(4)]
        for r in range(32):
            hit = [h == r for h in high]
            for k in range(3):
                row = row_of(k, r)
                for g in range(4):
                    total[g][k] = jnp.where(hit[g], lookup(row, low[g]), total[g][k])
        for g in range(4):
            for k in range(3):
                top = ((4 * half + g) * 3 + k) * 8
                out_ref[top : top + 8, :] = total[g][k]


def three_parts(value):
    high = value.astype(bf16).astype(f32)
    rest = value - high
    middle = rest.astype(bf16).astype(f32)
    return high, middle, rest - middle


def cluster_rows(ref, c, rows):
    return jnp.concatenate([ref[q, pl.ds(c, rows, stride=4), :] for q in range(8)], axis=1)


def remote(source, target, send, receive, device):
    copy = pltpu.make_async_remote_copy(
        src_ref=source,
        dst_ref=target,
        send_sem=send,
        recv_sem=receive,
        device_id=(device,),
        device_id_type=MESH,
    )
    copy.start()
    return copy


def first_stage(messages, held, send, receive, outer, inner):
    copies = []
    for i in range(1, 8):
        p = (inner + i) % 8
        copies.append(
            remote(
                messages.at[pl.ds(pl.multiple_of(p * 24, 8), 24)],
                held.at[pl.ds(pl.multiple_of(inner * 24, 8), 24)],
                send.at[i - 1],
                receive.at[i - 1],
                outer * 8 + p,
            )
        )
    mine = pl.ds(pl.multiple_of(inner * 24, 8), 24)
    held[mine, :] = messages[mine, :]
    return copies


def second_stage(held, ready, landed, send, receive, outer, inner):
    lane = lax.broadcasted_iota(jnp.int32, (4, 128), 1)
    for m in range(8):
        for k in range(3):
            first = held[pl.ds(k * 8 + m, 4, stride=48), :]
            second = held[pl.ds(24 + k * 8 + m, 4, stride=48), :]
            ready[2 * m, 4 * k : 4 * k + 4, :] = jnp.where(
                lane < 64, first, pltpu.roll(second, 64, 1)
            )
            ready[2 * m + 1, 4 * k : 4 * k + 4, :] = jnp.where(
                lane < 64, pltpu.roll(first, 64, 1), second
            )
    copies = []
    for i in range(1, 16):
        p = (outer + i) % 16
        copies.append(
            remote(
                ready.at[p],
                landed.at[outer],
                send.at[i - 1],
                receive.at[i - 1],
                p * 8 + inner,
            )
        )
    landed[outer] = ready[outer]
    return copies


def finish(copies):
    for copy in copies:
        copy.wait()


def exponent_rows(source_ref, target_ref, left, right):
    left[...] = jnp.zeros_like(left)
    right[...] = jnp.zeros_like(right)
    ones = jnp.ones((4, 1024), f32)
    source_norm = jnp.zeros((4, 1024), f32)
    target_norm = jnp.zeros((4, 1024), f32)
    pairs = []
    for d in range(3):
        s = source_ref[d]
        t = target_ref[d]
        source_norm += s * s
        target_norm += t * t
        sh, sm, sl = three_parts(s)
        th, tm, tl = three_parts(t * (2.0 * kernel_sharpness * log2_e))
        pairs += [(sh, th), (sh, tm), (sm, th), (sh, tl), (sl, th), (sm, tm)]
    pairs += [(p, ones) for p in three_parts(source_norm * (-kernel_sharpness * log2_e))]
    pairs += [(ones, p) for p in three_parts(target_norm * (-kernel_sharpness * log2_e))]
    for row, (a, b) in enumerate(pairs):
        for q in range(8):
            left[q, 4 * row : 4 * row + 4, :] = a[:, 128 * q : 128 * (q + 1)]
            right[q, 4 * row : 4 * row + 4, :] = b[:, 128 * q : 128 * (q + 1)]


def kernel_values(c, left, right, upper, lower):
    source_rows = cluster_rows(left, c, 32).T.astype(bf16)
    target_rows = cluster_rows(right, c, 32).astype(bf16)
    for p in range(4):
        rows = slice(256 * p, 256 * (p + 1))
        kernel = jnp.exp2(jnp.dot(source_rows[rows], target_rows, preferred_element_type=f32))
        high = kernel.astype(bf16)
        upper[c, rows, :] = high
        lower[c, rows, :] = (kernel - high.astype(f32)).astype(bf16)


def gather_members(table, slot_ref, member):
    member[...] = jnp.zeros_like(member)
    index = [
        jnp.concatenate(
            [slot_ref[:, 256 * m : 256 * m + 128], slot_ref[:, 256 * m + 128 : 256 * m + 256]],
            axis=0,
        )
        for m in range(4)
    ]
    high = [jnp.right_shift(i, 7) for i in index]
    low = [jnp.bitwise_and(i, 127) for i in index]

    def gather(part, total):
        total = list(total)
        for r in range(16):
            zy, j = part * 4 + r // 4, r % 4
            hit = [h == part * 16 + r for h in high]
            for k in range(3):
                line = table[zy, 4 * k + j : 4 * k + j + 1, :]
                for m in range(4):
                    total[3 * m + k] = jnp.where(hit[m], lookup(line, low[m]), total[3 * m + k])
        return tuple(total)

    total = lax.fori_loop(
        0, 4, gather, tuple(jnp.zeros((8, 128), f32) for _ in range(12))
    )
    for m in range(4):
        for k in range(3):
            value = total[3 * m + k]
            member[2 * m, 4 * k : 4 * k + 4, :] = value[0:4]
            member[2 * m + 1, 4 * k : 4 * k + 4, :] = value[4:8]


def contribute(c, member, inverse, upper, lower, weight_ref, result):
    members = cluster_rows(member, c, 8)
    padded = jnp.concatenate([members, jnp.zeros((8, 1024), f32)], axis=0)
    coupling = lax.dot_general(
        padded.astype(bf16), inverse[c], (((1,), (1,)), ((), ())), preferred_element_type=f32
    )
    coefficient = members + coupling[0:8]
    high = coefficient.astype(bf16).astype(f32)
    both = jnp.concatenate([high, coefficient - high], axis=0).astype(bf16)
    summed = jnp.dot(both, upper[c], preferred_element_type=f32)
    summed += jnp.dot(both, lower[c], preferred_element_type=f32)
    result[c] = (summed[0:8] + summed[8:16]) * weight_ref[c : c + 1, :]


def scatter(table, vertex_ref, values, places, total, out_ref):
    def chunk(group, carry):
        product = jnp.zeros((384, 128), f32)
        for part in range(4):
            zy = group * 4 + part
            for j in range(4):
                vertex = vertex_ref[pl.ds(zy * 4 + j, 1), :]
                high = jnp.broadcast_to(jnp.right_shift(vertex, 7), (64, 128))
                low = jnp.broadcast_to(jnp.bitwise_and(vertex, 127), (128, 128))
                at_high = high == lax.broadcasted_iota(jnp.int32, (64, 128), 0)
                at_low = low == lax.broadcasted_iota(jnp.int32, (128, 128), 0)
                lanes = slice(128 * j, 128 * j + 128)
                places[part, :, lanes] = jnp.where(at_low, 1.0, 0.0).astype(bf16)
                for k in range(3):
                    value = table[zy, 4 * k + j : 4 * k + j + 1, :]
                    upper = value.astype(bf16).astype(f32)
                    for s, half in enumerate((upper, value - upper)):
                        spread = jnp.broadcast_to(half, (64, 128))
                        top = (2 * k + s) * 64
                        values[part, top : top + 64, lanes] = jnp.where(
                            at_high, spread, 0.0
                        ).astype(bf16)
            product += lax.dot_general(
                values[part],
                places[part],
                (((1,), (1,)), ((), ())),
                preferred_element_type=f32,
            )
        total[...] += product
        return carry

    total[...] = jnp.zeros_like(total)
    lax.fori_loop(0, 4, chunk, 0)
    for k in range(3):
        top = 2 * k * 64
        for q in range(4):
            out_ref[k, :, 128 * q : 128 * (q + 1)] = (
                total[pl.ds(top + q, 16, stride=4), :]
                + total[pl.ds(top + 64 + q, 16, stride=4), :]
            )


def neighbour_band(band):
    row = jnp.bitwise_and(lax.broadcasted_iota(jnp.int32, (512, 256), 0), 255)
    column = lax.broadcasted_iota(jnp.int32, (512, 256), 1)
    near = (row == column + 1) | (row == column - 1)
    band[...] = jnp.where(near, 1.0, 0.0).astype(bf16)


def clear_margins(field):
    count = field.shape[1]
    for q in range(4):
        for x in range(count):
            field[q, x, 0:8, :] = jnp.zeros((8, 128), f32)
            field[q, x, 104:112, :] = jnp.zeros((8, 128), f32)


def swept(source, target, band, count, start, place):
    lane = lax.broadcasted_iota(jnp.int32, (count, 96, 128), 2)
    line = lax.broadcasted_iota(jnp.int32, (count, 96, 128), 1)
    here = pl.ds(start, count)
    center = [source[q, here, 8:104, :] for q in range(4)]
    upper, lower = [], []
    for part in center:
        high = part.astype(bf16)
        upper.append(high.reshape(count * 96, 128))
        lower.append((part - high.astype(f32)).astype(bf16).reshape(count * 96, 128))
    along = []
    for q in (0, 2):
        parts = jnp.concatenate([upper[q], upper[q + 1], lower[q], lower[q + 1]], axis=1)
        along.append(jnp.dot(parts, band[...], preferred_element_type=f32))
    for q in range(4):
        beside = along[q // 2][:, 128 * (q % 2) : 128 * (q % 2) + 128].reshape(count, 96, 128)
        if q == 1:
            beside = beside + jnp.where(lane == 127, pltpu.roll(center[2], 127, 2), 0.0)
        if q == 2:
            beside = beside + jnp.where(lane == 0, pltpu.roll(center[1], 1, 2), 0.0)
        beside = beside + (source[q, here, 7:103, :] + source[q, here, 9:105, :])
        beside = beside + (
            source[q, pl.ds(start - 1, count), 8:104, :]
            + source[q, pl.ds(start + 1, count), 8:104, :]
        )
        moved = center[q] * keep_rate + beside * spread_rate
        target[q, pl.ds(place, count), 8:104, :] = jnp.where(line == 0, center[q], moved)


def close_end(field, x, inside):
    @pl.when(jnp.logical_not(inside))
    def _():
        for q in range(4):
            field[q, x, 8:104, :] = jnp.zeros((96, 128), f32)


def add_wall(inter, before, after, field):
    lane = lax.broadcasted_iota(jnp.int32, (16, 512), 1)
    line = lax.broadcasted_iota(jnp.int32, (16, 512), 0)
    beside = jnp.where(line == 0, before, pltpu.roll(inter, 1, 0))
    beside = beside + jnp.where(line == 15, after, pltpu.roll(inter, 15, 0))
    beside = beside + jnp.where(lane == 0, 0.0, pltpu.roll(inter, 1, 1))
    beside = beside + jnp.where(lane == 511, 0.0, pltpu.roll(inter, 511, 1))
    first = spread_rate * ((1.0 + keep_rate) * inter + spread_rate * beside)
    second = (spread_rate * spread_rate) * inter
    row = lax.broadcasted_iota(jnp.int32, (8, 512), 0)
    for x in range(16):
        extra = jnp.where(
            row == 0,
            inter[x : x + 1],
            jnp.where(row == 1, first[x : x + 1], jnp.where(row == 2, second[x : x + 1], 0.0)),
        )
        field[x, 0:8, :] += extra


def transfer_kernel(
    disp_hbm, node_hbm, slot_hbm, source_hbm, target_hbm, weight_hbm, pick_hbm, vertex_hbm,
    inv_hbm, mesh_hbm,
    inter_hbm, edge_hbm, left_hbm, right_hbm, part_hbm,
    disp_ref, node_ref, slot_ref, source_ref, target_ref, weight_ref, pick_ref, vertex_ref,
    messages, held, ready, landed, messages2, held2, ready2, landed2,
    inverse, member, left, right, upper, lower, result, values, places, total,
    inter_ref, ends, near, field, once, halo, band,
    fetched, loaded, send1, recv1, send2, recv2, send3, recv3, send4, recv4, send5, recv5, stored,
):
    me = lax.axis_index("dev")
    outer, inner = me // 8, me % 8
    before, after = (me + 127) % 128, (me + 1) % 128
    has_left, has_right = me > 0, me < 127

    small = [
        (disp_hbm, disp_ref), (node_hbm, node_ref), (slot_hbm, slot_ref),
        (source_hbm, source_ref), (target_hbm, target_ref), (weight_hbm, weight_ref),
        (pick_hbm, pick_ref), (vertex_hbm, vertex_ref),
    ]
    fetches = [pltpu.make_async_copy(a, b, fetched.at[i]) for i, (a, b) in enumerate(small)]
    for fetch in fetches:
        fetch.start()
    barrier = pltpu.get_barrier_semaphore()
    peers = [outer * 8 + (inner + i) % 8 for i in range(1, 8)]
    peers += [((outer + i) % 16) * 8 + inner for i in range(1, 16)]
    peers += [before, after]
    for peer in peers:
        pl.semaphore_signal(barrier, inc=1, device_id=(peer,), device_id_type=MESH)
    loads = [pltpu.make_async_copy(inv_hbm.at[c], inverse.at[c], loaded.at[c]) for c in range(4)]
    loads += [
        pltpu.make_async_copy(
            mesh_hbm.at[0, :, :, pl.ds(128 * q, 128)],
            field.at[q, pl.ds(2, 16), pl.ds(8, 96)],
            loaded.at[4 + q],
        )
        for q in range(4)
    ]
    for load in loads:
        load.start()

    finish(fetches[:2])
    pick_messages(
        node_ref, lambda k, r: disp_ref[k : k + 1, r * 128 : (r + 1) * 128], messages
    )
    pl.semaphore_wait(barrier, 24)

    copies = first_stage(messages, held, send1, recv1, outer, inner)
    finish(fetches[2:])
    neighbour_band(band)
    clear_margins(field)
    clear_margins(once)
    exponent_rows(source_ref, target_ref, left, right)
    kernel_values(0, left, right, upper, lower)
    kernel_values(1, left, right, upper, lower)
    finish(copies)
    copies = second_stage(held, ready, landed, send2, recv2, outer, inner)
    kernel_values(2, left, right, upper, lower)
    kernel_values(3, left, right, upper, lower)
    finish(copies)
    halos = [
        remote(mesh_hbm.at[0, pl.ds(14, 2)], halo.at[0], send5.at[0], recv5.at[0], after),
        remote(mesh_hbm.at[0, pl.ds(0, 2)], halo.at[1], send5.at[1], recv5.at[1], before),
    ]
    late = [
        remote(mesh_hbm.at[1, pl.ds(14, 2)], left_hbm.at[0], send5.at[2], recv5.at[2], after),
        remote(mesh_hbm.at[1, pl.ds(0, 2)], right_hbm.at[0], send5.at[3], recv5.at[3], before),
    ]

    gather_members(landed, slot_ref, member)
    for c in range(4):
        loads[c].wait()
        contribute(c, member, inverse, upper, lower, weight_ref, result)
    pick_messages(
        pick_ref,
        lambda k, r: result[r // 8, k : k + 1, (r % 8) * 128 : (r % 8 + 1) * 128],
        messages2,
    )
    finish(loads[4:])
    copies = first_stage(messages2, held2, send3, recv3, outer, inner)
    finish(halos)
    for q in range(4):
        lanes = slice(128 * q, 128 * (q + 1))
        for side in range(2):
            for x in range(2):
                field[q, 18 * side + x, 8:104, :] = halo[side, x, :, lanes]
        for x in range(1, 19):
            field[q, x, 8:9, :] = jnp.zeros((1, 128), f32)
    close_end(field, 1, has_left)
    close_end(field, 18, has_right)
    for i in range(2):
        swept(field, once, band, 9, 9 * i + 1, 9 * i)
    close_end(once, 0, has_left)
    close_end(once, 17, has_right)
    finish(copies)
    copies = second_stage(held2, ready2, landed2, send4, recv4, outer, inner)
    for i in range(2):
        swept(once, field, band, 8, 8 * i + 1, 8 * i + 2)
    whole = [
        pltpu.make_async_copy(
            field.at[q, pl.ds(2, 16), pl.ds(8, 96)],
            part_hbm.at[:, :, pl.ds(128 * q, 128)],
            stored.at[q],
        )
        for q in range(4)
    ]
    for copy in whole:
        copy.start()
    finish(copies)
    halos = late + [
        remote(mesh_hbm.at[2, pl.ds(14, 2)], left_hbm.at[1], send5.at[6], recv5.at[6], after),
        remote(mesh_hbm.at[2, pl.ds(0, 2)], right_hbm.at[1], send5.at[7], recv5.at[7], before),
    ]

    scatter(landed2, vertex_ref, values, places, total, inter_ref)
    ends[...] = jnp.zeros_like(ends)
    for k in range(3):
        ends[0, k : k + 1, :] = inter_ref[k, 0:1, :]
        ends[1, k : k + 1, :] = inter_ref[k, 15:16, :]
    edges = [
        remote(ends.at[1], near.at[0], send5.at[4], recv5.at[4], after),
        remote(ends.at[0], near.at[1], send5.at[5], recv5.at[5], before),
    ]
    wall = pltpu.make_async_copy(inter_ref, inter_hbm, stored.at[4])
    wall.start()
    finish(edges)
    edge = pltpu.make_async_copy(near, edge_hbm, stored.at[5])
    edge.start()
    finish(whole)
    wall.wait()
    edge.wait()
    finish(halos)


def smooth_kernel(
    place_ref, inter_ref, edge_ref, part_hbm, mesh_hbm, left_hbm, right_hbm, out_hbm,
    field, once, swept_part, band, arrived, leaving,
):
    place = place_ref[0]
    has_left, has_right = place > 0, place < 127

    def fetch(k, half):
        first, count = ((0, 9), (9, 7))[half]
        side, at = ((left_hbm, 0), (right_hbm, 18))[half]
        copies = []
        for q in range(4):
            lanes = pl.ds(128 * q, 128)
            copies.append(
                pltpu.make_async_copy(
                    mesh_hbm.at[k, pl.ds(first, count), :, lanes],
                    field.at[k - 1, q, pl.ds(first + 2, count), pl.ds(8, 96)],
                    arrived.at[k, half, q, 0],
                )
            )
            copies.append(
                pltpu.make_async_copy(
                    side.at[k - 1, :, :, lanes],
                    field.at[k - 1, q, pl.ds(at, 2), pl.ds(8, 96)],
                    arrived.at[k, half, q, 1],
                )
            )
        return copies

    def store(k, half):
        return [
            pltpu.make_async_copy(
                field.at[k - 1, q, pl.ds(2 + 8 * half, 8), pl.ds(8, 96)],
                out_hbm.at[k, pl.ds(8 * half, 8), :, pl.ds(128 * q, 128)],
                leaving.at[k, half, q],
            )
            for q in range(4)
        ]

    for k in (1, 2):
        for half in range(2):
            for copy in fetch(k, half):
                copy.start()
    early = pltpu.make_async_copy(part_hbm, swept_part, arrived.at[0, 0, 0, 0])
    early.start()
    done = pltpu.make_async_copy(swept_part, out_hbm.at[0], leaving.at[0, 0, 0])
    neighbour_band(band)
    clear_margins(once)
    for k in (1, 2):
        part = field.at[k - 1]
        clear_margins(part)
        for half in range(2):
            finish(fetch(k, half))
            for q in range(4):
                lanes = slice(128 * q, 128 * (q + 1))
                for x in range(9 * half, 9 + 7 * half):
                    part[q, x + 2, 8:9, :] = inter_ref[k, x : x + 1, lanes]
                end = 1 + 17 * half
                part[q, end, 8:9, :] = edge_ref[half, k : k + 1, lanes]
            close_end(part, 1 + 17 * half, (has_left, has_right)[half])
            swept(part, once, band, 9, 9 * half + 1, 9 * half)
        close_end(once, 0, has_left)
        close_end(once, 17, has_right)
        if k == 1:
            early.wait()
            add_wall(
                inter_ref[0],
                jnp.where(has_left, edge_ref[0, 0:1, :], 0.0),
                jnp.where(has_right, edge_ref[1, 0:1, :], 0.0),
                swept_part,
            )
            done.start()
        for half in range(2):
            swept(once, part, band, 8, 8 * half + 1, 8 * half + 2)
            for copy in store(k, half):
                copy.start()
    done.wait()
    for k in (1, 2):
        for half in range(2):
            finish(store(k, half))


def transfer(
    displacement, send_node, member_slot, inverse_part, source_coord, target_coord,
    unity_weight, result_pick, receive_vertex, mesh_before,
):
    hbm = pl.BlockSpec(memory_space=pl.ANY)
    dma = pltpu.SemaphoreType.DMA
    halo = jax.ShapeDtypeStruct((2, 2, 96, 512), f32)
    exchange = [
        pltpu.VMEM((192, 128), f32),
        pltpu.VMEM((192, 128), f32),
        pltpu.VMEM((16, 12, 128), f32),
        pltpu.VMEM((16, 12, 128), f32),
    ]
    small = [
        displacement,
        send_node.reshape(64, 128),
        member_slot,
        source_coord.transpose(1, 0, 2),
        target_coord.transpose(1, 0, 2),
        unity_weight,
        result_pick.reshape(64, 128),
        receive_vertex.reshape(64, 128),
    ]
    return pl.pallas_call(
        transfer_kernel,
        out_shape=(
            jax.ShapeDtypeStruct((3, 16, 512), f32),
            jax.ShapeDtypeStruct((2, 8, 512), f32),
            halo,
            halo,
            jax.ShapeDtypeStruct((16, 96, 512), f32),
        ),
        in_specs=[hbm] * 10,
        out_specs=(hbm,) * 5,
        scratch_shapes=[pltpu.VMEM(a.shape, a.dtype) for a in small]
        + exchange
        + exchange
        + [
            pltpu.VMEM((4, 1024, 1024), bf16),
            pltpu.VMEM((8, 32, 128), f32),
            pltpu.VMEM((8, 128, 128), f32),
            pltpu.VMEM((8, 128, 128), f32),
            pltpu.VMEM((4, 1024, 1024), bf16),
            pltpu.VMEM((4, 1024, 1024), bf16),
            pltpu.VMEM((4, 8, 1024), f32),
            pltpu.VMEM((4, 384, 512), bf16),
            pltpu.VMEM((4, 128, 512), bf16),
            pltpu.VMEM((384, 128), f32),
            pltpu.VMEM((3, 16, 512), f32),
            pltpu.VMEM((2, 8, 512), f32),
            pltpu.VMEM((2, 8, 512), f32),
            pltpu.VMEM((4, 20, 112, 128), f32),
            pltpu.VMEM((4, 18, 112, 128), f32),
            pltpu.VMEM((2, 2, 96, 512), f32),
            pltpu.VMEM((512, 256), bf16),
            dma((8,)),
            dma((8,)),
            dma((7,)),
            dma((7,)),
            dma((15,)),
            dma((15,)),
            dma((7,)),
            dma((7,)),
            dma((15,)),
            dma((15,)),
            dma((8,)),
            dma((8,)),
            dma((6,)),
        ],
        compiler_params=pltpu.CompilerParams(
            collective_id=1, has_side_effects=True, vmem_limit_bytes=63 << 20
        ),
    )(*small, inverse_part, mesh_before)


def smooth(place, interface, edges, part, mesh_before, left, right):
    hbm = pl.BlockSpec(memory_space=pl.ANY)
    return pl.pallas_call(
        smooth_kernel,
        out_shape=jax.ShapeDtypeStruct((3, 16, 96, 512), f32),
        in_specs=[pl.BlockSpec(memory_space=pltpu.SMEM), vmem(), vmem(), hbm, hbm, hbm, hbm],
        out_specs=hbm,
        scratch_shapes=[
            pltpu.VMEM((2, 4, 20, 112, 128), f32),
            pltpu.VMEM((4, 18, 112, 128), f32),
            pltpu.VMEM((16, 96, 512), f32),
            pltpu.VMEM((512, 256), bf16),
            pltpu.SemaphoreType.DMA((3, 2, 4, 2)),
            pltpu.SemaphoreType.DMA((3, 2, 4)),
        ],
        compiler_params=pltpu.CompilerParams(vmem_limit_bytes=63 << 20),
    )(place, interface, edges, part, mesh_before, left, right)


def local(
    displacement,
    send_node,
    member_slot,
    inverse_part,
    source_coord,
    target_coord,
    unity_weight,
    result_pick,
    receive_vertex,
    mesh_before,
):
    place = lax.axis_index("dev").astype(jnp.int32).reshape(1)
    interface, edges, left, right, part = transfer(
        displacement, send_node, member_slot, inverse_part, source_coord, target_coord,
        unity_weight, result_pick, receive_vertex, mesh_before,
    )
    return smooth(place, interface, edges, part, mesh_before, left, right)


def solution(mesh):
    in_specs = (
        P(None, "dev"),
        P("dev"),
        P("dev", None),
        P("dev", None, None),
        P("dev", None, None),
        P("dev", None, None),
        P("dev", None),
        P("dev"),
        P("dev"),
        P(None, "dev", None, None),
    )
    out_specs = P(None, "dev", None, None)
    return jax.shard_map(local, mesh=mesh, in_specs=in_specs, out_specs=out_specs, check_vma=False)
```

```python
import jax
import jax.numpy as jnp
from jax import lax
from jax.experimental import pallas as pl
from jax.experimental.pallas import tpu as pltpu
from jax.sharding import PartitionSpec as P

relax_rate = 0.8
kernel_sharpness = 8.0
log2_e = 1.4426950408889634
spread_rate = relax_rate / 6.0
keep_rate = 1.0 - relax_rate

MESH = pl.DeviceIdType.MESH
f32 = jnp.float32
bf16 = jnp.bfloat16


def vmem():
    return pl.BlockSpec(memory_space=pltpu.VMEM)


def lookup(row, lanes):
    spread = jnp.broadcast_to(row, lanes.shape)
    return jnp.take_along_axis(spread, lanes, axis=1, mode="promise_in_bounds")


def message_index(index_ref, step):
    x, core = step // 2, step % 2
    even = index_ref[pl.ds(x, 8, stride=8), :]
    odd = index_ref[pl.ds(4 + x, 8, stride=8), :]
    lane = lax.broadcasted_iota(jnp.int32, (8, 128), 1)
    if core == 0:
        return jnp.where(lane < 64, even, pltpu.roll(odd, 64, 1))
    return jnp.where(lane < 64, pltpu.roll(even, 64, 1), odd)


def pick_messages(index_ref, row_of, out_ref):
    for half in range(2):
        index = [message_index(index_ref, 4 * half + g) for g in range(4)]
        high = [jnp.right_shift(i, 7) for i in index]
        low = [jnp.bitwise_and(i, 127) for i in index]
        total = [[jnp.zeros((8, 128), f32) for _ in range(3)] for _ in range(4)]
        for r in range(32):
            hit = [h == r for h in high]
            for k in range(3):
                row = row_of(k, r)
                for g in range(4):
                    total[g][k] = jnp.where(hit[g], lookup(row, low[g]), total[g][k])
        for g in range(4):
            for k in range(3):
                top = ((4 * half + g) * 3 + k) * 8
                out_ref[top : top + 8, :] = total[g][k]


def three_parts(value):
    high = value.astype(bf16).astype(f32)
    rest = value - high
    middle = rest.astype(bf16).astype(f32)
    return high, middle, rest - middle


def cluster_rows(ref, c, rows):
    return jnp.concatenate([ref[q, pl.ds(c, rows, stride=4), :] for q in range(8)], axis=1)


def remote(source, target, send, receive, device):
    copy = pltpu.make_async_remote_copy(
        src_ref=source,
        dst_ref=target,
        send_sem=send,
        recv_sem=receive,
        device_id=(device,),
        device_id_type=MESH,
    )
    copy.start()
    return copy


def first_stage(messages, held, send, receive, outer, inner):
    copies = []
    for i in range(1, 8):
        p = (inner + i) % 8
        copies.append(
            remote(
                messages.at[pl.ds(pl.multiple_of(p * 24, 8), 24)],
                held.at[pl.ds(pl.multiple_of(inner * 24, 8), 24)],
                send.at[i - 1],
                receive.at[i - 1],
                outer * 8 + p,
            )
        )
    mine = pl.ds(pl.multiple_of(inner * 24, 8), 24)
    held[mine, :] = messages[mine, :]
    return copies


def second_stage(held, ready, landed, send, receive, outer, inner):
    lane = lax.broadcasted_iota(jnp.int32, (4, 128), 1)
    for m in range(8):
        for k in range(3):
            first = held[pl.ds(k * 8 + m, 4, stride=48), :]
            second = held[pl.ds(24 + k * 8 + m, 4, stride=48), :]
            ready[2 * m, 4 * k : 4 * k + 4, :] = jnp.where(
                lane < 64, first, pltpu.roll(second, 64, 1)
            )
            ready[2 * m + 1, 4 * k : 4 * k + 4, :] = jnp.where(
                lane < 64, pltpu.roll(first, 64, 1), second
            )
    copies = []
    for i in range(1, 16):
        p = (outer + i) % 16
        copies.append(
            remote(
                ready.at[p],
                landed.at[outer],
                send.at[i - 1],
                receive.at[i - 1],
                p * 8 + inner,
            )
        )
    landed[outer] = ready[outer]
    return copies


def finish(copies):
    for copy in copies:
        copy.wait()


def exponent_rows(source_ref, target_ref, left, right):
    left[...] = jnp.zeros_like(left)
    right[...] = jnp.zeros_like(right)
    ones = jnp.ones((4, 1024), f32)
    source_norm = jnp.zeros((4, 1024), f32)
    target_norm = jnp.zeros((4, 1024), f32)
    pairs = []
    for d in range(3):
        s = source_ref[d]
        t = target_ref[d]
        source_norm += s * s
        target_norm += t * t
        sh, sm, sl = three_parts(s)
        th, tm, tl = three_parts(t * (2.0 * kernel_sharpness * log2_e))
        pairs += [(sh, th), (sh, tm), (sm, th), (sh, tl), (sl, th), (sm, tm)]
    pairs += [(p, ones) for p in three_parts(source_norm * (-kernel_sharpness * log2_e))]
    pairs += [(ones, p) for p in three_parts(target_norm * (-kernel_sharpness * log2_e))]
    for row, (a, b) in enumerate(pairs):
        for q in range(8):
            left[q, 4 * row : 4 * row + 4, :] = a[:, 128 * q : 128 * (q + 1)]
            right[q, 4 * row : 4 * row + 4, :] = b[:, 128 * q : 128 * (q + 1)]


def kernel_values(c, left, right, upper, lower):
    source_rows = cluster_rows(left, c, 32).T.astype(bf16)
    target_rows = cluster_rows(right, c, 32).astype(bf16)
    for p in range(4):
        rows = slice(256 * p, 256 * (p + 1))
        kernel = jnp.exp2(jnp.dot(source_rows[rows], target_rows, preferred_element_type=f32))
        high = kernel.astype(bf16)
        upper[c, rows, :] = high
        lower[c, rows, :] = (kernel - high.astype(f32)).astype(bf16)


def gather_members(table, slot_ref, member):
    member[...] = jnp.zeros_like(member)
    index = [
        jnp.concatenate(
            [slot_ref[:, 256 * m : 256 * m + 128], slot_ref[:, 256 * m + 128 : 256 * m + 256]],
            axis=0,
        )
        for m in range(4)
    ]
    high = [jnp.right_shift(i, 7) for i in index]
    low = [jnp.bitwise_and(i, 127) for i in index]

    def gather(part, total):
        total = list(total)
        for r in range(16):
            zy, j = part * 4 + r // 4, r % 4
            hit = [h == part * 16 + r for h in high]
            for k in range(3):
                line = table[zy, 4 * k + j : 4 * k + j + 1, :]
                for m in range(4):
                    total[3 * m + k] = jnp.where(hit[m], lookup(line, low[m]), total[3 * m + k])
        return tuple(total)

    total = lax.fori_loop(
        0, 4, gather, tuple(jnp.zeros((8, 128), f32) for _ in range(12))
    )
    for m in range(4):
        for k in range(3):
            value = total[3 * m + k]
            member[2 * m, 4 * k : 4 * k + 4, :] = value[0:4]
            member[2 * m + 1, 4 * k : 4 * k + 4, :] = value[4:8]


def contribute(c, member, inverse, upper, lower, weight_ref, result):
    members = cluster_rows(member, c, 8)
    padded = jnp.concatenate([members, jnp.zeros((8, 1024), f32)], axis=0)
    coupling = lax.dot_general(
        padded.astype(bf16), inverse[c], (((1,), (1,)), ((), ())), preferred_element_type=f32
    )
    coefficient = members + coupling[0:8]
    high = coefficient.astype(bf16).astype(f32)
    both = jnp.concatenate([high, coefficient - high], axis=0).astype(bf16)
    summed = jnp.dot(both, upper[c], preferred_element_type=f32)
    summed += jnp.dot(both, lower[c], preferred_element_type=f32)
    result[c] = (summed[0:8] + summed[8:16]) * weight_ref[c : c + 1, :]


def scatter(table, vertex_ref, values, places, total, out_ref):
    def chunk(group, carry):
        product = jnp.zeros((384, 128), f32)
        for part in range(4):
            zy = group * 4 + part
            for j in range(4):
                vertex = vertex_ref[pl.ds(zy * 4 + j, 1), :]
                high = jnp.broadcast_to(jnp.right_shift(vertex, 7), (64, 128))
                low = jnp.broadcast_to(jnp.bitwise_and(vertex, 127), (128, 128))
                at_high = high == lax.broadcasted_iota(jnp.int32, (64, 128), 0)
                at_low = low == lax.broadcasted_iota(jnp.int32, (128, 128), 0)
                lanes = slice(128 * j, 128 * j + 128)
                places[part, :, lanes] = jnp.where(at_low, 1.0, 0.0).astype(bf16)
                for k in range(3):
                    value = table[zy, 4 * k + j : 4 * k + j + 1, :]
                    upper = value.astype(bf16).astype(f32)
                    for s, half in enumerate((upper, value - upper)):
                        spread = jnp.broadcast_to(half, (64, 128))
                        top = (2 * k + s) * 64
                        values[part, top : top + 64, lanes] = jnp.where(
                            at_high, spread, 0.0
                        ).astype(bf16)
            product += lax.dot_general(
                values[part],
                places[part],
                (((1,), (1,)), ((), ())),
                preferred_element_type=f32,
            )
        total[...] += product
        return carry

    total[...] = jnp.zeros_like(total)
    lax.fori_loop(0, 4, chunk, 0)
    for k in range(3):
        top = 2 * k * 64
        for q in range(4):
            out_ref[k, :, 128 * q : 128 * (q + 1)] = (
                total[pl.ds(top + q, 16, stride=4), :]
                + total[pl.ds(top + 64 + q, 16, stride=4), :]
            )


def neighbour_band(band):
    row = jnp.bitwise_and(lax.broadcasted_iota(jnp.int32, (512, 256), 0), 255)
    column = lax.broadcasted_iota(jnp.int32, (512, 256), 1)
    near = (row == column + 1) | (row == column - 1)
    band[...] = jnp.where(near, 1.0, 0.0).astype(bf16)


def clear_margins(field):
    count = field.shape[1]
    for q in range(4):
        for x in range(count):
            field[q, x, 0:8, :] = jnp.zeros((8, 128), f32)
            field[q, x, 104:112, :] = jnp.zeros((8, 128), f32)


def swept(source, target, band, count, start, place):
    lane = lax.broadcasted_iota(jnp.int32, (count, 96, 128), 2)
    line = lax.broadcasted_iota(jnp.int32, (count, 96, 128), 1)
    here = pl.ds(start, count)
    center = [source[q, here, 8:104, :] for q in range(4)]
    upper, lower = [], []
    for part in center:
        high = part.astype(bf16)
        upper.append(high.reshape(count * 96, 128))
        lower.append((part - high.astype(f32)).astype(bf16).reshape(count * 96, 128))
    along = []
    for q in (0, 2):
        parts = jnp.concatenate([upper[q], upper[q + 1], lower[q], lower[q + 1]], axis=1)
        along.append(jnp.dot(parts, band[...], preferred_element_type=f32))
    for q in range(4):
        beside = along[q // 2][:, 128 * (q % 2) : 128 * (q % 2) + 128].reshape(count, 96, 128)
        if q == 1:
            beside = beside + jnp.where(lane == 127, pltpu.roll(center[2], 127, 2), 0.0)
        if q == 2:
            beside = beside + jnp.where(lane == 0, pltpu.roll(center[1], 1, 2), 0.0)
        beside = beside + (source[q, here, 7:103, :] + source[q, here, 9:105, :])
        beside = beside + (
            source[q, pl.ds(start - 1, count), 8:104, :]
            + source[q, pl.ds(start + 1, count), 8:104, :]
        )
        moved = center[q] * keep_rate + beside * spread_rate
        target[q, pl.ds(place, count), 8:104, :] = jnp.where(line == 0, center[q], moved)


def close_end(field, x, inside):
    @pl.when(jnp.logical_not(inside))
    def _():
        for q in range(4):
            field[q, x, 8:104, :] = jnp.zeros((96, 128), f32)


def sweep_open(field, once, halo, band, has_left, has_right):
    for q in range(4):
        lanes = slice(128 * q, 128 * (q + 1))
        for side in range(2):
            for x in range(2):
                field[q, 18 * side + x, 8:104, :] = halo[side, x, :, lanes]
        for x in range(1, 19):
            field[q, x, 8:9, :] = jnp.zeros((1, 128), f32)
    close_end(field, 1, has_left)
    close_end(field, 18, has_right)
    for i in range(2):
        swept(field, once, band, 9, 9 * i + 1, 9 * i)
    close_end(once, 0, has_left)
    close_end(once, 17, has_right)
    for i in range(2):
        swept(once, field, band, 8, 8 * i + 1, 8 * i + 2)


def add_wall(inter, before, after, field):
    lane = lax.broadcasted_iota(jnp.int32, (16, 512), 1)
    line = lax.broadcasted_iota(jnp.int32, (16, 512), 0)
    beside = jnp.where(line == 0, before, pltpu.roll(inter, 1, 0))
    beside = beside + jnp.where(line == 15, after, pltpu.roll(inter, 15, 0))
    beside = beside + jnp.where(lane == 0, 0.0, pltpu.roll(inter, 1, 1))
    beside = beside + jnp.where(lane == 511, 0.0, pltpu.roll(inter, 511, 1))
    first = spread_rate * ((1.0 + keep_rate) * inter + spread_rate * beside)
    second = (spread_rate * spread_rate) * inter
    row = lax.broadcasted_iota(jnp.int32, (8, 512), 0)
    for x in range(16):
        extra = jnp.where(
            row == 0,
            inter[x : x + 1],
            jnp.where(row == 1, first[x : x + 1], jnp.where(row == 2, second[x : x + 1], 0.0)),
        )
        field[x, 0:8, :] += extra


def transfer_kernel(
    disp_hbm, node_hbm, slot_hbm, source_hbm, target_hbm, weight_hbm, pick_hbm, vertex_hbm,
    inv_hbm, mesh_hbm,
    inter_hbm, edge_hbm, left_hbm, right_hbm, part_hbm,
    disp_ref, node_ref, slot_ref, source_ref, target_ref, weight_ref, pick_ref, vertex_ref,
    messages, held, ready, landed, messages2, held2, ready2, landed2,
    inverse, member, left, right, upper, lower, result, values, places, total,
    inter_ref, ends, near, field, once, halo, band,
    fetched, loaded, send1, recv1, send2, recv2, send3, recv3, send4, recv4, send5, recv5, stored,
):
    me = lax.axis_index("dev")
    outer, inner = me // 8, me % 8
    before, after = (me + 127) % 128, (me + 1) % 128
    has_left, has_right = me > 0, me < 127

    small = [
        (disp_hbm, disp_ref), (node_hbm, node_ref), (slot_hbm, slot_ref),
        (source_hbm, source_ref), (target_hbm, target_ref), (weight_hbm, weight_ref),
        (pick_hbm, pick_ref), (vertex_hbm, vertex_ref),
    ]
    fetches = [pltpu.make_async_copy(a, b, fetched.at[i]) for i, (a, b) in enumerate(small)]
    for fetch in fetches:
        fetch.start()
    barrier = pltpu.get_barrier_semaphore()
    peers = [outer * 8 + (inner + i) % 8 for i in range(1, 8)]
    peers += [((outer + i) % 16) * 8 + inner for i in range(1, 16)]
    peers += [before, after]
    for peer in peers:
        pl.semaphore_signal(barrier, inc=1, device_id=(peer,), device_id_type=MESH)
    loads = [pltpu.make_async_copy(inv_hbm.at[c], inverse.at[c], loaded.at[c]) for c in range(4)]
    loads += [
        pltpu.make_async_copy(
            mesh_hbm.at[k, :, :, pl.ds(128 * q, 128)],
            field.at[k, q, pl.ds(2, 16), pl.ds(8, 96)],
            loaded.at[4 + 4 * k + q],
        )
        for k in range(2)
        for q in range(4)
    ]
    for load in loads:
        load.start()

    finish(fetches[:2])
    pick_messages(
        node_ref, lambda k, r: disp_ref[k : k + 1, r * 128 : (r + 1) * 128], messages
    )
    pl.semaphore_wait(barrier, 24)

    copies = first_stage(messages, held, send1, recv1, outer, inner)
    finish(fetches[2:])
    neighbour_band(band)
    clear_margins(field.at[0])
    clear_margins(field.at[1])
    clear_margins(once)
    exponent_rows(source_ref, target_ref, left, right)
    kernel_values(0, left, right, upper, lower)
    kernel_values(1, left, right, upper, lower)
    finish(copies)
    copies = second_stage(held, ready, landed, send2, recv2, outer, inner)
    kernel_values(2, left, right, upper, lower)
    kernel_values(3, left, right, upper, lower)
    finish(copies)
    halos = []
    for k in range(2):
        halos += [
            remote(
                mesh_hbm.at[k, pl.ds(14, 2)], halo.at[k, 0],
                send5.at[2 * k], recv5.at[2 * k], after,
            ),
            remote(
                mesh_hbm.at[k, pl.ds(0, 2)], halo.at[k, 1],
                send5.at[2 * k + 1], recv5.at[2 * k + 1], before,
            ),
        ]

    gather_members(landed, slot_ref, member)
    for c in range(4):
        loads[c].wait()
        contribute(c, member, inverse, upper, lower, weight_ref, result)
    pick_messages(
        pick_ref,
        lambda k, r: result[r // 8, k : k + 1, (r % 8) * 128 : (r % 8 + 1) * 128],
        messages2,
    )
    finish(loads[4:])
    copies = first_stage(messages2, held2, send3, recv3, outer, inner)
    finish(halos[:2])
    sweep_open(field.at[0], once, halo.at[0], band, has_left, has_right)
    finish(copies)
    copies = second_stage(held2, ready2, landed2, send4, recv4, outer, inner)
    finish(halos[2:])
    sweep_open(field.at[1], once, halo.at[1], band, has_left, has_right)
    whole = [
        pltpu.make_async_copy(
            field.at[k, q, pl.ds(2, 16), pl.ds(8, 96)],
            part_hbm.at[k, :, :, pl.ds(128 * q, 128)],
            stored.at[4 * k + q],
        )
        for k in range(2)
        for q in range(4)
    ]
    for copy in whole:
        copy.start()
    finish(copies)
    halos = [
        remote(mesh_hbm.at[2, pl.ds(14, 2)], left_hbm, send5.at[6], recv5.at[6], after),
        remote(mesh_hbm.at[2, pl.ds(0, 2)], right_hbm, send5.at[7], recv5.at[7], before),
    ]

    scatter(landed2, vertex_ref, values, places, total, inter_ref)
    ends[...] = jnp.zeros_like(ends)
    for k in range(3):
        ends[0, k : k + 1, :] = inter_ref[k, 0:1, :]
        ends[1, k : k + 1, :] = inter_ref[k, 15:16, :]
    edges = [
        remote(ends.at[1], near.at[0], send5.at[4], recv5.at[4], after),
        remote(ends.at[0], near.at[1], send5.at[5], recv5.at[5], before),
    ]
    wall = pltpu.make_async_copy(inter_ref, inter_hbm, stored.at[8])
    wall.start()
    finish(edges)
    edge = pltpu.make_async_copy(near, edge_hbm, stored.at[9])
    edge.start()
    finish(whole)
    wall.wait()
    edge.wait()
    finish(halos)


def smooth_kernel(
    place_ref, inter_ref, edge_ref, part_hbm, mesh_hbm, left_hbm, right_hbm, out_hbm,
    field, once, opened, band, arrived, arrived_open, leaving, leaving_open,
):
    place = place_ref[0]
    has_left, has_right = place > 0, place < 127

    def fetch(half):
        first, count = ((0, 9), (9, 7))[half]
        side, at = ((left_hbm, 0), (right_hbm, 18))[half]
        copies = []
        for q in range(4):
            lanes = pl.ds(128 * q, 128)
            copies.append(
                pltpu.make_async_copy(
                    mesh_hbm.at[2, pl.ds(first, count), :, lanes],
                    field.at[q, pl.ds(first + 2, count), pl.ds(8, 96)],
                    arrived.at[half, q, 0],
                )
            )
            copies.append(
                pltpu.make_async_copy(
                    side.at[:, :, lanes],
                    field.at[q, pl.ds(at, 2), pl.ds(8, 96)],
                    arrived.at[half, q, 1],
                )
            )
        return copies

    def store(half):
        return [
            pltpu.make_async_copy(
                field.at[q, pl.ds(2 + 8 * half, 8), pl.ds(8, 96)],
                out_hbm.at[2, pl.ds(8 * half, 8), :, pl.ds(128 * q, 128)],
                leaving.at[half, q],
            )
            for q in range(4)
        ]

    arriving = [fetch(0), fetch(1)]
    for copy in arriving[0] + arriving[1]:
        copy.start()
    early = [
        pltpu.make_async_copy(part_hbm.at[k], opened.at[k], arrived_open.at[k]) for k in range(2)
    ]
    for copy in early:
        copy.start()
    stores = [
        pltpu.make_async_copy(opened.at[k], out_hbm.at[k], leaving_open.at[k]) for k in range(2)
    ]
    neighbour_band(band)
    clear_margins(once)
    clear_margins(field)
    for half in range(2):
        finish(arriving[half])
        for q in range(4):
            lanes = slice(128 * q, 128 * (q + 1))
            for x in range(9 * half, 9 + 7 * half):
                field[q, x + 2, 8:9, :] = inter_ref[2, x : x + 1, lanes]
            field[q, 1 + 17 * half, 8:9, :] = edge_ref[half, 2:3, lanes]
        close_end(field, 1 + 17 * half, (has_left, has_right)[half])
        swept(field, once, band, 9, 9 * half + 1, 9 * half)
        early[half].wait()
        add_wall(
            inter_ref[half],
            jnp.where(has_left, edge_ref[0, half : half + 1, :], 0.0),
            jnp.where(has_right, edge_ref[1, half : half + 1, :], 0.0),
            opened.at[half],
        )
        stores[half].start()
    close_end(once, 0, has_left)
    close_end(once, 17, has_right)
    for half in range(2):
        swept(once, field, band, 8, 8 * half + 1, 8 * half + 2)
        stores += store(half)
        for copy in stores[-4:]:
            copy.start()
    finish(stores)


def transfer(
    displacement, send_node, member_slot, inverse_part, source_coord, target_coord,
    unity_weight, result_pick, receive_vertex, mesh_before,
):
    hbm = pl.BlockSpec(memory_space=pl.ANY)
    dma = pltpu.SemaphoreType.DMA
    halo = jax.ShapeDtypeStruct((2, 96, 512), f32)
    exchange = [
        pltpu.VMEM((192, 128), f32),
        pltpu.VMEM((192, 128), f32),
        pltpu.VMEM((16, 12, 128), f32),
        pltpu.VMEM((16, 12, 128), f32),
    ]
    small = [
        displacement,
        send_node.reshape(64, 128),
        member_slot,
        source_coord.transpose(1, 0, 2),
        target_coord.transpose(1, 0, 2),
        unity_weight,
        result_pick.reshape(64, 128),
        receive_vertex.reshape(64, 128),
    ]
    return pl.pallas_call(
        transfer_kernel,
        out_shape=(
            jax.ShapeDtypeStruct((3, 16, 512), f32),
            jax.ShapeDtypeStruct((2, 8, 512), f32),
            halo,
            halo,
            jax.ShapeDtypeStruct((2, 16, 96, 512), f32),
        ),
        in_specs=[hbm] * 10,
        out_specs=(hbm,) * 5,
        scratch_shapes=[pltpu.VMEM(a.shape, a.dtype) for a in small]
        + exchange
        + exchange
        + [
            pltpu.VMEM((4, 1024, 1024), bf16),
            pltpu.VMEM((8, 32, 128), f32),
            pltpu.VMEM((8, 128, 128), f32),
            pltpu.VMEM((8, 128, 128), f32),
            pltpu.VMEM((4, 1024, 1024), bf16),
            pltpu.VMEM((4, 1024, 1024), bf16),
            pltpu.VMEM((4, 8, 1024), f32),
            pltpu.VMEM((4, 384, 512), bf16),
            pltpu.VMEM((4, 128, 512), bf16),
            pltpu.VMEM((384, 128), f32),
            pltpu.VMEM((3, 16, 512), f32),
            pltpu.VMEM((2, 8, 512), f32),
            pltpu.VMEM((2, 8, 512), f32),
            pltpu.VMEM((2, 4, 20, 112, 128), f32),
            pltpu.VMEM((4, 18, 112, 128), f32),
            pltpu.VMEM((2, 2, 2, 96, 512), f32),
            pltpu.VMEM((512, 256), bf16),
            dma((8,)),
            dma((12,)),
            dma((7,)),
            dma((7,)),
            dma((15,)),
            dma((15,)),
            dma((7,)),
            dma((7,)),
            dma((15,)),
            dma((15,)),
            dma((8,)),
            dma((8,)),
            dma((10,)),
        ],
        compiler_params=pltpu.CompilerParams(
            collective_id=1, has_side_effects=True, vmem_limit_bytes=63 << 20
        ),
    )(*small, inverse_part, mesh_before)


def smooth(place, interface, edges, part, mesh_before, left, right):
    hbm = pl.BlockSpec(memory_space=pl.ANY)
    return pl.pallas_call(
        smooth_kernel,
        out_shape=jax.ShapeDtypeStruct((3, 16, 96, 512), f32),
        in_specs=[pl.BlockSpec(memory_space=pltpu.SMEM), vmem(), vmem(), hbm, hbm, hbm, hbm],
        out_specs=hbm,
        scratch_shapes=[
            pltpu.VMEM((4, 20, 112, 128), f32),
            pltpu.VMEM((4, 18, 112, 128), f32),
            pltpu.VMEM((2, 16, 96, 512), f32),
            pltpu.VMEM((512, 256), bf16),
            pltpu.SemaphoreType.DMA((2, 4, 2)),
            pltpu.SemaphoreType.DMA((2,)),
            pltpu.SemaphoreType.DMA((2, 4)),
            pltpu.SemaphoreType.DMA((2,)),
        ],
        compiler_params=pltpu.CompilerParams(vmem_limit_bytes=63 << 20),
    )(place, interface, edges, part, mesh_before, left, right)


def local(
    displacement,
    send_node,
    member_slot,
    inverse_part,
    source_coord,
    target_coord,
    unity_weight,
    result_pick,
    receive_vertex,
    mesh_before,
):
    place = lax.axis_index("dev").astype(jnp.int32).reshape(1)
    interface, edges, left, right, part = transfer(
        displacement, send_node, member_slot, inverse_part, source_coord, target_coord,
        unity_weight, result_pick, receive_vertex, mesh_before,
    )
    return smooth(place, interface, edges, part, mesh_before, left, right)


def solution(mesh):
    in_specs = (
        P(None, "dev"),
        P("dev"),
        P("dev", None),
        P("dev", None, None),
        P("dev", None, None),
        P("dev", None, None),
        P("dev", None),
        P("dev"),
        P("dev"),
        P(None, "dev", None, None),
    )
    out_specs = P(None, "dev", None, None)
    return jax.shard_map(local, mesh=mesh, in_specs=in_specs, out_specs=out_specs, check_vma=False)
```

```python
import jax
import jax.numpy as jnp
from jax import lax
from jax.experimental import pallas as pl
from jax.experimental.pallas import tpu as pltpu
from jax.sharding import PartitionSpec as P

relax_rate = 0.8
kernel_sharpness = 8.0
log2_e = 1.4426950408889634
spread_rate = relax_rate / 6.0
keep_rate = 1.0 - relax_rate

MESH = pl.DeviceIdType.MESH
f32 = jnp.float32
bf16 = jnp.bfloat16


def vmem():
    return pl.BlockSpec(memory_space=pltpu.VMEM)


def lookup(row, lanes):
    spread = jnp.broadcast_to(row, lanes.shape)
    return jnp.take_along_axis(spread, lanes, axis=1, mode="promise_in_bounds")


def message_index(index_ref, step):
    x, core = step // 2, step % 2
    even = index_ref[pl.ds(x, 8, stride=8), :]
    odd = index_ref[pl.ds(4 + x, 8, stride=8), :]
    lane = lax.broadcasted_iota(jnp.int32, (8, 128), 1)
    if core == 0:
        return jnp.where(lane < 64, even, pltpu.roll(odd, 64, 1))
    return jnp.where(lane < 64, pltpu.roll(even, 64, 1), odd)


def pick_messages(index_ref, row_of, out_ref):
    for half in range(2):
        index = [message_index(index_ref, 4 * half + g) for g in range(4)]
        high = [jnp.right_shift(i, 7) for i in index]
        low = [jnp.bitwise_and(i, 127) for i in index]
        total = [[jnp.zeros((8, 128), f32) for _ in range(3)] for _ in range(4)]
        for r in range(32):
            hit = [h == r for h in high]
            for k in range(3):
                row = row_of(k, r)
                for g in range(4):
                    total[g][k] = jnp.where(hit[g], lookup(row, low[g]), total[g][k])
        for g in range(4):
            for k in range(3):
                top = ((4 * half + g) * 3 + k) * 8
                out_ref[top : top + 8, :] = total[g][k]


def three_parts(value):
    high = value.astype(bf16).astype(f32)
    rest = value - high
    middle = rest.astype(bf16).astype(f32)
    return high, middle, rest - middle


def cluster_rows(ref, c, rows):
    return jnp.concatenate([ref[q, pl.ds(c, rows, stride=4), :] for q in range(8)], axis=1)


def remote(source, target, send, receive, device):
    copy = pltpu.make_async_remote_copy(
        src_ref=source,
        dst_ref=target,
        send_sem=send,
        recv_sem=receive,
        device_id=(device,),
        device_id_type=MESH,
    )
    copy.start()
    return copy


def first_stage(messages, held, send, receive, outer, inner):
    copies = []
    for i in range(1, 8):
        p = (inner + i) % 8
        copies.append(
            remote(
                messages.at[pl.ds(pl.multiple_of(p * 24, 8), 24)],
                held.at[pl.ds(pl.multiple_of(inner * 24, 8), 24)],
                send.at[i - 1],
                receive.at[i - 1],
                outer * 8 + p,
            )
        )
    mine = pl.ds(pl.multiple_of(inner * 24, 8), 24)
    held[mine, :] = messages[mine, :]
    return copies


def second_stage(held, ready, landed, send, receive, outer, inner):
    lane = lax.broadcasted_iota(jnp.int32, (4, 128), 1)
    for m in range(8):
        for k in range(3):
            first = held[pl.ds(k * 8 + m, 4, stride=48), :]
            second = held[pl.ds(24 + k * 8 + m, 4, stride=48), :]
            ready[2 * m, 4 * k : 4 * k + 4, :] = jnp.where(
                lane < 64, first, pltpu.roll(second, 64, 1)
            )
            ready[2 * m + 1, 4 * k : 4 * k + 4, :] = jnp.where(
                lane < 64, pltpu.roll(first, 64, 1), second
            )
    copies = []
    for i in range(1, 16):
        p = (outer + i) % 16
        copies.append(
            remote(
                ready.at[p],
                landed.at[outer],
                send.at[i - 1],
                receive.at[i - 1],
                p * 8 + inner,
            )
        )
    landed[outer] = ready[outer]
    return copies


def shift(source_last, source_first, left, right, send, receive, me):
    has_left, has_right = me > 0, me < 127

    def descriptor(source, target, i, device):
        return pltpu.make_async_remote_copy(
            src_ref=source,
            dst_ref=target,
            send_sem=send[i],
            recv_sem=receive[i],
            device_id=(device,),
            device_id_type=MESH,
        )

    ahead = descriptor(source_last, left, 0, (me + 1) % 128)
    back = descriptor(source_first, right, 1, (me + 127) % 128)

    @pl.when(has_right)
    def _():
        ahead.start()

    @pl.when(has_left)
    def _():
        back.start()

    def wait():
        @pl.when(has_right)
        def _():
            ahead.wait_send()
            back.wait_recv()

        @pl.when(has_left)
        def _():
            back.wait_send()
            ahead.wait_recv()

    return wait


def finish(copies):
    for copy in copies:
        copy.wait()


def exponent_rows(source_ref, target_ref, left, right):
    left[...] = jnp.zeros_like(left)
    right[...] = jnp.zeros_like(right)
    ones = jnp.ones((4, 1024), f32)
    source_norm = jnp.zeros((4, 1024), f32)
    target_norm = jnp.zeros((4, 1024), f32)
    pairs = []
    for d in range(3):
        s = source_ref[d]
        t = target_ref[d]
        source_norm += s * s
        target_norm += t * t
        sh, sm, sl = three_parts(s)
        th, tm, tl = three_parts(t * (2.0 * kernel_sharpness * log2_e))
        pairs += [(sh, th), (sh, tm), (sm, th), (sh, tl), (sl, th), (sm, tm)]
    pairs += [(p, ones) for p in three_parts(source_norm * (-kernel_sharpness * log2_e))]
    pairs += [(ones, p) for p in three_parts(target_norm * (-kernel_sharpness * log2_e))]
    for row, (a, b) in enumerate(pairs):
        for q in range(8):
            left[q, 4 * row : 4 * row + 4, :] = a[:, 128 * q : 128 * (q + 1)]
            right[q, 4 * row : 4 * row + 4, :] = b[:, 128 * q : 128 * (q + 1)]


def kernel_values(c, left, right, upper, lower):
    source_rows = cluster_rows(left, c, 32).T.astype(bf16)
    target_rows = cluster_rows(right, c, 32).astype(bf16)
    for p in range(4):
        rows = slice(256 * p, 256 * (p + 1))
        kernel = jnp.exp2(jnp.dot(source_rows[rows], target_rows, preferred_element_type=f32))
        high = kernel.astype(bf16)
        upper[c, rows, :] = high
        lower[c, rows, :] = (kernel - high.astype(f32)).astype(bf16)


def gather_members(table, slot_ref, member):
    member[...] = jnp.zeros_like(member)
    index = [
        jnp.concatenate(
            [slot_ref[:, 256 * m : 256 * m + 128], slot_ref[:, 256 * m + 128 : 256 * m + 256]],
            axis=0,
        )
        for m in range(4)
    ]
    high = [jnp.right_shift(i, 7) for i in index]
    low = [jnp.bitwise_and(i, 127) for i in index]

    def gather(part, total):
        total = list(total)
        for r in range(16):
            zy, j = part * 4 + r // 4, r % 4
            hit = [h == part * 16 + r for h in high]
            for k in range(3):
                line = table[zy, 4 * k + j : 4 * k + j + 1, :]
                for m in range(4):
                    total[3 * m + k] = jnp.where(hit[m], lookup(line, low[m]), total[3 * m + k])
        return tuple(total)

    total = lax.fori_loop(
        0, 4, gather, tuple(jnp.zeros((8, 128), f32) for _ in range(12))
    )
    for m in range(4):
        for k in range(3):
            value = total[3 * m + k]
            member[2 * m, 4 * k : 4 * k + 4, :] = value[0:4]
            member[2 * m + 1, 4 * k : 4 * k + 4, :] = value[4:8]


def contribute(c, member, inverse, upper, lower, weight_ref, result):
    members = cluster_rows(member, c, 8)
    padded = jnp.concatenate([members, jnp.zeros((8, 1024), f32)], axis=0)
    coupling = lax.dot_general(
        padded.astype(bf16), inverse[c], (((1,), (1,)), ((), ())), preferred_element_type=f32
    )
    coefficient = members + coupling[0:8]
    high = coefficient.astype(bf16).astype(f32)
    both = jnp.concatenate([high, coefficient - high], axis=0).astype(bf16)
    summed = jnp.dot(both, upper[c], preferred_element_type=f32)
    summed += jnp.dot(both, lower[c], preferred_element_type=f32)
    result[c] = (summed[0:8] + summed[8:16]) * weight_ref[c : c + 1, :]


def scatter(table, vertex_ref, values, places, total, out_ref):
    def chunk(group, carry):
        product = jnp.zeros((384, 128), f32)
        for part in range(4):
            zy = group * 4 + part
            for j in range(4):
                vertex = vertex_ref[pl.ds(zy * 4 + j, 1), :]
                high = jnp.broadcast_to(jnp.right_shift(vertex, 7), (64, 128))
                low = jnp.broadcast_to(jnp.bitwise_and(vertex, 127), (128, 128))
                at_high = high == lax.broadcasted_iota(jnp.int32, (64, 128), 0)
                at_low = low == lax.broadcasted_iota(jnp.int32, (128, 128), 0)
                lanes = slice(128 * j, 128 * j + 128)
                places[part, :, lanes] = jnp.where(at_low, 1.0, 0.0).astype(bf16)
                for k in range(3):
                    value = table[zy, 4 * k + j : 4 * k + j + 1, :]
                    upper = value.astype(bf16).astype(f32)
                    for s, half in enumerate((upper, value - upper)):
                        spread = jnp.broadcast_to(half, (64, 128))
                        top = (2 * k + s) * 64
                        values[part, top : top + 64, lanes] = jnp.where(
                            at_high, spread, 0.0
                        ).astype(bf16)
            product += lax.dot_general(
                values[part],
                places[part],
                (((1,), (1,)), ((), ())),
                preferred_element_type=f32,
            )
        total[...] += product
        return carry

    total[...] = jnp.zeros_like(total)
    lax.fori_loop(0, 4, chunk, 0)
    for k in range(3):
        top = 2 * k * 64
        for q in range(4):
            out_ref[k, :, 128 * q : 128 * (q + 1)] = (
                total[pl.ds(top + q, 16, stride=4), :]
                + total[pl.ds(top + 64 + q, 16, stride=4), :]
            )


def neighbour_band(band):
    row = jnp.bitwise_and(lax.broadcasted_iota(jnp.int32, (512, 256), 0), 255)
    column = lax.broadcasted_iota(jnp.int32, (512, 256), 1)
    near = (row == column + 1) | (row == column - 1)
    band[...] = jnp.where(near, 1.0, 0.0).astype(bf16)


def clear_margins(field):
    count = field.shape[1]
    for q in range(4):
        for x in range(count):
            field[q, x, 0:8, :] = jnp.zeros((8, 128), f32)
            field[q, x, 104:112, :] = jnp.zeros((8, 128), f32)


def swept(source, target, band, count, start, place):
    lane = lax.broadcasted_iota(jnp.int32, (count, 96, 128), 2)
    line = lax.broadcasted_iota(jnp.int32, (count, 96, 128), 1)
    here = pl.ds(start, count)
    center = [source[q, here, 8:104, :] for q in range(4)]
    upper, lower = [], []
    for part in center:
        high = part.astype(bf16)
        upper.append(high.reshape(count * 96, 128))
        lower.append((part - high.astype(f32)).astype(bf16).reshape(count * 96, 128))
    along = []
    for q in (0, 2):
        parts = jnp.concatenate([upper[q], upper[q + 1], lower[q], lower[q + 1]], axis=1)
        along.append(jnp.dot(parts, band[...], preferred_element_type=f32))
    for q in range(4):
        beside = along[q // 2][:, 128 * (q % 2) : 128 * (q % 2) + 128].reshape(count, 96, 128)
        if q == 1:
            beside = beside + jnp.where(lane == 127, pltpu.roll(center[2], 127, 2), 0.0)
        if q == 2:
            beside = beside + jnp.where(lane == 0, pltpu.roll(center[1], 1, 2), 0.0)
        beside = beside + (source[q, here, 7:103, :] + source[q, here, 9:105, :])
        beside = beside + (
            source[q, pl.ds(start - 1, count), 8:104, :]
            + source[q, pl.ds(start + 1, count), 8:104, :]
        )
        moved = center[q] * keep_rate + beside * spread_rate
        target[q, pl.ds(place, count), 8:104, :] = jnp.where(line == 0, center[q], moved)


def close_end(field, x, inside):
    @pl.when(jnp.logical_not(inside))
    def _():
        for q in range(4):
            field[q, x, 8:104, :] = jnp.zeros((96, 128), f32)


def sweep_open(field, once, halo, band, has_left, has_right):
    for q in range(4):
        lanes = slice(128 * q, 128 * (q + 1))
        for side in range(2):
            for x in range(2):
                field[q, 18 * side + x, 8:104, :] = halo[side, x, :, lanes]
        for x in range(1, 19):
            field[q, x, 8:9, :] = jnp.zeros((1, 128), f32)
    close_end(field, 1, has_left)
    close_end(field, 18, has_right)
    for i in range(2):
        swept(field, once, band, 9, 9 * i + 1, 9 * i)
    close_end(once, 0, has_left)
    close_end(once, 17, has_right)
    for i in range(2):
        swept(once, field, band, 8, 8 * i + 1, 8 * i + 2)


def add_wall(inter, before, after, field):
    lane = lax.broadcasted_iota(jnp.int32, (16, 512), 1)
    line = lax.broadcasted_iota(jnp.int32, (16, 512), 0)
    beside = jnp.where(line == 0, before, pltpu.roll(inter, 1, 0))
    beside = beside + jnp.where(line == 15, after, pltpu.roll(inter, 15, 0))
    beside = beside + jnp.where(lane == 0, 0.0, pltpu.roll(inter, 1, 1))
    beside = beside + jnp.where(lane == 511, 0.0, pltpu.roll(inter, 511, 1))
    first = spread_rate * ((1.0 + keep_rate) * inter + spread_rate * beside)
    second = (spread_rate * spread_rate) * inter
    row = lax.broadcasted_iota(jnp.int32, (8, 512), 0)
    for x in range(16):
        extra = jnp.where(
            row == 0,
            inter[x : x + 1],
            jnp.where(row == 1, first[x : x + 1], jnp.where(row == 2, second[x : x + 1], 0.0)),
        )
        field[x, 0:8, :] += extra


def transfer_kernel(
    disp_hbm, node_hbm, slot_hbm, source_hbm, target_hbm, weight_hbm, pick_hbm, vertex_hbm,
    inv_hbm, mesh_hbm,
    inter_hbm, edge_hbm, left_hbm, right_hbm, part_hbm,
    disp_ref, node_ref, slot_ref, source_ref, target_ref, weight_ref, pick_ref, vertex_ref,
    messages, held, ready, landed, messages2, held2, ready2, landed2,
    inverse, member, left, right, upper, lower, result, values, places, total,
    inter_ref, ends, near, field, once, halo, band,
    fetched, loaded, send1, recv1, send2, recv2, send3, recv3, send4, recv4, send5, recv5, stored,
):
    me = lax.axis_index("dev")
    outer, inner = me // 8, me % 8
    before, after = (me + 127) % 128, (me + 1) % 128
    has_left, has_right = me > 0, me < 127

    small = [
        (disp_hbm, disp_ref), (node_hbm, node_ref), (slot_hbm, slot_ref),
        (source_hbm, source_ref), (target_hbm, target_ref), (weight_hbm, weight_ref),
        (pick_hbm, pick_ref), (vertex_hbm, vertex_ref),
    ]
    fetches = [pltpu.make_async_copy(a, b, fetched.at[i]) for i, (a, b) in enumerate(small)]
    for fetch in fetches:
        fetch.start()
    @pl.when(jnp.logical_not(has_left))
    def _():
        near[0] = jnp.zeros((8, 512), f32)
        for k in range(2):
            halo[k, 0] = jnp.zeros((2, 96, 512), f32)

    @pl.when(jnp.logical_not(has_right))
    def _():
        near[1] = jnp.zeros((8, 512), f32)
        for k in range(2):
            halo[k, 1] = jnp.zeros((2, 96, 512), f32)

    barrier = pltpu.get_barrier_semaphore()
    peers = [outer * 8 + (inner + i) % 8 for i in range(1, 8)]
    peers += [((outer + i) % 16) * 8 + inner for i in range(1, 16)]
    peers += [before, after]
    for peer in peers:
        pl.semaphore_signal(barrier, inc=1, device_id=(peer,), device_id_type=MESH)
    loads = [pltpu.make_async_copy(inv_hbm.at[c], inverse.at[c], loaded.at[c]) for c in range(4)]
    loads += [
        pltpu.make_async_copy(
            mesh_hbm.at[k, :, :, pl.ds(128 * q, 128)],
            field.at[k, q, pl.ds(2, 16), pl.ds(8, 96)],
            loaded.at[4 + 4 * k + q],
        )
        for k in range(2)
        for q in range(4)
    ]
    for load in loads:
        load.start()

    finish(fetches[:2])
    pick_messages(
        node_ref, lambda k, r: disp_ref[k : k + 1, r * 128 : (r + 1) * 128], messages
    )
    pl.semaphore_wait(barrier, 24)

    copies = first_stage(messages, held, send1, recv1, outer, inner)
    finish(fetches[2:])
    neighbour_band(band)
    clear_margins(field.at[0])
    clear_margins(field.at[1])
    clear_margins(once)
    exponent_rows(source_ref, target_ref, left, right)
    kernel_values(0, left, right, upper, lower)
    kernel_values(1, left, right, upper, lower)
    finish(copies)
    copies = second_stage(held, ready, landed, send2, recv2, outer, inner)

    def send_halo(k):
        return shift(
            mesh_hbm.at[k, pl.ds(14, 2)],
            mesh_hbm.at[k, pl.ds(0, 2)],
            halo.at[k, 0] if k < 2 else left_hbm,
            halo.at[k, 1] if k < 2 else right_hbm,
            (send5.at[2 * k], send5.at[2 * k + 1]),
            (recv5.at[2 * k], recv5.at[2 * k + 1]),
            me,
        )

    halo_waits = [send_halo(0)]
    kernel_values(2, left, right, upper, lower)
    kernel_values(3, left, right, upper, lower)
    finish(copies)
    halo_waits.append(send_halo(1))

    gather_members(landed, slot_ref, member)
    for c in range(4):
        loads[c].wait()
        contribute(c, member, inverse, upper, lower, weight_ref, result)
    pick_messages(
        pick_ref,
        lambda k, r: result[r // 8, k : k + 1, (r % 8) * 128 : (r % 8 + 1) * 128],
        messages2,
    )
    finish(loads[4:])
    copies = first_stage(messages2, held2, send3, recv3, outer, inner)
    halo_waits[0]()
    sweep_open(field.at[0], once, halo.at[0], band, has_left, has_right)
    finish(copies)
    copies = second_stage(held2, ready2, landed2, send4, recv4, outer, inner)
    halo_waits[1]()
    sweep_open(field.at[1], once, halo.at[1], band, has_left, has_right)
    whole = [
        pltpu.make_async_copy(
            field.at[k, q, pl.ds(2, 16), pl.ds(8, 96)],
            part_hbm.at[k, :, :, pl.ds(128 * q, 128)],
            stored.at[4 * k + q],
        )
        for k in range(2)
        for q in range(4)
    ]
    for copy in whole:
        copy.start()
    finish(copies)
    halo_waits.append(send_halo(2))

    scatter(landed2, vertex_ref, values, places, total, inter_ref)
    ends[...] = jnp.zeros_like(ends)
    for k in range(3):
        ends[0, k : k + 1, :] = inter_ref[k, 0:1, :]
        ends[1, k : k + 1, :] = inter_ref[k, 15:16, :]
    edge_wait = shift(
        ends.at[1],
        ends.at[0],
        near.at[0],
        near.at[1],
        (send5.at[6], send5.at[7]),
        (recv5.at[6], recv5.at[7]),
        me,
    )
    wall = pltpu.make_async_copy(inter_ref, inter_hbm, stored.at[8])
    wall.start()
    edge_wait()
    edge = pltpu.make_async_copy(near, edge_hbm, stored.at[9])
    edge.start()
    finish(whole)
    wall.wait()
    edge.wait()
    halo_waits[2]()


def smooth_kernel(
    place_ref, inter_ref, edge_ref, part_hbm, mesh_hbm, left_hbm, right_hbm, out_hbm,
    field, once, opened, band, arrived, arrived_open, leaving, leaving_open,
):
    place = place_ref[0]
    has_left, has_right = place > 0, place < 127

    def fetch(half):
        first, count = ((0, 9), (9, 7))[half]
        side, at = ((left_hbm, 0), (right_hbm, 18))[half]
        copies = []
        for q in range(4):
            lanes = pl.ds(128 * q, 128)
            copies.append(
                pltpu.make_async_copy(
                    mesh_hbm.at[2, pl.ds(first, count), :, lanes],
                    field.at[q, pl.ds(first + 2, count), pl.ds(8, 96)],
                    arrived.at[half, q, 0],
                )
            )
            copies.append(
                pltpu.make_async_copy(
                    side.at[:, :, lanes],
                    field.at[q, pl.ds(at, 2), pl.ds(8, 96)],
                    arrived.at[half, q, 1],
                )
            )
        return copies

    def store(half):
        return [
            pltpu.make_async_copy(
                field.at[q, pl.ds(2 + 8 * half, 8), pl.ds(8, 96)],
                out_hbm.at[2, pl.ds(8 * half, 8), :, pl.ds(128 * q, 128)],
                leaving.at[half, q],
            )
            for q in range(4)
        ]

    arriving = [fetch(0), fetch(1)]
    for copy in arriving[0] + arriving[1]:
        copy.start()
    early = [
        pltpu.make_async_copy(part_hbm.at[k], opened.at[k], arrived_open.at[k]) for k in range(2)
    ]
    for copy in early:
        copy.start()
    stores = [
        pltpu.make_async_copy(opened.at[k], out_hbm.at[k], leaving_open.at[k]) for k in range(2)
    ]
    neighbour_band(band)
    clear_margins(once)
    clear_margins(field)
    for half in range(2):
        finish(arriving[half])
        for q in range(4):
            lanes = slice(128 * q, 128 * (q + 1))
            for x in range(9 * half, 9 + 7 * half):
                field[q, x + 2, 8:9, :] = inter_ref[2, x : x + 1, lanes]
            field[q, 1 + 17 * half, 8:9, :] = edge_ref[half, 2:3, lanes]
        close_end(field, 1 + 17 * half, (has_left, has_right)[half])
        swept(field, once, band, 9, 9 * half + 1, 9 * half)
        early[half].wait()
        add_wall(
            inter_ref[half],
            jnp.where(has_left, edge_ref[0, half : half + 1, :], 0.0),
            jnp.where(has_right, edge_ref[1, half : half + 1, :], 0.0),
            opened.at[half],
        )
        stores[half].start()
    close_end(once, 0, has_left)
    close_end(once, 17, has_right)
    for half in range(2):
        swept(once, field, band, 8, 8 * half + 1, 8 * half + 2)
        stores += store(half)
        for copy in stores[-4:]:
            copy.start()
    finish(stores)


def transfer(
    displacement, send_node, member_slot, inverse_part, source_coord, target_coord,
    unity_weight, result_pick, receive_vertex, mesh_before,
):
    hbm = pl.BlockSpec(memory_space=pl.ANY)
    dma = pltpu.SemaphoreType.DMA
    halo = jax.ShapeDtypeStruct((2, 96, 512), f32)
    exchange = [
        pltpu.VMEM((192, 128), f32),
        pltpu.VMEM((192, 128), f32),
        pltpu.VMEM((16, 12, 128), f32),
        pltpu.VMEM((16, 12, 128), f32),
    ]
    small = [
        displacement,
        send_node.reshape(64, 128),
        member_slot,
        source_coord.transpose(1, 0, 2),
        target_coord.transpose(1, 0, 2),
        unity_weight,
        result_pick.reshape(64, 128),
        receive_vertex.reshape(64, 128),
    ]
    return pl.pallas_call(
        transfer_kernel,
        out_shape=(
            jax.ShapeDtypeStruct((3, 16, 512), f32),
            jax.ShapeDtypeStruct((2, 8, 512), f32),
            halo,
            halo,
            jax.ShapeDtypeStruct((2, 16, 96, 512), f32),
        ),
        in_specs=[hbm] * 10,
        out_specs=(hbm,) * 5,
        scratch_shapes=[pltpu.VMEM(a.shape, a.dtype) for a in small]
        + exchange
        + exchange
        + [
            pltpu.VMEM((4, 1024, 1024), bf16),
            pltpu.VMEM((8, 32, 128), f32),
            pltpu.VMEM((8, 128, 128), f32),
            pltpu.VMEM((8, 128, 128), f32),
            pltpu.VMEM((4, 1024, 1024), bf16),
            pltpu.VMEM((4, 1024, 1024), bf16),
            pltpu.VMEM((4, 8, 1024), f32),
            pltpu.VMEM((4, 384, 512), bf16),
            pltpu.VMEM((4, 128, 512), bf16),
            pltpu.VMEM((384, 128), f32),
            pltpu.VMEM((3, 16, 512), f32),
            pltpu.VMEM((2, 8, 512), f32),
            pltpu.VMEM((2, 8, 512), f32),
            pltpu.VMEM((2, 4, 20, 112, 128), f32),
            pltpu.VMEM((4, 18, 112, 128), f32),
            pltpu.VMEM((2, 2, 2, 96, 512), f32),
            pltpu.VMEM((512, 256), bf16),
            dma((8,)),
            dma((12,)),
            dma((7,)),
            dma((7,)),
            dma((15,)),
            dma((15,)),
            dma((7,)),
            dma((7,)),
            dma((15,)),
            dma((15,)),
            dma((8,)),
            dma((8,)),
            dma((10,)),
        ],
        compiler_params=pltpu.CompilerParams(
            collective_id=1, has_side_effects=True, vmem_limit_bytes=63 << 20
        ),
    )(*small, inverse_part, mesh_before)


def smooth(place, interface, edges, part, mesh_before, left, right):
    hbm = pl.BlockSpec(memory_space=pl.ANY)
    return pl.pallas_call(
        smooth_kernel,
        out_shape=jax.ShapeDtypeStruct((3, 16, 96, 512), f32),
        in_specs=[pl.BlockSpec(memory_space=pltpu.SMEM), vmem(), vmem(), hbm, hbm, hbm, hbm],
        out_specs=hbm,
        scratch_shapes=[
            pltpu.VMEM((4, 20, 112, 128), f32),
            pltpu.VMEM((4, 18, 112, 128), f32),
            pltpu.VMEM((2, 16, 96, 512), f32),
            pltpu.VMEM((512, 256), bf16),
            pltpu.SemaphoreType.DMA((2, 4, 2)),
            pltpu.SemaphoreType.DMA((2,)),
            pltpu.SemaphoreType.DMA((2, 4)),
            pltpu.SemaphoreType.DMA((2,)),
        ],
        compiler_params=pltpu.CompilerParams(vmem_limit_bytes=63 << 20),
    )(place, interface, edges, part, mesh_before, left, right)


def local(
    displacement,
    send_node,
    member_slot,
    inverse_part,
    source_coord,
    target_coord,
    unity_weight,
    result_pick,
    receive_vertex,
    mesh_before,
):
    place = lax.axis_index("dev").astype(jnp.int32).reshape(1)
    interface, edges, left, right, part = transfer(
        displacement, send_node, member_slot, inverse_part, source_coord, target_coord,
        unity_weight, result_pick, receive_vertex, mesh_before,
    )
    return smooth(place, interface, edges, part, mesh_before, left, right)


def solution(mesh):
    in_specs = (
        P(None, "dev"),
        P("dev"),
        P("dev", None),
        P("dev", None, None),
        P("dev", None, None),
        P("dev", None, None),
        P("dev", None),
        P("dev"),
        P("dev"),
        P(None, "dev", None, None),
    )
    out_specs = P(None, "dev", None, None)
    return jax.shard_map(local, mesh=mesh, in_specs=in_specs, out_specs=out_specs, check_vma=False)
```

```python
import jax
import jax.numpy as jnp
from jax import lax
from jax.experimental import pallas as pl
from jax.experimental.pallas import tpu as pltpu
from jax.sharding import PartitionSpec as P

relax_rate = 0.8
kernel_sharpness = 8.0
log2_e = 1.4426950408889634
spread_rate = relax_rate / 6.0
keep_rate = 1.0 - relax_rate

MESH = pl.DeviceIdType.MESH
f32 = jnp.float32
bf16 = jnp.bfloat16


def vmem():
    return pl.BlockSpec(memory_space=pltpu.VMEM)


def lookup(row, lanes):
    spread = jnp.broadcast_to(row, lanes.shape)
    return jnp.take_along_axis(spread, lanes, axis=1, mode="promise_in_bounds")


def message_index(index_ref, step):
    x, core = step // 2, step % 2
    even = index_ref[pl.ds(x, 8, stride=8), :]
    odd = index_ref[pl.ds(4 + x, 8, stride=8), :]
    lane = lax.broadcasted_iota(jnp.int32, (8, 128), 1)
    if core == 0:
        return jnp.where(lane < 64, even, pltpu.roll(odd, 64, 1))
    return jnp.where(lane < 64, pltpu.roll(even, 64, 1), odd)


def pick_messages(index_ref, row_of, out_ref):
    for half in range(2):
        index = [message_index(index_ref, 4 * half + g) for g in range(4)]
        high = [jnp.right_shift(i, 7) for i in index]
        low = [jnp.bitwise_and(i, 127) for i in index]
        total = [[jnp.zeros((8, 128), f32) for _ in range(3)] for _ in range(4)]
        for r in range(32):
            hit = [h == r for h in high]
            for k in range(3):
                row = row_of(k, r)
                for g in range(4):
                    total[g][k] = jnp.where(hit[g], lookup(row, low[g]), total[g][k])
        for g in range(4):
            for k in range(3):
                top = ((4 * half + g) * 3 + k) * 8
                out_ref[top : top + 8, :] = total[g][k]


def three_parts(value):
    high = value.astype(bf16).astype(f32)
    rest = value - high
    middle = rest.astype(bf16).astype(f32)
    return high, middle, rest - middle


def cluster_rows(ref, c, rows):
    return jnp.concatenate([ref[q, pl.ds(c, rows, stride=4), :] for q in range(8)], axis=1)


def remote(source, target, send, receive, device):
    copy = pltpu.make_async_remote_copy(
        src_ref=source,
        dst_ref=target,
        send_sem=send,
        recv_sem=receive,
        device_id=(device,),
        device_id_type=MESH,
    )
    copy.start()
    return copy


def first_stage(messages, held, send, receive, outer, inner):
    copies = []
    for i in range(1, 8):
        p = (inner + i) % 8
        copies.append(
            remote(
                messages.at[pl.ds(pl.multiple_of(p * 24, 8), 24)],
                held.at[pl.ds(pl.multiple_of(inner * 24, 8), 24)],
                send.at[i - 1],
                receive.at[i - 1],
                outer * 8 + p,
            )
        )
    mine = pl.ds(pl.multiple_of(inner * 24, 8), 24)
    held[mine, :] = messages[mine, :]
    return copies


def second_stage(held, ready, landed, send, receive, outer, inner):
    lane = lax.broadcasted_iota(jnp.int32, (4, 128), 1)
    for m in range(8):
        for k in range(3):
            first = held[pl.ds(k * 8 + m, 4, stride=48), :]
            second = held[pl.ds(24 + k * 8 + m, 4, stride=48), :]
            ready[2 * m, 4 * k : 4 * k + 4, :] = jnp.where(
                lane < 64, first, pltpu.roll(second, 64, 1)
            )
            ready[2 * m + 1, 4 * k : 4 * k + 4, :] = jnp.where(
                lane < 64, pltpu.roll(first, 64, 1), second
            )
    copies = []
    for i in range(1, 16):
        p = (outer + i) % 16
        copies.append(
            remote(
                ready.at[p],
                landed.at[outer],
                send.at[i - 1],
                receive.at[i - 1],
                p * 8 + inner,
            )
        )
    landed[outer] = ready[outer]
    return copies


def shift(source_last, source_first, left, right, send, receive, me):
    has_left, has_right = me > 0, me < 127

    def descriptor(source, target, i, device):
        return pltpu.make_async_remote_copy(
            src_ref=source,
            dst_ref=target,
            send_sem=send[i],
            recv_sem=receive[i],
            device_id=(device,),
            device_id_type=MESH,
        )

    ahead = descriptor(source_last, left, 0, (me + 1) % 128)
    back = descriptor(source_first, right, 1, (me + 127) % 128)

    @pl.when(has_right)
    def _():
        ahead.start()

    @pl.when(has_left)
    def _():
        back.start()

    def wait():
        @pl.when(has_right)
        def _():
            ahead.wait_send()
            back.wait_recv()

        @pl.when(has_left)
        def _():
            back.wait_send()
            ahead.wait_recv()

    return wait


def finish(copies):
    for copy in copies:
        copy.wait()


def exponent_rows(source_ref, target_ref, left, right):
    left[...] = jnp.zeros_like(left)
    right[...] = jnp.zeros_like(right)
    ones = jnp.ones((4, 1024), f32)
    source_norm = jnp.zeros((4, 1024), f32)
    target_norm = jnp.zeros((4, 1024), f32)
    pairs = []
    for d in range(3):
        s = source_ref[d]
        t = target_ref[d]
        source_norm += s * s
        target_norm += t * t
        sh, sm, sl = three_parts(s)
        th, tm, tl = three_parts(t * (2.0 * kernel_sharpness * log2_e))
        pairs += [(sh, th), (sh, tm), (sm, th), (sh, tl), (sl, th), (sm, tm)]
    pairs += [(p, ones) for p in three_parts(source_norm * (-kernel_sharpness * log2_e))]
    pairs += [(ones, p) for p in three_parts(target_norm * (-kernel_sharpness * log2_e))]
    for row, (a, b) in enumerate(pairs):
        for q in range(8):
            left[q, 4 * row : 4 * row + 4, :] = a[:, 128 * q : 128 * (q + 1)]
            right[q, 4 * row : 4 * row + 4, :] = b[:, 128 * q : 128 * (q + 1)]


def kernel_values(c, left, right, upper, lower):
    source_rows = cluster_rows(left, c, 32).T.astype(bf16)
    target_rows = cluster_rows(right, c, 32).astype(bf16)
    for p in range(4):
        rows = slice(256 * p, 256 * (p + 1))
        kernel = jnp.exp2(jnp.dot(source_rows[rows], target_rows, preferred_element_type=f32))
        high = kernel.astype(bf16)
        upper[c, rows, :] = high
        lower[c, rows, :] = (kernel - high.astype(f32)).astype(bf16)


def gather_members(table, slot_ref, member):
    member[...] = jnp.zeros_like(member)
    index = [
        jnp.concatenate(
            [slot_ref[:, 256 * m : 256 * m + 128], slot_ref[:, 256 * m + 128 : 256 * m + 256]],
            axis=0,
        )
        for m in range(4)
    ]
    high = [jnp.right_shift(i, 7) for i in index]
    low = [jnp.bitwise_and(i, 127) for i in index]

    def gather(part, total):
        total = list(total)
        for r in range(16):
            zy, j = part * 4 + r // 4, r % 4
            hit = [h == part * 16 + r for h in high]
            for k in range(3):
                line = table[zy, 4 * k + j : 4 * k + j + 1, :]
                for m in range(4):
                    total[3 * m + k] = jnp.where(hit[m], lookup(line, low[m]), total[3 * m + k])
        return tuple(total)

    total = lax.fori_loop(
        0, 4, gather, tuple(jnp.zeros((8, 128), f32) for _ in range(12))
    )
    for m in range(4):
        for k in range(3):
            value = total[3 * m + k]
            member[2 * m, 4 * k : 4 * k + 4, :] = value[0:4]
            member[2 * m + 1, 4 * k : 4 * k + 4, :] = value[4:8]


def contribute(c, member, inverse, upper, lower, weight_ref, result):
    members = cluster_rows(member, c, 8)
    padded = jnp.concatenate([members, jnp.zeros((8, 1024), f32)], axis=0)
    coupling = lax.dot_general(
        padded.astype(bf16), inverse[c], (((1,), (1,)), ((), ())), preferred_element_type=f32
    )
    coefficient = members + coupling[0:8]
    high = coefficient.astype(bf16).astype(f32)
    both = jnp.concatenate([high, coefficient - high], axis=0).astype(bf16)
    summed = jnp.dot(both, upper[c], preferred_element_type=f32)
    summed += jnp.dot(both, lower[c], preferred_element_type=f32)
    result[c] = (summed[0:8] + summed[8:16]) * weight_ref[c : c + 1, :]


def scatter(table, vertex_ref, values, places, total, out_ref):
    def chunk(group, carry):
        product = jnp.zeros((384, 128), f32)
        for part in range(4):
            zy = group * 4 + part
            for j in range(4):
                vertex = vertex_ref[pl.ds(zy * 4 + j, 1), :]
                high = jnp.broadcast_to(jnp.right_shift(vertex, 7), (64, 128))
                low = jnp.broadcast_to(jnp.bitwise_and(vertex, 127), (128, 128))
                at_high = high == lax.broadcasted_iota(jnp.int32, (64, 128), 0)
                at_low = low == lax.broadcasted_iota(jnp.int32, (128, 128), 0)
                lanes = slice(128 * j, 128 * j + 128)
                places[part, :, lanes] = jnp.where(at_low, 1.0, 0.0).astype(bf16)
                for k in range(3):
                    value = table[zy, 4 * k + j : 4 * k + j + 1, :]
                    upper = value.astype(bf16).astype(f32)
                    for s, half in enumerate((upper, value - upper)):
                        spread = jnp.broadcast_to(half, (64, 128))
                        top = (2 * k + s) * 64
                        values[part, top : top + 64, lanes] = jnp.where(
                            at_high, spread, 0.0
                        ).astype(bf16)
            product += lax.dot_general(
                values[part],
                places[part],
                (((1,), (1,)), ((), ())),
                preferred_element_type=f32,
            )
        total[...] += product
        return carry

    total[...] = jnp.zeros_like(total)
    lax.fori_loop(0, 4, chunk, 0)
    for k in range(3):
        top = 2 * k * 64
        for q in range(4):
            out_ref[k, :, 128 * q : 128 * (q + 1)] = (
                total[pl.ds(top + q, 16, stride=4), :]
                + total[pl.ds(top + 64 + q, 16, stride=4), :]
            )


def neighbour_band(band):
    row = jnp.bitwise_and(lax.broadcasted_iota(jnp.int32, (512, 256), 0), 255)
    column = lax.broadcasted_iota(jnp.int32, (512, 256), 1)
    near = (row == column + 1) | (row == column - 1)
    band[...] = jnp.where(near, 1.0, 0.0).astype(bf16)


def clear_margins(field):
    count = field.shape[1]
    for q in range(4):
        for x in range(count):
            field[q, x, 0:8, :] = jnp.zeros((8, 128), f32)
            field[q, x, 104:112, :] = jnp.zeros((8, 128), f32)


def swept(source, target, band, count, start, place):
    lane = lax.broadcasted_iota(jnp.int32, (count, 96, 128), 2)
    line = lax.broadcasted_iota(jnp.int32, (count, 96, 128), 1)
    here = pl.ds(start, count)
    center = [source[q, here, 8:104, :] for q in range(4)]
    upper, lower = [], []
    for part in center:
        high = part.astype(bf16)
        upper.append(high.reshape(count * 96, 128))
        lower.append((part - high.astype(f32)).astype(bf16).reshape(count * 96, 128))
    along = []
    for q in (0, 2):
        parts = jnp.concatenate([upper[q], upper[q + 1], lower[q], lower[q + 1]], axis=1)
        along.append(jnp.dot(parts, band[...], preferred_element_type=f32))
    for q in range(4):
        beside = along[q // 2][:, 128 * (q % 2) : 128 * (q % 2) + 128].reshape(count, 96, 128)
        if q == 1:
            beside = beside + jnp.where(lane == 127, pltpu.roll(center[2], 127, 2), 0.0)
        if q == 2:
            beside = beside + jnp.where(lane == 0, pltpu.roll(center[1], 1, 2), 0.0)
        beside = beside + (source[q, here, 7:103, :] + source[q, here, 9:105, :])
        beside = beside + (
            source[q, pl.ds(start - 1, count), 8:104, :]
            + source[q, pl.ds(start + 1, count), 8:104, :]
        )
        moved = center[q] * keep_rate + beside * spread_rate
        target[q, pl.ds(place, count), 8:104, :] = jnp.where(line == 0, center[q], moved)


def close_end(field, x, inside):
    @pl.when(jnp.logical_not(inside))
    def _():
        for q in range(4):
            field[q, x, 8:104, :] = jnp.zeros((96, 128), f32)


def sweep_open(field, once, halo, band, has_left, has_right):
    for q in range(4):
        lanes = slice(128 * q, 128 * (q + 1))
        for side in range(2):
            for x in range(2):
                field[q, 18 * side + x, 8:104, :] = halo[side, x, :, lanes]
        for x in range(1, 19):
            field[q, x, 8:9, :] = jnp.zeros((1, 128), f32)
    close_end(field, 1, has_left)
    close_end(field, 18, has_right)
    for i in range(2):
        swept(field, once, band, 9, 9 * i + 1, 9 * i)
    close_end(once, 0, has_left)
    close_end(once, 17, has_right)
    for i in range(2):
        swept(once, field, band, 8, 8 * i + 1, 8 * i + 2)


def add_wall(inter, before, after, field):
    lane = lax.broadcasted_iota(jnp.int32, (16, 512), 1)
    line = lax.broadcasted_iota(jnp.int32, (16, 512), 0)
    beside = jnp.where(line == 0, before, pltpu.roll(inter, 1, 0))
    beside = beside + jnp.where(line == 15, after, pltpu.roll(inter, 15, 0))
    beside = beside + jnp.where(lane == 0, 0.0, pltpu.roll(inter, 1, 1))
    beside = beside + jnp.where(lane == 511, 0.0, pltpu.roll(inter, 511, 1))
    first = spread_rate * ((1.0 + keep_rate) * inter + spread_rate * beside)
    second = (spread_rate * spread_rate) * inter
    row = lax.broadcasted_iota(jnp.int32, (8, 512), 0)
    for x in range(16):
        extra = jnp.where(
            row == 0,
            inter[x : x + 1],
            jnp.where(row == 1, first[x : x + 1], jnp.where(row == 2, second[x : x + 1], 0.0)),
        )
        field[x, 0:8, :] += extra


def transfer_kernel(
    disp_hbm, node_hbm, slot_hbm, source_hbm, target_hbm, weight_hbm, pick_hbm, vertex_hbm,
    inv_hbm, mesh_hbm,
    inter_hbm, edge_hbm, left_hbm, right_hbm, part_hbm,
    disp_ref, node_ref, slot_ref, source_ref, target_ref, weight_ref, pick_ref, vertex_ref,
    messages, held, ready, landed, messages2, held2, ready2, landed2,
    inverse, member, left, right, upper, lower, result, values, places, total,
    inter_ref, ends, near, field, once, halo, band,
    fetched, loaded, send1, recv1, send2, recv2, send3, recv3, send4, recv4, send5, recv5, stored,
):
    me = lax.axis_index("dev")
    outer, inner = me // 8, me % 8
    before, after = (me + 127) % 128, (me + 1) % 128
    has_left, has_right = me > 0, me < 127

    small = [
        (disp_hbm, disp_ref), (node_hbm, node_ref), (slot_hbm, slot_ref),
        (source_hbm, source_ref), (target_hbm, target_ref), (weight_hbm, weight_ref),
        (pick_hbm, pick_ref), (vertex_hbm, vertex_ref),
    ]
    fetches = [pltpu.make_async_copy(a, b, fetched.at[i]) for i, (a, b) in enumerate(small)]
    for fetch in fetches:
        fetch.start()
    @pl.when(jnp.logical_not(has_left))
    def _():
        near[0] = jnp.zeros((8, 512), f32)
        for k in range(2):
            halo[k, 0] = jnp.zeros((2, 96, 512), f32)

    @pl.when(jnp.logical_not(has_right))
    def _():
        near[1] = jnp.zeros((8, 512), f32)
        for k in range(2):
            halo[k, 1] = jnp.zeros((2, 96, 512), f32)

    barrier = pltpu.get_barrier_semaphore()
    peers = [outer * 8 + (inner + i) % 8 for i in range(1, 8)]
    peers += [((outer + i) % 16) * 8 + inner for i in range(1, 16)]
    peers += [before, after]
    for peer in peers:
        pl.semaphore_signal(barrier, inc=1, device_id=(peer,), device_id_type=MESH)
    loads = [pltpu.make_async_copy(inv_hbm.at[c], inverse.at[c], loaded.at[c]) for c in range(4)]
    loads += [
        pltpu.make_async_copy(
            mesh_hbm.at[k, :, :, pl.ds(128 * q, 128)],
            field.at[k, q, pl.ds(2, 16), pl.ds(8, 96)],
            loaded.at[4 + 4 * k + q],
        )
        for k in range(2)
        for q in range(4)
    ]
    for load in loads:
        load.start()

    finish(fetches[:2])
    pick_messages(
        node_ref, lambda k, r: disp_ref[k : k + 1, r * 128 : (r + 1) * 128], messages
    )
    pl.semaphore_wait(barrier, 24)

    copies = first_stage(messages, held, send1, recv1, outer, inner)
    finish(fetches[2:])
    neighbour_band(band)
    clear_margins(field.at[0])
    clear_margins(field.at[1])
    clear_margins(once)
    exponent_rows(source_ref, target_ref, left, right)
    kernel_values(0, left, right, upper, lower)
    kernel_values(1, left, right, upper, lower)
    finish(copies)
    copies = second_stage(held, ready, landed, send2, recv2, outer, inner)

    def send_halo(k):
        return shift(
            mesh_hbm.at[k, pl.ds(14, 2)],
            mesh_hbm.at[k, pl.ds(0, 2)],
            halo.at[k, 0] if k < 2 else left_hbm,
            halo.at[k, 1] if k < 2 else right_hbm,
            (send5.at[2 * k], send5.at[2 * k + 1]),
            (recv5.at[2 * k], recv5.at[2 * k + 1]),
            me,
        )

    kernel_values(2, left, right, upper, lower)
    kernel_values(3, left, right, upper, lower)
    finish(copies)
    halo_waits = [send_halo(0), send_halo(1)]

    gather_members(landed, slot_ref, member)
    for c in range(4):
        loads[c].wait()
        contribute(c, member, inverse, upper, lower, weight_ref, result)
    pick_messages(
        pick_ref,
        lambda k, r: result[r // 8, k : k + 1, (r % 8) * 128 : (r % 8 + 1) * 128],
        messages2,
    )
    finish(loads[4:])
    copies = first_stage(messages2, held2, send3, recv3, outer, inner)
    halo_waits[0]()
    sweep_open(field.at[0], once, halo.at[0], band, has_left, has_right)
    finish(copies)
    copies = second_stage(held2, ready2, landed2, send4, recv4, outer, inner)
    halo_waits[1]()
    sweep_open(field.at[1], once, halo.at[1], band, has_left, has_right)
    whole = [
        pltpu.make_async_copy(
            field.at[k, q, pl.ds(2, 16), pl.ds(8, 96)],
            part_hbm.at[k, :, :, pl.ds(128 * q, 128)],
            stored.at[4 * k + q],
        )
        for k in range(2)
        for q in range(4)
    ]
    for copy in whole:
        copy.start()
    finish(copies)
    halo_waits.append(send_halo(2))

    scatter(landed2, vertex_ref, values, places, total, inter_ref)
    ends[...] = jnp.zeros_like(ends)
    for k in range(3):
        ends[0, k : k + 1, :] = inter_ref[k, 0:1, :]
        ends[1, k : k + 1, :] = inter_ref[k, 15:16, :]
    edge_wait = shift(
        ends.at[1],
        ends.at[0],
        near.at[0],
        near.at[1],
        (send5.at[6], send5.at[7]),
        (recv5.at[6], recv5.at[7]),
        me,
    )
    wall = pltpu.make_async_copy(inter_ref, inter_hbm, stored.at[8])
    wall.start()
    edge_wait()
    edge = pltpu.make_async_copy(near, edge_hbm, stored.at[9])
    edge.start()
    finish(whole)
    wall.wait()
    edge.wait()
    halo_waits[2]()


def smooth_kernel(
    place_ref, inter_ref, edge_ref, part_hbm, mesh_hbm, left_hbm, right_hbm, out_hbm,
    field, once, opened, band, arrived, arrived_open, leaving, leaving_open,
):
    place = place_ref[0]
    has_left, has_right = place > 0, place < 127

    def fetch(half):
        first, count = ((0, 9), (9, 7))[half]
        side, at = ((left_hbm, 0), (right_hbm, 18))[half]
        copies = []
        for q in range(4):
            lanes = pl.ds(128 * q, 128)
            copies.append(
                pltpu.make_async_copy(
                    mesh_hbm.at[2, pl.ds(first, count), :, lanes],
                    field.at[q, pl.ds(first + 2, count), pl.ds(8, 96)],
                    arrived.at[half, q, 0],
                )
            )
            copies.append(
                pltpu.make_async_copy(
                    side.at[:, :, lanes],
                    field.at[q, pl.ds(at, 2), pl.ds(8, 96)],
                    arrived.at[half, q, 1],
                )
            )
        return copies

    def store(half):
        return [
            pltpu.make_async_copy(
                field.at[q, pl.ds(2 + 8 * half, 8), pl.ds(8, 96)],
                out_hbm.at[2, pl.ds(8 * half, 8), :, pl.ds(128 * q, 128)],
                leaving.at[half, q],
            )
            for q in range(4)
        ]

    arriving = [fetch(0), fetch(1)]
    for copy in arriving[0] + arriving[1]:
        copy.start()
    early = [
        pltpu.make_async_copy(part_hbm.at[k], opened.at[k], arrived_open.at[k]) for k in range(2)
    ]
    for copy in early:
        copy.start()
    stores = [
        pltpu.make_async_copy(opened.at[k], out_hbm.at[k], leaving_open.at[k]) for k in range(2)
    ]
    neighbour_band(band)
    clear_margins(once)
    clear_margins(field)
    for half in range(2):
        finish(arriving[half])
        for q in range(4):
            lanes = slice(128 * q, 128 * (q + 1))
            for x in range(9 * half, 9 + 7 * half):
                field[q, x + 2, 8:9, :] = inter_ref[2, x : x + 1, lanes]
            field[q, 1 + 17 * half, 8:9, :] = edge_ref[half, 2:3, lanes]
        close_end(field, 1 + 17 * half, (has_left, has_right)[half])
        swept(field, once, band, 9, 9 * half + 1, 9 * half)
        early[half].wait()
        add_wall(
            inter_ref[half],
            jnp.where(has_left, edge_ref[0, half : half + 1, :], 0.0),
            jnp.where(has_right, edge_ref[1, half : half + 1, :], 0.0),
            opened.at[half],
        )
        stores[half].start()
    close_end(once, 0, has_left)
    close_end(once, 17, has_right)
    for half in range(2):
        swept(once, field, band, 8, 8 * half + 1, 8 * half + 2)
        stores += store(half)
        for copy in stores[-4:]:
            copy.start()
    finish(stores)


def transfer(
    displacement, send_node, member_slot, inverse_part, source_coord, target_coord,
    unity_weight, result_pick, receive_vertex, mesh_before,
):
    hbm = pl.BlockSpec(memory_space=pl.ANY)
    dma = pltpu.SemaphoreType.DMA
    halo = jax.ShapeDtypeStruct((2, 96, 512), f32)
    exchange = [
        pltpu.VMEM((192, 128), f32),
        pltpu.VMEM((192, 128), f32),
        pltpu.VMEM((16, 12, 128), f32),
        pltpu.VMEM((16, 12, 128), f32),
    ]
    small = [
        displacement,
        send_node.reshape(64, 128),
        member_slot,
        source_coord.transpose(1, 0, 2),
        target_coord.transpose(1, 0, 2),
        unity_weight,
        result_pick.reshape(64, 128),
        receive_vertex.reshape(64, 128),
    ]
    return pl.pallas_call(
        transfer_kernel,
        out_shape=(
            jax.ShapeDtypeStruct((3, 16, 512), f32),
            jax.ShapeDtypeStruct((2, 8, 512), f32),
            halo,
            halo,
            jax.ShapeDtypeStruct((2, 16, 96, 512), f32),
        ),
        in_specs=[hbm] * 10,
        out_specs=(hbm,) * 5,
        scratch_shapes=[pltpu.VMEM(a.shape, a.dtype) for a in small]
        + exchange
        + exchange
        + [
            pltpu.VMEM((4, 1024, 1024), bf16),
            pltpu.VMEM((8, 32, 128), f32),
            pltpu.VMEM((8, 128, 128), f32),
            pltpu.VMEM((8, 128, 128), f32),
            pltpu.VMEM((4, 1024, 1024), bf16),
            pltpu.VMEM((4, 1024, 1024), bf16),
            pltpu.VMEM((4, 8, 1024), f32),
            pltpu.VMEM((4, 384, 512), bf16),
            pltpu.VMEM((4, 128, 512), bf16),
            pltpu.VMEM((384, 128), f32),
            pltpu.VMEM((3, 16, 512), f32),
            pltpu.VMEM((2, 8, 512), f32),
            pltpu.VMEM((2, 8, 512), f32),
            pltpu.VMEM((2, 4, 20, 112, 128), f32),
            pltpu.VMEM((4, 18, 112, 128), f32),
            pltpu.VMEM((2, 2, 2, 96, 512), f32),
            pltpu.VMEM((512, 256), bf16),
            dma((8,)),
            dma((12,)),
            dma((7,)),
            dma((7,)),
            dma((15,)),
            dma((15,)),
            dma((7,)),
            dma((7,)),
            dma((15,)),
            dma((15,)),
            dma((8,)),
            dma((8,)),
            dma((10,)),
        ],
        compiler_params=pltpu.CompilerParams(
            collective_id=1, has_side_effects=True, vmem_limit_bytes=63 << 20
        ),
    )(*small, inverse_part, mesh_before)


def smooth(place, interface, edges, part, mesh_before, left, right):
    hbm = pl.BlockSpec(memory_space=pl.ANY)
    return pl.pallas_call(
        smooth_kernel,
        out_shape=jax.ShapeDtypeStruct((3, 16, 96, 512), f32),
        in_specs=[pl.BlockSpec(memory_space=pltpu.SMEM), vmem(), vmem(), hbm, hbm, hbm, hbm],
        out_specs=hbm,
        scratch_shapes=[
            pltpu.VMEM((4, 20, 112, 128), f32),
            pltpu.VMEM((4, 18, 112, 128), f32),
            pltpu.VMEM((2, 16, 96, 512), f32),
            pltpu.VMEM((512, 256), bf16),
            pltpu.SemaphoreType.DMA((2, 4, 2)),
            pltpu.SemaphoreType.DMA((2,)),
            pltpu.SemaphoreType.DMA((2, 4)),
            pltpu.SemaphoreType.DMA((2,)),
        ],
        compiler_params=pltpu.CompilerParams(vmem_limit_bytes=63 << 20),
    )(place, interface, edges, part, mesh_before, left, right)


def local(
    displacement,
    send_node,
    member_slot,
    inverse_part,
    source_coord,
    target_coord,
    unity_weight,
    result_pick,
    receive_vertex,
    mesh_before,
):
    place = lax.axis_index("dev").astype(jnp.int32).reshape(1)
    interface, edges, left, right, part = transfer(
        displacement, send_node, member_slot, inverse_part, source_coord, target_coord,
        unity_weight, result_pick, receive_vertex, mesh_before,
    )
    return smooth(place, interface, edges, part, mesh_before, left, right)


def solution(mesh):
    in_specs = (
        P(None, "dev"),
        P("dev"),
        P("dev", None),
        P("dev", None, None),
        P("dev", None, None),
        P("dev", None, None),
        P("dev", None),
        P("dev"),
        P("dev"),
        P(None, "dev", None, None),
    )
    out_specs = P(None, "dev", None, None)
    return jax.shard_map(local, mesh=mesh, in_specs=in_specs, out_specs=out_specs, check_vma=False)
```
